512 devices in a mesh: lat: 8 (over y, z_hi), lon: 64 (over z_lo, x, core).
Axes of the slice: x: 4, y: 4, z: 16 (z_hi: 2, z_lo: 8; z = z_hi * 8 + z_lo), core: 2. Of those that a mesh axis runs over, the one named last changes fastest.
Arguments:
- inputs: bfloat16 [2, 48, 768, 192], P(None, 'lat', 'lon'), may hold values from -6 to 6
- cotangent: bfloat16 [2, 48, 768, 192], P(None, 'lat', 'lon'), may hold values from -6 to 6
- gains: float32 [2, 192], replicated, may hold values from 0.5 to 1.5
- qkv_weights: bfloat16 [2, 192, 576], replicated, may hold values from -0.4375 to 0.4375
- proj_weights: bfloat16 [2, 192, 192], replicated, may hold values from -0.4375 to 0.4375
- bias_tables: float32 [2, 8, 6, 23, 144], P(None, 'lat'), may hold values from -4 to 340
- pad_rows: int32 [48], replicated, may hold values 0 or 1
Outputs:
- outputs: bfloat16 [2, 48, 768, 192], P(None, 'lat', 'lon')
- d_inputs: bfloat16 [2, 48, 768, 192], P(None, 'lat', 'lon')
- d_gains: float32 [2, 192], replicated
- d_qkv: float32 [2, 192, 576], replicated
- d_proj: float32 [2, 192, 192], replicated
- d_tables: float32 [2, 8, 6, 23, 144], P(None, 'lat')
The draws below stay inside these ranges and needn't reach their ends.
All inputs are finite; a program needn't handle non-finite values.
Results may differ from the reference program's by a relative error of at most 0.015.
Values may be sent and summed in bfloat16 or wider, within the bound.
A program may use at most 64 MiB of HBM per device.

```python
import jax
import jax.numpy as jnp
import numpy as np
from jax import lax

LEVELS = 2
C = 192
HEADS = 6
LAT = 48
LON = 768
LAT_WINDOWS = 8


def draw_bias_tables(key, part):
    key = jax.random.fold_in(key, 11)
    base_key = jax.random.fold_in(key, 0)
    shape = (2, LAT_WINDOWS, HEADS, 23, 144)
    return jnp.clip(jax.random.normal(base_key, shape, jnp.float32), -4.0, 4.0)


def place_ends(array, stream_key, least, top_value):
    extent = array.shape
    spot = [jax.random.randint(jax.random.fold_in(stream_key, axis), (), 0, extent[axis]) for axis in range(len(extent))]
    array = array.at[tuple(spot)].set(least)
    longest = extent.index(max(extent))
    spot[longest] = (spot[longest] + 1) % extent[longest]
    return array.at[tuple(spot)].set(top_value)


def steps_of(rng, shape, cuts, smallest, top_value):
    factor_of, own = 1.0, jax.random.fold_in(rng, 6)
    for dim, shards_of in cuts:
        heights = jnp.exp(jax.random.uniform(jax.random.fold_in(own, dim), (shards_of,), jnp.float32, smallest / len(cuts), top_value / len(cuts)))
        factor_of = factor_of * jnp.repeat(heights, shape[dim] // shards_of).reshape([-1 if axis == dim else 1 for axis in range(len(shape))])
    return factor_of


def gaussian(key, extent, scale, limit, cuts=(), kind=jnp.bfloat16):
    entries = scale * jax.random.normal(key, extent, jnp.float32)
    if cuts:
        entries = entries * steps_of(key, extent, cuts, -0.22, 0.18)
    return jnp.clip(entries, -limit, limit).astype(kind)


def setup_inputs(seed: int = 0) -> dict:
    keys = jax.random.split(jax.random.key(seed), 8)
    inputs = gaussian(keys[0], (LEVELS, LAT, LON, C), 1.0, 6.0, ((1, 8), (2, 64)))
    cotangent = gaussian(keys[1], (LEVELS, LAT, LON, C), 1.0, 6.0, ((1, 8), (2, 64)))
    gains = jnp.clip(1.0 + 0.1 * jax.random.normal(keys[2], (2, C), jnp.float32), 0.5, 1.5)
    qkv_weights = gaussian(keys[3], (2, C, 3 * C), C ** -0.5, 0.4375)
    proj_weights = gaussian(keys[4], (2, C, C), C ** -0.5, 0.4375)
    bias_tables = draw_bias_tables(jax.random.fold_in(keys[7], 71), 0)
    pad_rows = place_ends((jax.random.randint(keys[6], (LAT,), 0, 8) < 7).astype(jnp.int32), jax.random.fold_in(keys[6], 1), 0, 1)
    return dict(inputs=inputs, cotangent=cotangent, gains=gains, qkv_weights=qkv_weights, proj_weights=proj_weights, bias_tables=bias_tables, pad_rows=pad_rows)


def offset_table():
    distance = np.arange(23)[:, None, None]
    query_col = np.arange(12)[None, :, None]
    key_col = np.arange(12)[None, None, :]
    return jnp.asarray((key_col - query_col + 11 == distance).astype(np.float32))

def product(form, left, right):
    return jnp.einsum(form, left.astype(jnp.float32), right.astype(jnp.float32), precision=lax.Precision.HIGHEST)

def to_windows(field):
    level_count, row_count, col_count = field.shape[:3]
    remain = field.shape[3:]
    shaped = field.reshape((level_count, row_count // 6, 6, col_count // 12, 12) + remain)
    order = (1, 3, 0, 2, 4) + tuple(range(5, 5 + len(remain)))
    return shaped.transpose(order).reshape((row_count // 6, col_count // 12, level_count * 72) + remain)

def from_windows(windows, level_count, row_count, col_count):
    remain = windows.shape[3:]
    shaped = windows.reshape((row_count // 6, col_count // 12, level_count, 6, 12) + remain)
    order = (2, 0, 3, 1, 4) + tuple(range(5, 5 + len(remain)))
    return shaped.transpose(order).reshape((level_count, row_count, col_count) + remain)

def shifted_regions(level_count, row_count, col_count, row_start, total_rows):
    rows = row_start + jnp.arange(row_count, dtype=jnp.int32)
    band = (rows >= total_rows - 6).astype(jnp.int32) + (rows >= total_rows - 3).astype(jnp.int32)
    levels = 3 * jnp.arange(level_count, dtype=jnp.int32)
    ids = levels[:, None] + band[None, :]
    return jnp.broadcast_to(ids[:, :, None], (level_count, row_count, col_count))

def expand_bias(table):
    window_count, head_count = table.shape[:2]
    divided = table.reshape(window_count, head_count, 23, 2, 2, 6, 6)
    full = jnp.einsum('thdabce,dfg->thacfbeg', divided, offset_table(), precision=lax.Precision.HIGHEST)
    return full.reshape(window_count, head_count, 144, 144)

def fold_bias(grads):
    window_count, head_count = grads.shape[:2]
    divided = grads.reshape(window_count, head_count, 2, 6, 12, 2, 6, 12)
    folded = jnp.einsum('thacfbeg,dfg->thdabce', divided, offset_table(), precision=lax.Precision.HIGHEST)
    return folded.reshape(window_count, head_count, 23, 144)

def attend_forward(hidden, gain, w_qkv, w_proj, bias, allowed):
    head_count = bias.shape[1]
    feature_count = hidden.shape[-1]
    head_size = feature_count // head_count
    score_scale = head_size ** (-0.5)
    values = hidden.astype(jnp.float32)
    center = values - lax.optimization_barrier(jnp.mean(values, -1, keepdims=True))
    inverse = lax.rsqrt(lax.optimization_barrier(jnp.mean(center * center, -1, keepdims=True)) + 1e-05)
    normed = center * inverse
    scaled = (normed * gain).astype(jnp.bfloat16)
    packed = product('absc,cf->absf', scaled, w_qkv).astype(jnp.bfloat16)
    divided = packed.reshape(packed.shape[:3] + (3, head_count, head_size))
    query_part = divided[:, :, :, 0]
    key_part = divided[:, :, :, 1]
    value_part = divided[:, :, :, 2]
    scores = product('abqhd,abkhd->abhqk', query_part, key_part) * score_scale + bias[:, None]
    permit = allowed[:, :, None]
    scores = jnp.where(permit, scores, -1e+30)
    row_max = lax.optimization_barrier(jnp.max(scores, -1, keepdims=True))
    weight = jnp.where(permit, jnp.exp(scores - row_max), 0.0)
    attention = weight / lax.optimization_barrier(jnp.sum(weight, -1, keepdims=True))
    rounded = attention.astype(jnp.bfloat16)
    mixture = product('abhqk,abkhd->abqhd', rounded, value_part).astype(jnp.bfloat16).reshape(hidden.shape)
    output = (values + product('absc,cf->absf', mixture, w_proj)).astype(jnp.bfloat16)
    return (output, (normed, inverse, scaled, query_part, key_part, value_part, attention, rounded, mixture))

def attend_backward(incoming, saved, gain, w_qkv, w_proj):
    normed, inverse, scaled, query_part, key_part, value_part, attention, rounded, mixture = saved
    head_count, head_size = query_part.shape[-2:]
    score_scale = head_size ** (-0.5)
    d_proj = product('absc,absf->cf', mixture, incoming)
    back_grad = product('absf,cf->absc', incoming, w_proj).astype(jnp.bfloat16)
    back_grad = back_grad.reshape(back_grad.shape[:3] + (head_count, head_size))
    d_attention = product('abqhd,abkhd->abhqk', back_grad, value_part)
    d_values = product('abhqk,abqhd->abkhd', rounded, back_grad).astype(jnp.bfloat16)
    d_scores = attention * (d_attention - lax.optimization_barrier(jnp.sum(d_attention * attention, -1, keepdims=True)))
    d_bias = lax.optimization_barrier(jnp.sum(d_scores, 1))
    d_rounded = (d_scores * score_scale).astype(jnp.bfloat16)
    d_query = product('abhqk,abkhd->abqhd', d_rounded, key_part).astype(jnp.bfloat16)
    d_keys = product('abhqk,abqhd->abkhd', d_rounded, query_part).astype(jnp.bfloat16)
    d_packed = jnp.stack([d_query, d_keys, d_values], 3).reshape(incoming.shape[:3] + (w_qkv.shape[1],))
    d_qkv = product('absc,absf->cf', scaled, d_packed)
    d_scaled = product('absf,cf->absc', d_packed, w_qkv)
    d_gain = lax.optimization_barrier(jnp.sum(d_scaled * normed, (0, 1, 2)))
    d_normed = d_scaled * gain
    d_hidden = inverse * (d_normed - lax.optimization_barrier(jnp.mean(d_normed, -1, keepdims=True)) - normed * lax.optimization_barrier(jnp.mean(d_normed * normed, -1, keepdims=True)))
    result = (incoming.astype(jnp.float32) + d_hidden).astype(jnp.bfloat16)
    return (result, d_gain, d_qkv, d_proj, d_bias)

def run_forward(windows, gain, w_qkv, w_proj, bias, allowed):

    def single(items):
        window_row, bias_row, allow_row = items
        output, ignored = attend_forward(window_row[None], gain, w_qkv, w_proj, bias_row[None], allow_row[None])
        return output[0]
    return lax.map(single, (windows, bias, allowed))

def run_backward(windows, incoming, gain, w_qkv, w_proj, bias, allowed):

    def single(items):
        window_row, grad_row, bias_row, allow_row = items
        ignored, saved = attend_forward(window_row[None], gain, w_qkv, w_proj, bias_row[None], allow_row[None])
        result = attend_backward(grad_row[None], saved, gain, w_qkv, w_proj)
        return (result[0][0], result[1], result[2], result[3], result[4][0])
    d_hidden, d_gain, d_qkv, d_proj, d_bias = lax.map(single, (windows, incoming, bias, allowed))
    return (d_hidden, lax.optimization_barrier(jnp.sum(d_gain, 0)), lax.optimization_barrier(jnp.sum(d_qkv, 0)), lax.optimization_barrier(jnp.sum(d_proj, 0)), fold_bias(d_bias))

def shift_forward(field):
    return jnp.roll(field, (-1, -3, -6), (0, 1, 2))

def shift_back(field):
    return jnp.roll(field, (1, 3, 6), (0, 1, 2))

def reference(inputs, cotangent, gains, qkv_weights, proj_weights, bias_tables, pad_rows):
    level_count, row_count, col_count = inputs.shape[:3]
    diagonal = jnp.eye(144, dtype=bool)

    def key_valid(rows_ok):
        field = jnp.broadcast_to(rows_ok[None, :, None], (level_count, row_count, col_count))
        return to_windows(field)[:, :, None, :]
    valid = pad_rows == 1
    allow_first = key_valid(valid) | diagonal
    regions = to_windows(shifted_regions(level_count, row_count, col_count, 0, row_count))
    allow_second = (regions[:, :, :, None] == regions[:, :, None, :]) & (key_valid(jnp.roll(valid, -3)) | diagonal)
    bias_first = expand_bias(bias_tables[0])
    bias_second = expand_bias(bias_tables[1])
    first_in = to_windows(inputs)
    first = run_forward(first_in, gains[0], qkv_weights[0], proj_weights[0], bias_first, allow_first)
    first_field = from_windows(first, level_count, row_count, col_count)
    second_in = to_windows(shift_forward(first_field))
    second = run_forward(second_in, gains[1], qkv_weights[1], proj_weights[1], bias_second, allow_second)
    outputs = shift_back(from_windows(second, level_count, row_count, col_count))
    back_second = run_backward(second_in, to_windows(shift_forward(cotangent)), gains[1], qkv_weights[1], proj_weights[1], bias_second, allow_second)
    returned = to_windows(shift_back(from_windows(back_second[0], level_count, row_count, col_count)))
    back_first = run_backward(first_in, returned, gains[0], qkv_weights[0], proj_weights[0], bias_first, allow_first)
    d_inputs = from_windows(back_first[0], level_count, row_count, col_count)
    d_gains = jnp.stack([back_first[1], back_second[1]])
    d_qkv = jnp.stack([back_first[2], back_second[2]])
    d_proj = jnp.stack([back_first[3], back_second[3]])
    d_tables = jnp.stack([back_first[4], back_second[4]])
    return (outputs, d_inputs, d_gains, d_qkv, d_proj, d_tables)
```

```python
import jax
import jax.numpy as jnp
import numpy as np
from jax import lax
from jax.experimental import pallas as pl
from jax.experimental.pallas import tpu as pltpu
from jax.sharding import PartitionSpec as P

F32 = jnp.float32
BF16 = jnp.bfloat16
MESH = pl.DeviceIdType.MESH
HEADS = 6
SCALE = 32 ** (-0.5)


def orders():
    pos_a = np.zeros((2, 6, 12), np.int64)
    pos_n = np.zeros((2, 6, 12), np.int64)
    pos_b = np.zeros((2, 6, 12), np.int64)
    slot = np.zeros((2, 6, 12), np.int64)
    for l in range(2):
        for r in range(6):
            for c in range(12):
                pos_n[l, r, c] = l * 72 + r * 12 + c
                pos_a[l, r, c] = c * 12 + l * 6 + r
                pos_b[l, r, c] = l * 72 + c * 6 + r
                quarter = (r // 3) * 2 + c // 6
                slot[l, r, c] = quarter * 48 + l * 18 + (r % 3) * 6 + c % 6
    return pos_n.ravel(), pos_a.ravel(), pos_b.ravel(), slot.ravel()


def one_hot(rows, cols, shape):
    out = np.zeros(shape, np.float32)
    out[rows, cols] = 1.0
    return out


def constants():
    pos_n, pos_a, pos_b, slot = orders()
    perm = np.stack([one_hot(pos_a, pos_n, (144, 144)), one_hot(pos_n, pos_a, (144, 144))])
    to_slot = np.stack([one_hot(slot, p, (192, 144)) for p in (pos_n, pos_a, pos_b)])
    from_slot = np.stack([one_hot(p, slot, (144, 192)) for p in (pos_n, pos_a, pos_b)])
    exp1 = np.zeros((2, 3, 3, 24, 1024), np.float32)
    exp2 = np.zeros((2, 3, 3, 24, 512), np.float32)
    for par in range(2):
        for h in range(3):
            for o in range(23):
                start = 144 * par + 288 * h + (22 - o) * 12
                exp1[par, h, :, o, start : start + 12] = 1.0
                start = 72 * par + 144 * h + (22 - o) * 6
                exp2[par, h, :, o, start : start + 6] = 1.0
    lanes = np.arange(1024)
    info = np.zeros((8, 1024), np.int32)
    info[0] = lanes % 12
    info[1] = lanes % 144
    info[2] = (lanes // 144) % 2 + 2 * (lanes >= 864)
    info[3] = lanes % 6
    info[4] = lanes % 72
    info[5] = (lanes // 72) % 2 + 2 * (lanes >= 432)
    return (
        jnp.asarray(perm, BF16),
        jnp.asarray(to_slot, BF16),
        jnp.asarray(from_slot, BF16),
        jnp.asarray(exp1.reshape(2, 216, 1024), BF16),
        jnp.asarray(exp2.reshape(2, 216, 512), BF16),
        jnp.asarray(exp1[:, :, 0].reshape(2, 72, 1024), BF16),
        jnp.asarray(exp2[:, :, 0].reshape(2, 72, 512), BF16),
        jnp.asarray(info),
    )


def nn(a, b):
    return lax.dot_general(a, b, (((1,), (0,)), ((), ())), preferred_element_type=F32)


def nt(a, b):
    return lax.dot_general(a, b, (((1,), (1,)), ((), ())), preferred_element_type=F32)


def tn(a, b):
    return lax.dot_general(a, b, (((0,), (0,)), ((), ())), preferred_element_type=F32)


def head_stack(x):
    lane = lax.broadcasted_iota(jnp.int32, (1, 192), 1)
    parts = [jnp.where((lane >= 32 * h) & (lane < 32 * h + 32), x, 0.0) for h in range(HEADS)]
    return jnp.concatenate(parts, 0).astype(BF16)


def head_diagonal(x, n):
    return jnp.concatenate(
        [x[32 * h : 32 * h + 32, n * h : n * h + n] for h in range(HEADS)], 0
    )


def split_table(s, tab_ref, block):
    out = []
    for h in range(HEADS):
        s.tab[h, 0:23, :] = tab_ref[block, 0, h]
    for par in range(2):
        parts = []
        for h in range(3):
            t = s.tab[2 * h + par]
            hi = t.astype(BF16).astype(F32)
            rest = t - hi
            mid = rest.astype(BF16).astype(F32)
            parts += [hi, mid, rest - mid]
        out.append(jnp.concatenate(parts, 0).astype(BF16))
    return out


def row_flags(pad_ref, start, total):
    rows = lax.broadcasted_iota(jnp.int32, (6, 1), 0)
    flags = jnp.zeros((6, 1), jnp.int32)
    for r in range(6):
        flags = jnp.where(rows == r, pad_ref[lax.rem(start + r, total)], flags)
    return rows, flags == 1


def expand_first(s, tab_ref, exp_ref, info_ref, pad_ref, lat):
    for par, parts in enumerate(split_table(s, tab_ref, 0)):
        s.wide[par] = tn(parts, exp_ref[par])
    l12 = info_ref[0:1, :]
    l144 = info_ref[1:2, 0:864]
    odd = info_ref[2:3, 0:864] == 1
    rows, valid = row_flags(pad_ref, 6 * lat, 48)
    for lk in range(2):
        strips = []
        for par in range(2):
            strip = jnp.zeros((6, 1024), F32)
            for e in range(12):
                at = 72 * (e // 6) + 36 * lk + 6 * (e % 6)
                strip = jnp.where(l12 == e, s.wide[par, at : at + 6, :], strip)
            strips.append(strip)
        for ck in range(12):
            turn = (1024 - (11 - ck) * 12) % 1024
            even_part, odd_part = [
                (pltpu.roll(x, turn, 1) if turn else x)[:, 0:864] for x in strips
            ]
            at = 12 * ck + 6 * lk
            keep = valid | (l144 == rows + at)
            s.bias1[at : at + 6, :] = jnp.where(
                keep, jnp.where(odd, odd_part, even_part), -1e30
            )


def expand_second(s, tab_ref, exp_ref, info_ref, pad_ref, lat):
    for par, parts in enumerate(split_table(s, tab_ref, 1)):
        s.wide[par, :, 0:512] = tn(parts, exp_ref[par])
    l6 = info_ref[3:4, 0:512]
    l72 = info_ref[4:5, 0:432]
    odd = info_ref[5:6, 0:432] == 1
    rows, valid = row_flags(pad_ref, 6 * lat + 3, 48)
    q_band = jnp.where(lat == 7, (info_ref[3:4, 0:432] >= 3).astype(jnp.int32), 0)
    k_band = jnp.where(lat == 7, (rows >= 3).astype(jnp.int32), 0)
    same = q_band == k_band
    for lev in range(2):
        strips = []
        for par in range(2):
            strip = jnp.zeros((6, 512), F32)
            for e in range(6):
                at = 108 * (1 - lev) + 6 * e
                strip = jnp.where(l6 == e, s.wide[par, at : at + 6, 0:512], strip)
            strips.append(strip)
        for ck in range(12):
            turn = (512 - (11 - ck) * 6) % 512
            even_part, odd_part = [
                (pltpu.roll(x, turn, 1) if turn else x)[:, 0:432] for x in strips
            ]
            at = 6 * ck
            keep = (valid | (l72 == rows + at)) & same
            s.bias2[lev, at : at + 6, :] = jnp.where(
                keep, jnp.where(odd, odd_part, even_part), -1e30
            )


def fold_first(s, one_ref, info_ref):
    l12 = info_ref[0:1, :]
    for par in range(2):
        mine = info_ref[2:3, :] == par
        for lk in range(2):
            acc = jnp.zeros((6, 1024), F32)
            for ck in range(12):
                at = 12 * ck + 6 * lk
                piece = jnp.where(mine, s.ds[at : at + 6, :], 0.0)
                turn = (11 - ck) * 12
                acc = acc + (pltpu.roll(piece, turn, 1) if turn else piece)
            for e in range(12):
                at = 72 * (e // 6) + 36 * lk + 6 * (e % 6)
                s.wide[par, at : at + 6, :] = jnp.where(l12 == e, acc, 0.0)
    return [nt(one_ref[par], s.wide[par].astype(BF16)) for par in range(2)]


def fold_second(s, one_ref, info_ref):
    l6 = info_ref[3:4, 0:512]
    s.wide[:, :, 0:512] = jnp.zeros((2, 144, 512), F32)
    for par in range(2):
        mine = info_ref[5:6, 0:512] == par
        for lev in range(2):
            acc = jnp.zeros((6, 512), F32)
            for ck in range(12):
                at = 72 * lev + 6 * ck
                piece = jnp.where(mine, s.ds[at : at + 6, 0:512], 0.0)
                turn = (11 - ck) * 6
                acc = acc + (pltpu.roll(piece, turn, 1) if turn else piece)
            for e in range(6):
                at = 108 * (1 - lev) + 6 * e
                s.wide[par, at : at + 6, 0:512] = jnp.where(l6 == e, acc, 0.0)
    return [nt(one_ref[par], s.wide[par, :, 0:512].astype(BF16)) for par in range(2)]


def forward(s, j, x, gain, wqkv_ref, wproj_ref, bias, groups):
    n = 144 // groups
    center = x - jnp.mean(x, -1, keepdims=True)
    inverse = lax.rsqrt(jnp.mean(center * center, -1, keepdims=True) + 1e-05)
    normed = center * inverse
    scaled = (normed * gain).astype(BF16)
    packed = nn(scaled, wqkv_ref[j])
    q, k, v = packed[:, 0:192], packed[:, 192:384], packed[:, 384:576]
    s.normed[j] = normed
    s.inverse[j] = inverse
    s.scaled[j] = scaled
    s.k[j] = k
    s.v[j] = v
    attended = []
    for g in range(groups):
        rows = slice(g * n, g * n + n)
        qm = head_stack(q[rows])
        s.qm[j, g * 6 * n : (g + 1) * 6 * n, :] = qm
        scores = nt(k[rows].astype(BF16), qm) * SCALE + bias(g)
        weight = jnp.exp(scores - jnp.max(scores, 0, keepdims=True))
        probs = weight * (1.0 / jnp.sum(weight, 0, keepdims=True))
        s.probs[j, rows, 0 : 6 * n] = probs
        mixed_t = head_diagonal(tn(v[rows].astype(BF16), probs.astype(BF16)), n)
        s.mixed_t[j, g, :, 0:n] = mixed_t
        attended.append(tn(mixed_t.astype(BF16), wproj_ref[j]))
    att = attended[0] if groups == 1 else jnp.concatenate(attended, 0)
    return (x + att).astype(BF16)


def backward(s, j, g_in, gain, wqkv_ref, wproj_ref, groups):
    n = 144 // groups
    back = nt(g_in, wproj_ref[j])
    dqs, dks, dvs = [], [], []
    for g in range(groups):
        rows = slice(g * n, g * n + n)
        backm = head_stack(back[rows])
        probs = s.probs[j, rows, 0 : 6 * n]
        k = s.k[j, rows, :].astype(BF16)
        v = s.v[j, rows, :].astype(BF16)
        qm = s.qm[j, g * 6 * n : (g + 1) * 6 * n, :]
        d_probs = nt(v, backm)
        dvs.append(nn(probs.astype(BF16), backm))
        d_scores = probs * (d_probs - jnp.sum(d_probs * probs, 0, keepdims=True))
        s.ds[rows, 0 : 6 * n] = d_scores
        d_rounded = (d_scores * SCALE).astype(BF16)
        dks.append(nn(d_rounded, qm))
        dqs.append(head_diagonal(tn(k, d_rounded), n).T)
    if groups == 1:
        dq, dk, dv = dqs[0], dks[0], dvs[0]
    else:
        dq, dk, dv = [jnp.concatenate(p, 0) for p in (dqs, dks, dvs)]
    dq, dk, dv = dq.astype(BF16), dk.astype(BF16), dv.astype(BF16)
    w = wqkv_ref[j]
    d_scaled = nt(dq, w[:, 0:192]) + nt(dk, w[:, 192:384]) + nt(dv, w[:, 384:576])
    normed = s.normed[j]
    d_normed = d_scaled * gain
    d_hidden = s.inverse[j] * (
        d_normed
        - jnp.mean(d_normed, -1, keepdims=True)
        - normed * jnp.mean(d_normed * normed, -1, keepdims=True)
    )
    result = (g_in.astype(F32) + d_hidden).astype(BF16)
    return result, (dq, dk, dv, d_scaled)


def gradients(s, j, g_in, saved, folded, groups):
    n = 144 // groups
    dq, dk, dv, d_scaled = saved
    scaled = s.scaled[j]
    s.grad[:, 0:192] = tn(scaled, dq)
    s.grad[:, 192:384] = tn(scaled, dk)
    s.grad[:, 384:576] = tn(scaled, dv)
    d_proj = jnp.zeros((192, 192), F32)
    for g in range(groups):
        d_proj = d_proj + nn(
            s.mixed_t[j, g, :, 0:n].astype(BF16), g_in[g * n : g * n + n]
        )
    s.grad[:, 576:768] = d_proj
    for c in range(6):
        s.send[j, c] = s.grad[:, 128 * c : 128 * c + 128].astype(BF16)
    for h in range(HEADS):
        s.extra[24 * h : 24 * h + 24, 0:144] = folded[h % 2][24 * (h // 2) : 24 * (h // 2) + 24]
    s.extra[144:145, 0:192] = jnp.sum(d_scaled * s.normed[j], 0, keepdims=True)
    for c in range(2):
        s.send[j, 6 + c] = s.extra[:, 128 * c : 128 * c + 128].astype(BF16)


class Halo:
    def __init__(self, s, which, forward_shift):
        lat, lon = lax.axis_index("lat"), lax.axis_index("lon")
        nlat, nlon = lax.axis_size("lat"), lax.axis_size("lon")
        self.s, self.which = s, which
        self.copies = []
        self.stay = 3 if forward_shift else 0
        for i, quarter in enumerate(q for q in range(4) if q != self.stay):
            if forward_shift:
                by_lat, by_lon = quarter // 2 - 1 + nlat, quarter % 2 - 1 + nlon
            else:
                by_lat, by_lon = quarter // 2, quarter % 2
            self.copies.append(
                pltpu.make_async_remote_copy(
                    src_ref=s.halo_out.at[which, quarter],
                    dst_ref=s.halo_in.at[which, 3 - quarter],
                    send_sem=s.halo_send.at[which, i],
                    recv_sem=s.halo_recv.at[which, i],
                    device_id=(lax.rem(lat + by_lat, nlat), lax.rem(lon + by_lon, nlon)),
                    device_id_type=MESH,
                )
            )

    def start(self, quarters):
        for q in range(4):
            self.s.halo_out[self.which, q] = quarters[48 * q : 48 * q + 48]
        for copy in self.copies:
            copy.start()
        stay = self.stay
        self.s.halo_in[self.which, 3 - stay] = quarters[48 * stay : 48 * stay + 48]

    def finish(self):
        for copy in self.copies:
            copy.wait()
        return jnp.concatenate([self.s.halo_in[self.which, q] for q in range(4)], 0)


class Stage:
    def __init__(self, s, j, number, me, peer_id, src, dst):
        self.copies = []
        for d in range(1, 8):
            peer = lax.rem(me + d, 8)
            self.copies.append(
                pltpu.make_async_remote_copy(
                    src_ref=src(d, peer),
                    dst_ref=dst(d),
                    send_sem=s.ar_send.at[j, number, d],
                    recv_sem=s.ar_recv.at[j, number, d],
                    device_id=peer_id(peer),
                    device_id_type=MESH,
                )
            )

    def start(self):
        for copy in self.copies:
            copy.start()

    def finish(self):
        for copy in self.copies:
            copy.wait()


class Reduce:
    def __init__(self, s, j):
        lat, lon = lax.axis_index("lat"), lax.axis_index("lon")
        self.s, self.j = s, j
        self.line, self.z, self.lat = lax.rem(lon, 8), lon // 8, lat
        in_line = lambda p: (lat, (lon // 8) * 8 + p)
        in_z = lambda p: (lat, p * 8 + lax.rem(lon, 8))
        in_lat = lambda p: (p, lon)
        line, z = self.line, self.z
        self.stages = [
            Stage(s, j, 0, line, in_line, lambda d, p: s.send.at[j, p], lambda d: s.in1.at[j, d]),
            Stage(s, j, 1, z, in_z, lambda d, p: s.sum1.at[j, p], lambda d: s.in2.at[j, d]),
            Stage(s, j, 2, lat, in_lat, lambda d, p: s.sum2.at[j], lambda d: s.in3.at[j, d]),
            Stage(s, j, 3, z, in_z, lambda d, p: s.gather.at[j, z], lambda d: s.gather.at[j, z]),
            Stage(
                s, j, 4, line, in_line,
                lambda d, p: s.red.at[j, line], lambda d: s.red.at[j, line],
            ),
        ]

    def step(self, number):
        s, j = self.s, self.j
        if number > 0:
            self.stages[number - 1].finish()
        if number == 1:
            total = s.send[j, self.line].astype(F32)
            for d in range(1, 8):
                total = total + s.in1[j, d].astype(F32)
            for p in range(6):
                s.sum1[j, p] = total[32 * p : 32 * p + 32].astype(BF16)
            for p in range(6, 8):
                s.sum1[j, p] = jnp.zeros((32, 128), BF16)
        if number == 2:
            total = s.sum1[j, self.z].astype(F32)
            for d in range(1, 8):
                total = total + s.in2[j, d].astype(F32)
            s.sum2[j] = total.astype(BF16)
        if number == 3:
            own = s.sum2[j].astype(F32)
            total = own
            for d in range(1, 8):
                total = total + s.in3[j, d].astype(F32)
            rows = lax.broadcasted_iota(jnp.int32, (32, 1), 0) + self.z * 32
            table_until = jnp.where(self.line >= 6, 144, 0)
            s.gather[j, self.z] = jnp.where(rows < table_until, own, total).astype(BF16)
        if number == 4:
            for p in range(6):
                s.red[j, self.line, 32 * p : 32 * p + 32, :] = s.gather[j, p]
        if number < 5:
            self.stages[number].start()


def signal_partners():
    barrier = pltpu.get_barrier_semaphore()
    lat, lon = lax.axis_index("lat"), lax.axis_index("lon")
    nlat, nlon = lax.axis_size("lat"), lax.axis_size("lon")

    def signal(a, b):
        pl.semaphore_signal(barrier, inc=1, device_id=(a, b), device_id_type=MESH)

    for da, db in ((0, 1), (1, 0), (1, 1)):
        signal(lax.rem(lat + da, nlat), lax.rem(lon + db, nlon))
        signal(lax.rem(lat - da + nlat, nlat), lax.rem(lon - db + nlon, nlon))
    line, z = lax.rem(lon, 8), lon // 8
    for d in range(1, 8):
        signal(lat, z * 8 + lax.rem(line + d, 8))
        signal(lat, lax.rem(z + d, 8) * 8 + line)
        signal(lax.rem(lat + d, 8), lon)
    return barrier, 6 + 21


SCRATCH = dict(
    nat=pltpu.VMEM((144, 192), F32),
    tab=pltpu.VMEM((6, 24, 144), F32),
    wide=pltpu.VMEM((2, 144, 1024), F32),
    bias1=pltpu.VMEM((144, 864), F32),
    bias2=pltpu.VMEM((2, 72, 432), F32),
    ds=pltpu.VMEM((144, 1024), F32),
    normed=pltpu.VMEM((2, 144, 192), F32),
    inverse=pltpu.VMEM((2, 144, 1), F32),
    scaled=pltpu.VMEM((2, 144, 192), BF16),
    k=pltpu.VMEM((2, 144, 192), F32),
    v=pltpu.VMEM((2, 144, 192), F32),
    qm=pltpu.VMEM((2, 864, 192), BF16),
    probs=pltpu.VMEM((2, 144, 864), F32),
    mixed_t=pltpu.VMEM((2, 2, 192, 144), F32),
    grad=pltpu.VMEM((192, 768), F32),
    extra=pltpu.VMEM((192, 256), F32),
    halo_out=pltpu.VMEM((4, 4, 48, 192), BF16),
    halo_in=pltpu.VMEM((4, 4, 48, 192), BF16),
    send=pltpu.VMEM((2, 8, 192, 128), BF16),
    in1=pltpu.VMEM((2, 8, 192, 128), BF16),
    sum1=pltpu.VMEM((2, 8, 32, 128), BF16),
    in2=pltpu.VMEM((2, 8, 32, 128), BF16),
    sum2=pltpu.VMEM((2, 32, 128), BF16),
    in3=pltpu.VMEM((2, 8, 32, 128), BF16),
    gather=pltpu.VMEM((2, 8, 32, 128), BF16),
    red=pltpu.VMEM((2, 8, 192, 128), BF16),
    halo_send=pltpu.SemaphoreType.DMA((4, 3)),
    halo_recv=pltpu.SemaphoreType.DMA((4, 3)),
    ar_send=pltpu.SemaphoreType.DMA((2, 5, 8)),
    ar_recv=pltpu.SemaphoreType.DMA((2, 5, 8)),
)


class Names:
    pass


def main_kernel(
    x_ref, cot_ref, gains_ref, wqkv_ref, wproj_ref, tab_ref, pad_ref,
    perm_ref, to_ref, from_ref, exp1_ref, exp2_ref, one1_ref, one2_ref, info_ref,
    out_ref, dx_ref, red_ref, *scratch,
):
    s = Names()
    for name, ref in zip(SCRATCH, scratch):
        setattr(s, name, ref)
    lat = lax.axis_index("lat")
    barrier, expected = signal_partners()

    s.tab[...] = jnp.zeros((6, 24, 144), F32)
    s.ds[:, 768:1024] = jnp.zeros((144, 256), F32)
    s.extra[...] = jnp.zeros((192, 256), F32)

    def load(ref):
        for l in range(2):
            for r in range(6):
                at = 72 * l + 12 * r
                s.nat[at : at + 12, :] = ref[l, r].astype(F32)
        return s.nat[...].astype(BF16)

    def save(ref, value):
        s.nat[...] = value
        for l in range(2):
            for r in range(6):
                at = 72 * l + 12 * r
                ref[l, r] = s.nat[at : at + 12, :].astype(BF16)

    gain1, gain2 = gains_ref[0:1, :], gains_ref[1:2, :]
    x1 = nn(perm_ref[0], load(x_ref))
    expand_first(s, tab_ref, exp1_ref, info_ref, pad_ref, lat)
    first = forward(s, 0, x1, gain1, wqkv_ref, wproj_ref, lambda g: s.bias1[...], 1)
    pl.semaphore_wait(barrier, expected)

    h_first, h_cot, h_out, h_grad = [Halo(s, i, i < 2) for i in range(4)]
    h_first.start(nn(to_ref[1], first).astype(BF16))
    h_cot.start(nn(to_ref[0], load(cot_ref)).astype(BF16))
    expand_second(s, tab_ref, exp2_ref, info_ref, pad_ref, lat)
    x2 = nn(from_ref[2], h_first.finish())
    second = forward(s, 1, x2, gain2, wqkv_ref, wproj_ref, lambda g: s.bias2[g], 2)
    h_out.start(nn(to_ref[2], second).astype(BF16))
    g2 = nn(from_ref[2], h_cot.finish()).astype(BF16)
    dh2, saved2 = backward(s, 1, g2, gain2, wqkv_ref, wproj_ref, 2)
    h_grad.start(nn(to_ref[2], dh2).astype(BF16))
    gradients(s, 1, g2, saved2, fold_second(s, one2_ref, info_ref), 2)
    reduce2, reduce1 = Reduce(s, 1), Reduce(s, 0)
    reduce2.step(0)
    save(out_ref, nn(from_ref[0], h_out.finish()))
    g1 = nn(from_ref[1], h_grad.finish()).astype(BF16)
    reduce2.step(1)
    dx, saved1 = backward(s, 0, g1, gain1, wqkv_ref, wproj_ref, 1)
    reduce2.step(2)
    gradients(s, 0, g1, saved1, fold_first(s, one1_ref, info_ref), 1)
    reduce1.step(0)
    reduce2.step(3)
    save(dx_ref, nn(perm_ref[1], dx))
    reduce2.step(4)
    for number in range(1, 6):
        reduce1.step(number)
    reduce2.step(5)
    red_ref[...] = s.red[...]


def finish_kernel(red_ref, o_ref, d_ref, out_ref, dx_ref, gains_ref, dqkv_ref, dproj_ref, dtab_ref):
    out_ref[...] = o_ref[...]
    dx_ref[...] = d_ref[...]
    for j in range(2):
        for c in range(4):
            dqkv_ref[j, :, 128 * c : 128 * c + 128] = red_ref[j, c].astype(F32)
        mid = red_ref[j, 4].astype(F32)
        dqkv_ref[j, :, 512:576] = mid[:, 0:64]
        dproj_ref[j, :, 0:64] = mid[:, 64:128]
        dproj_ref[j, :, 64:192] = red_ref[j, 5].astype(F32)
        left = red_ref[j, 6].astype(F32)
        right = red_ref[j, 7].astype(F32)
        for h in range(HEADS):
            dtab_ref[j, 0, h, :, 0:128] = left[24 * h : 24 * h + 23]
            dtab_ref[j, 0, h, :, 128:144] = right[24 * h : 24 * h + 23, 0:16]
        gains_ref[j : j + 1, 0:128] = left[144:145]
        gains_ref[j : j + 1, 128:192] = right[144:145, 0:64]


def body(inputs, cotangent, gains, qkv_weights, proj_weights, bias_tables, pad_rows):
    vmem = pl.BlockSpec(memory_space=pltpu.VMEM)
    smem = pl.BlockSpec(memory_space=pltpu.SMEM)
    field = jax.ShapeDtypeStruct((2, 6, 12, 192), BF16)
    out, dx, red = pl.pallas_call(
        main_kernel,
        out_shape=(field, field, jax.ShapeDtypeStruct((2, 8, 192, 128), BF16)),
        in_specs=[vmem] * 6 + [smem] + [vmem] * 8,
        out_specs=(vmem,) * 3,
        scratch_shapes=list(SCRATCH.values()),
        compiler_params=pltpu.CompilerParams(
            collective_id=0, has_side_effects=True, vmem_limit_bytes=48 * 2**20
        ),
        name="both_blocks",
    )(inputs, cotangent, gains, qkv_weights, proj_weights, bias_tables, pad_rows, *constants())
    return pl.pallas_call(
        finish_kernel,
        out_shape=(
            field,
            field,
            jax.ShapeDtypeStruct((2, 192), F32),
            jax.ShapeDtypeStruct((2, 192, 576), F32),
            jax.ShapeDtypeStruct((2, 192, 192), F32),
            jax.ShapeDtypeStruct((2, 1, 6, 23, 144), F32),
        ),
        in_specs=[vmem] * 3,
        out_specs=(vmem,) * 6,
        compiler_params=pltpu.CompilerParams(vmem_limit_bytes=32 * 2**20),
        name="unpack",
    )(red, out, dx)


def solution(mesh):
    field = P(None, "lat", "lon", None)
    tables = P(None, "lat", None, None, None)
    return jax.shard_map(
        body,
        mesh=mesh,
        in_specs=(field, field, P(), P(), P(), tables, P()),
        out_specs=(field, field, P(), P(), P(), tables),
        check_vma=False,
    )
```

```python
import jax
import jax.numpy as jnp
from jax import lax
from jax.experimental import pallas as pl
from jax.experimental.pallas import tpu as pltpu
from jax.sharding import PartitionSpec as P

F32 = jnp.float32
BF16 = jnp.bfloat16
MESH = pl.DeviceIdType.MESH
HEADS = 6
SCALE = 32 ** (-0.5)


def div(x, d):
    return (x * (-(-(2**20) // d))) >> 20


def tokens_of(order, n):
    i = lax.broadcasted_iota(jnp.int32, (n, 1), 0)
    used = i < n
    if order == "n":
        r = div(i, 24)
        c = div(i - 24 * r, 2)
        l = i - 24 * r - 2 * c
    elif order == "a":
        c = div(i, 12)
        l = div(i - 12 * c, 6)
        r = i - 12 * c - 6 * l
    elif order == "b":
        l = div(i, 72)
        c = div(i - 72 * l, 6)
        r = i - 72 * l - 6 * c
    else:
        q = div(i, 48)
        inner = i - 48 * q
        used = inner < 36
        l = div(inner, 18)
        r = div(inner - 18 * l, 6)
        c = inner - 18 * l - 6 * r
        r, c = r + 3 * (q >> 1), c + 6 * (q & 1)
    return l, r, c, used


def place_in(order, l, r, c):
    if order == "n":
        return 24 * r + 2 * c + l
    if order == "a":
        return 12 * c + 6 * l + r
    if order == "b":
        return 72 * l + 6 * c + r
    lower, right = (r >= 3).astype(jnp.int32), (c >= 6).astype(jnp.int32)
    return 48 * (2 * lower + right) + 18 * l + 6 * (r - 3 * lower) + c - 6 * right


def reorder(to, of):
    size = {"s": 192}
    n, m = size.get(to, 144), size.get(of, 144)
    l, r, c, used = tokens_of(to, n)
    place = jnp.where(used, place_in(of, l, r, c), -1)
    return jnp.where(place == lax.broadcasted_iota(jnp.int32, (n, m), 1), 1.0, 0.0).astype(BF16)


def spread(lanes, step, par, parts):
    i = lax.broadcasted_iota(jnp.int32, (72 * parts, 1), 0)
    part = div(i, 72)
    h = div(i - 72 * part, 24)
    o = i - 72 * part - 24 * h
    start = 12 * step * par + 24 * step * h + (22 - o) * step
    at = lax.broadcasted_iota(jnp.int32, (72 * parts, lanes), 1) - start
    return jnp.where((at >= 0) & (at < step), 1.0, 0.0).astype(BF16)


def lane_info(lanes, step):
    lane = lax.broadcasted_iota(jnp.int32, (1, lanes), 1)
    head = div(lane, 12 * step)
    parity = jnp.where(head < HEADS, head & 1, 2)
    return lane - step * div(lane, step), lane - 12 * step * head, parity


def nn(a, b):
    return lax.dot_general(a, b, (((1,), (0,)), ((), ())), preferred_element_type=F32)


def nt(a, b):
    return lax.dot_general(a, b, (((1,), (1,)), ((), ())), preferred_element_type=F32)


def tn(a, b):
    return lax.dot_general(a, b, (((0,), (0,)), ((), ())), preferred_element_type=F32)


def head_stack(x):
    lane = lax.broadcasted_iota(jnp.int32, (1, 192), 1)
    parts = [jnp.where((lane >= 32 * h) & (lane < 32 * h + 32), x, 0.0) for h in range(HEADS)]
    return jnp.concatenate(parts, 0).astype(BF16)


def head_diagonal(x, n):
    return jnp.concatenate(
        [x[32 * h : 32 * h + 32, n * h : n * h + n] for h in range(HEADS)], 0
    )


def split_table(s, block):
    out = []
    for h in range(HEADS):
        s.tab[h, 0:23, :] = s.tab_in[block, h, :, 0, :]
    for par in range(2):
        parts = [[], [], []]
        for h in range(3):
            t = s.tab[2 * h + par]
            hi = t.astype(BF16).astype(F32)
            rest = t - hi
            mid = rest.astype(BF16).astype(F32)
            for part, value in zip(parts, (hi, mid, rest - mid)):
                part.append(value)
        out.append(jnp.concatenate(sum(parts, []), 0).astype(BF16))
    return out


def row_flags(s, start):
    rows = lax.broadcasted_iota(jnp.int32, (6, 1), 0)
    flags = jnp.zeros((6, 1), jnp.int32)
    for r in range(6):
        flags = jnp.where(rows == r, s.pad[lax.rem(start + r, 48)], flags)
    return rows, flags == 1


def expand_first(s, lat):
    for par, parts in enumerate(split_table(s, 0)):
        s.wide[par] = tn(parts, spread(1024, 12, par, 3))
    entry, token, parity = lane_info(1024, 12)
    token, odd = token[:, 0:864], parity[:, 0:864] == 1
    rows, valid = row_flags(s, 6 * lat)
    for lk in range(2):
        strips = []
        for par in range(2):
            strip = jnp.zeros((6, 1024), F32)
            for e in range(12):
                at = 72 * (e // 6) + 36 * lk + 6 * (e % 6)
                strip = jnp.where(entry == e, s.wide[par, at : at + 6, :], strip)
            strips.append(strip)
        for ck in range(12):
            turn = (1024 - (11 - ck) * 12) % 1024
            even_part, odd_part = [
                (pltpu.roll(x, turn, 1) if turn else x)[:, 0:864] for x in strips
            ]
            at = 12 * ck + 6 * lk
            keep = valid | (token == rows + at)
            s.bias1[at : at + 6, :] = jnp.where(
                keep, jnp.where(odd, odd_part, even_part), -1e30
            )


def expand_second(s, lat):
    for par, parts in enumerate(split_table(s, 1)):
        s.wide[par, :, 0:512] = tn(parts, spread(512, 6, par, 3))
    entry, token, parity = lane_info(512, 6)
    token, odd = token[:, 0:432], parity[:, 0:432] == 1
    rows, valid = row_flags(s, 6 * lat + 3)
    q_band = jnp.where(lat == 7, (entry[:, 0:432] >= 3).astype(jnp.int32), 0)
    k_band = jnp.where(lat == 7, (rows >= 3).astype(jnp.int32), 0)
    same = q_band == k_band
    for lev in range(2):
        strips = []
        for par in range(2):
            strip = jnp.zeros((6, 512), F32)
            for e in range(6):
                at = 108 * (1 - lev) + 6 * e
                strip = jnp.where(entry == e, s.wide[par, at : at + 6, 0:512], strip)
            strips.append(strip)
        for ck in range(12):
            turn = (512 - (11 - ck) * 6) % 512
            even_part, odd_part = [
                (pltpu.roll(x, turn, 1) if turn else x)[:, 0:432] for x in strips
            ]
            at = 6 * ck
            keep = (valid | (token == rows + at)) & same
            s.bias2[lev, at : at + 6, :] = jnp.where(
                keep, jnp.where(odd, odd_part, even_part), -1e30
            )


def fold_first(s):
    entry, _, parity = lane_info(1024, 12)
    for par in range(2):
        mine = parity == par
        for lk in range(2):
            acc = jnp.zeros((6, 1024), F32)
            for ck in range(12):
                at = 12 * ck + 6 * lk
                piece = jnp.where(mine, s.ds[at : at + 6, :], 0.0)
                turn = (11 - ck) * 12
                acc = acc + (pltpu.roll(piece, turn, 1) if turn else piece)
            for e in range(12):
                at = 72 * (e // 6) + 36 * lk + 6 * (e % 6)
                s.wide[par, at : at + 6, :] = jnp.where(entry == e, acc, 0.0)
    return [nt(spread(1024, 12, par, 1), s.wide[par].astype(BF16)) for par in range(2)]


def fold_second(s):
    entry, _, parity = lane_info(512, 6)
    s.wide[:, :, 0:512] = jnp.zeros((2, 144, 512), F32)
    for par in range(2):
        mine = parity == par
        for lev in range(2):
            acc = jnp.zeros((6, 512), F32)
            for ck in range(12):
                at = 72 * lev + 6 * ck
                piece = jnp.where(mine, s.ds[at : at + 6, 0:512], 0.0)
                turn = (11 - ck) * 6
                acc = acc + (pltpu.roll(piece, turn, 1) if turn else piece)
            for e in range(6):
                at = 108 * (1 - lev) + 6 * e
                s.wide[par, at : at + 6, 0:512] = jnp.where(entry == e, acc, 0.0)
    return [nt(spread(512, 6, par, 1), s.wide[par, :, 0:512].astype(BF16)) for par in range(2)]


def forward(s, j, x, gain, wqkv_ref, wproj_ref, bias, groups):
    n = 144 // groups
    center = x - jnp.mean(x, -1, keepdims=True)
    inverse = lax.rsqrt(jnp.mean(center * center, -1, keepdims=True) + 1e-05)
    normed = center * inverse
    scaled = (normed * gain).astype(BF16)
    packed = nn(scaled, wqkv_ref[j])
    q, k, v = packed[:, 0:192], packed[:, 192:384], packed[:, 384:576]
    s.normed[j] = normed
    s.inverse[j] = inverse
    s.scaled[j] = scaled
    s.k[j] = k
    s.v[j] = v
    attended = []
    for g in range(groups):
        rows = slice(g * n, g * n + n)
        qm = head_stack(q[rows])
        s.qm[j, g * 6 * n : (g + 1) * 6 * n, :] = qm
        scores = nt(k[rows].astype(BF16), qm) * SCALE + bias(g)
        weight = jnp.exp(scores - jnp.max(scores, 0, keepdims=True))
        probs = weight * (1.0 / jnp.sum(weight, 0, keepdims=True))
        s.probs[j, rows, 0 : 6 * n] = probs
        mixed_t = head_diagonal(tn(v[rows].astype(BF16), probs.astype(BF16)), n)
        s.mixed_t[j, g, :, 0:n] = mixed_t
        attended.append(tn(mixed_t.astype(BF16), wproj_ref[j]))
    att = attended[0] if groups == 1 else jnp.concatenate(attended, 0)
    return (x + att).astype(BF16)


def backward(s, j, g_in, gain, wqkv_ref, wproj_ref, groups):
    n = 144 // groups
    back = nt(g_in, wproj_ref[j])
    dqs, dks, dvs = [], [], []
    for g in range(groups):
        rows = slice(g * n, g * n + n)
        backm = head_stack(back[rows])
        probs = s.probs[j, rows, 0 : 6 * n]
        k = s.k[j, rows, :].astype(BF16)
        v = s.v[j, rows, :].astype(BF16)
        qm = s.qm[j, g * 6 * n : (g + 1) * 6 * n, :]
        d_probs = nt(v, backm)
        dvs.append(nn(probs.astype(BF16), backm))
        d_scores = probs * (d_probs - jnp.sum(d_probs * probs, 0, keepdims=True))
        s.ds[rows, 0 : 6 * n] = d_scores
        d_rounded = (d_scores * SCALE).astype(BF16)
        dks.append(nn(d_rounded, qm))
        dqs.append(head_diagonal(tn(k, d_rounded), n).T)
    if groups == 1:
        dq, dk, dv = dqs[0], dks[0], dvs[0]
    else:
        dq, dk, dv = [jnp.concatenate(p, 0) for p in (dqs, dks, dvs)]
    dq, dk, dv = dq.astype(BF16), dk.astype(BF16), dv.astype(BF16)
    w = wqkv_ref[j]
    d_scaled = nt(dq, w[:, 0:192]) + nt(dk, w[:, 192:384]) + nt(dv, w[:, 384:576])
    normed = s.normed[j]
    d_normed = d_scaled * gain
    d_hidden = s.inverse[j] * (
        d_normed
        - jnp.mean(d_normed, -1, keepdims=True)
        - normed * jnp.mean(d_normed * normed, -1, keepdims=True)
    )
    result = (g_in.astype(F32) + d_hidden).astype(BF16)
    return result, (dq, dk, dv, d_scaled)


def gradients(s, j, g_in, saved, folded, groups):
    n = 144 // groups
    dq, dk, dv, d_scaled = saved
    scaled = s.scaled[j]
    s.grad[:, 0:192] = tn(scaled, dq)
    s.grad[:, 192:384] = tn(scaled, dk)
    s.grad[:, 384:576] = tn(scaled, dv)
    d_proj = jnp.zeros((192, 192), F32)
    for g in range(groups):
        d_proj = d_proj + nn(
            s.mixed_t[j, g, :, 0:n].astype(BF16), g_in[g * n : g * n + n]
        )
    s.grad[:, 576:768] = d_proj
    for h in range(HEADS):
        s.extra[24 * h : 24 * h + 24, 0:144] = folded[h % 2][24 * (h // 2) : 24 * (h // 2) + 24]
    s.extra[144:145, 0:192] = jnp.sum(d_scaled * s.normed[j], 0, keepdims=True)
    for half in range(2):
        for slot in range(12):
            column, row = half * 384 + (slot // 4) * 128, (slot % 4) * 48
            s.payload[j, half, slot] = s.grad[row : row + 48, column : column + 128].astype(BF16)
        for slot, row in ((12, 144), (13, 0), (14, 48), (15, 96)):
            s.payload[j, half, slot] = s.extra[
                row : row + 48, 128 * half : 128 * half + 128
            ].astype(BF16)


class Halo:
    def __init__(self, s, which, forward_shift):
        lat, lon = lax.axis_index("lat"), lax.axis_index("lon")
        nlat, nlon = lax.axis_size("lat"), lax.axis_size("lon")
        self.s, self.which = s, which
        self.copies = []
        self.stay = 3 if forward_shift else 0
        for i, quarter in enumerate(q for q in range(4) if q != self.stay):
            if forward_shift:
                by_lat, by_lon = quarter // 2 - 1 + nlat, quarter % 2 - 1 + nlon
            else:
                by_lat, by_lon = quarter // 2, quarter % 2
            self.copies.append(
                pltpu.make_async_remote_copy(
                    src_ref=s.halo_out.at[which, quarter],
                    dst_ref=s.halo_in.at[which, 3 - quarter],
                    send_sem=s.halo_send.at[which, i],
                    recv_sem=s.halo_recv.at[which, i],
                    device_id=(lax.rem(lat + by_lat, nlat), lax.rem(lon + by_lon, nlon)),
                    device_id_type=MESH,
                )
            )

    def start(self, quarters):
        for q in range(4):
            self.s.halo_out[self.which, q] = quarters[48 * q : 48 * q + 48]
        for copy in self.copies:
            copy.start()
        stay = self.stay
        self.s.halo_in[self.which, 3 - stay] = quarters[48 * stay : 48 * stay + 48]

    def finish(self):
        for copy in self.copies:
            copy.wait()
        return jnp.concatenate([self.s.halo_in[self.which, q] for q in range(4)], 0)


def place():
    lat, lon = lax.axis_index("lat"), lax.axis_index("lon")
    line = lax.rem(lon, 8)
    return lat, lon, lat // 2, lax.rem(lat, 2), lon // 8, line // 2, lax.rem(line, 2)


def sibling():
    lat, lon, y, zh, zl, x, core = place()
    return lat, zl * 8 + x * 2 + 1 - core


def plane_peers():
    lat, lon, y, zh, zl, x, core = place()
    out = []
    for dy in range(4):
        for dx in range(4):
            if dx or dy:
                py, px = lax.rem(y + dy, 4), lax.rem(x + dx, 4)
                out.append((dx if dy == 0 else 0, (py * 2 + zh, zl * 8 + px * 2 + core), py * 4 + px))
    return out


def near_peers():
    lat, lon, y, zh, zl, x, core = place()
    quad = (zl // 4) * 4
    return [(lat, (quad + lax.rem(zl + d, 4)) * 8 + x * 2 + core) for d in range(1, 4)]


def far_peers():
    lat, lon, y, zh, zl, x, core = place()
    out = []
    for d in range(1, 4):
        z = lax.rem(zh * 8 + zl + 4 * d, 16)
        out.append((y * 2 + z // 8, lax.rem(z, 8) * 8 + x * 2 + core))
    return out


def half_peer():
    lat, lon, y, zh, zl, x, core = place()
    return lat, lax.rem(zl + 4, 8) * 8 + x * 2 + core


class Reduce:
    def __init__(self, s, j):
        lat, lon, y, zh, zl, x, core = place()
        self.s, self.j, self.core, self.x = s, j, core, x
        self.own = y * 4 + x
        self.near, self.far, self.half = lax.rem(zl, 4), zh * 2 + zl // 4, zl // 4
        self.used = 0
        own, table = self.own, 16 + x
        near, far, half = self.near, self.far, self.half
        stages = [[self.copy(s.payload.at[j, 1 - core], s.in_core.at[j], sibling())], [], [], [], []]
        for i, (dx, peer, slot) in enumerate(plane_peers()):
            stages[1].append(self.copy(s.half.at[j, slot], s.in_plane.at[j, i], peer))
            stages[4].append(self.copy(s.red.at[j, core, own], s.red.at[j, core, own], peer))
            if dx:
                px = lax.rem(x + dx, 4)
                stages[1].append(self.copy(s.half.at[j, 13 + px], s.in_plane.at[j, 14 + dx], peer))
                stages[4].append(
                    self.copy(s.red.at[j, core, table], s.red.at[j, core, table], peer)
                )
        for peer in near_peers():
            stages[2].append(self.copy(s.near.at[j, near], s.near.at[j, near], peer))
        for peer in far_peers():
            stages[3].append(self.copy(s.far.at[j, far], s.far.at[j, far], peer))
        stages[3].append(self.copy(s.far_tab.at[j, half], s.far_tab.at[j, half], half_peer()))
        stages.append([self.copy(s.red.at[j, core], s.red.at[j, core], sibling())])
        self.stages = stages

    def copy(self, src, dst, peer):
        number, self.used = self.used, self.used + 1
        return pltpu.make_async_remote_copy(
            src_ref=src,
            dst_ref=dst,
            send_sem=self.s.ar_send.at[self.j, number],
            recv_sem=self.s.ar_recv.at[self.j, number],
            device_id=peer,
            device_id_type=MESH,
        )

    def step(self, number):
        s, j, core = self.s, self.j, self.core
        if number > 0:
            for copy in self.stages[number - 1]:
                copy.wait()
        if number == 1:
            for slot in range(16):
                total = s.payload[j, core, slot].astype(F32) + s.in_core[j, slot].astype(F32)
                s.half[j, slot] = total.astype(BF16)
        if number == 2:
            total = s.half[j, self.own].astype(F32)
            for i in range(15):
                total = total + s.in_plane[j, i].astype(F32)
            table = s.half[j, 13 + self.x].astype(F32)
            for i in range(15, 18):
                table = table + s.in_plane[j, i].astype(F32)
            s.near[j, self.near, 0:48] = total.astype(BF16)
            s.near[j, self.near, 48:96] = table.astype(BF16)
        if number == 3:
            total = s.near[j, 0].astype(F32)
            for i in range(1, 4):
                total = total + s.near[j, i].astype(F32)
            s.far[j, self.far] = total[0:48].astype(BF16)
            s.far_tab[j, self.half] = total[48:96].astype(BF16)
        if number == 4:
            total = s.far[j, 0].astype(F32)
            for i in range(1, 4):
                total = total + s.far[j, i].astype(F32)
            s.red[j, core, self.own] = total.astype(BF16)
            table = s.far_tab[j, 0].astype(F32) + s.far_tab[j, 1].astype(F32)
            s.red[j, core, 16 + self.x] = table.astype(BF16)
        if number < 6:
            for copy in self.stages[number]:
                copy.start()


def signal_partners():
    barrier = pltpu.get_barrier_semaphore()
    lat, lon = lax.axis_index("lat"), lax.axis_index("lon")
    nlat, nlon = lax.axis_size("lat"), lax.axis_size("lon")
    partners = [sibling()] + near_peers() + far_peers() + [p for _, p, _ in plane_peers()]
    partners.append(half_peer())
    for da, db in ((0, 1), (1, 0), (1, 1)):
        partners.append((lax.rem(lat + da, nlat), lax.rem(lon + db, nlon)))
        partners.append((lax.rem(lat - da + nlat, nlat), lax.rem(lon - db + nlon, nlon)))
    for partner in partners:
        pl.semaphore_signal(barrier, inc=1, device_id=partner, device_id_type=MESH)
    return barrier, len(partners)


SCRATCH = dict(
    x_in=pltpu.VMEM((6, 12, 2, 192), BF16),
    cot_in=pltpu.VMEM((6, 12, 2, 192), BF16),
    gains=pltpu.VMEM((2, 192), F32),
    wqkv=pltpu.VMEM((2, 192, 576), BF16),
    wproj=pltpu.VMEM((2, 192, 192), BF16),
    tab_in=pltpu.VMEM((2, 6, 23, 1, 144), F32),
    pad=pltpu.SMEM((48,), jnp.int32),
    loads=pltpu.SemaphoreType.DMA((7,)),
    tab=pltpu.VMEM((6, 24, 144), F32),
    wide=pltpu.VMEM((2, 144, 1024), F32),
    bias1=pltpu.VMEM((144, 864), F32),
    bias2=pltpu.VMEM((2, 72, 432), F32),
    ds=pltpu.VMEM((144, 1024), F32),
    normed=pltpu.VMEM((2, 144, 192), F32),
    inverse=pltpu.VMEM((2, 144, 1), F32),
    scaled=pltpu.VMEM((2, 144, 192), BF16),
    k=pltpu.VMEM((2, 144, 192), F32),
    v=pltpu.VMEM((2, 144, 192), F32),
    qm=pltpu.VMEM((2, 864, 192), BF16),
    probs=pltpu.VMEM((2, 144, 864), F32),
    mixed_t=pltpu.VMEM((2, 2, 192, 144), F32),
    grad=pltpu.VMEM((192, 768), F32),
    extra=pltpu.VMEM((192, 256), F32),
    halo_out=pltpu.VMEM((4, 4, 48, 192), BF16),
    halo_in=pltpu.VMEM((4, 4, 48, 192), BF16),
    payload=pltpu.VMEM((2, 2, 16, 48, 128), BF16),
    in_core=pltpu.VMEM((2, 16, 48, 128), BF16),
    half=pltpu.VMEM((2, 17, 48, 128), BF16),
    in_plane=pltpu.VMEM((2, 18, 48, 128), BF16),
    near=pltpu.VMEM((2, 4, 96, 128), BF16),
    far=pltpu.VMEM((2, 4, 48, 128), BF16),
    far_tab=pltpu.VMEM((2, 2, 48, 128), BF16),
    red=pltpu.VMEM((2, 2, 20, 48, 128), BF16),
    halo_send=pltpu.SemaphoreType.DMA((4, 3)),
    halo_recv=pltpu.SemaphoreType.DMA((4, 3)),
    ar_send=pltpu.SemaphoreType.DMA((2, 45)),
    ar_recv=pltpu.SemaphoreType.DMA((2, 45)),
)


class Names:
    pass


def main_kernel(
    x_ref, cot_ref, gains_ref, wqkv_ref, wproj_ref, tab_ref, pad_ref,
    out_ref, dx_ref, red_ref, *scratch,
):
    s = Names()
    for name, ref in zip(SCRATCH, scratch):
        setattr(s, name, ref)
    lat = lax.axis_index("lat")
    sources = dict(
        x_in=x_ref, tab_in=tab_ref, pad=pad_ref, gains=gains_ref, wqkv=wqkv_ref,
        wproj=wproj_ref, cot_in=cot_ref,
    )
    loads = {
        name: pltpu.make_async_copy(ref, getattr(s, name), s.loads.at[i])
        for i, (name, ref) in enumerate(sources.items())
    }
    for load in loads.values():
        load.start()
    barrier, expected = signal_partners()

    s.tab[...] = jnp.zeros((6, 24, 144), F32)
    s.ds[:, 768:1024] = jnp.zeros((144, 256), F32)
    s.extra[...] = jnp.zeros((192, 256), F32)
    s.half[:, 16] = jnp.zeros((2, 48, 128), BF16)
    s.red[:, :, 19] = jnp.zeros((2, 2, 48, 128), BF16)

    def field(ref):
        return ref[...].astype(F32).reshape(144, 192).astype(BF16)

    for name in ("tab_in", "pad"):
        loads[name].wait()
    expand_first(s, lat)
    for name in ("x_in", "gains", "wqkv", "wproj", "cot_in"):
        loads[name].wait()
    gain1, gain2 = s.gains[0:1, :], s.gains[1:2, :]
    x1 = nn(reorder("a", "n"), field(s.x_in))
    first = forward(s, 0, x1, gain1, s.wqkv, s.wproj, lambda g: s.bias1[...], 1)
    pl.semaphore_wait(barrier, expected)

    h_first, h_cot, h_out, h_grad = [Halo(s, i, i < 2) for i in range(4)]
    h_first.start(nn(reorder("s", "a"), first).astype(BF16))
    h_cot.start(nn(reorder("s", "n"), field(s.cot_in)).astype(BF16))
    expand_second(s, lat)
    x2 = nn(reorder("b", "s"), h_first.finish())
    second = forward(s, 1, x2, gain2, s.wqkv, s.wproj, lambda g: s.bias2[g], 2)
    h_out.start(nn(reorder("s", "b"), second).astype(BF16))
    g2 = nn(reorder("b", "s"), h_cot.finish()).astype(BF16)
    dh2, saved2 = backward(s, 1, g2, gain2, s.wqkv, s.wproj, 2)
    h_grad.start(nn(reorder("s", "b"), dh2).astype(BF16))
    gradients(s, 1, g2, saved2, fold_second(s), 2)
    reduce2, reduce1 = Reduce(s, 1), Reduce(s, 0)
    reduce2.step(0)
    out_ref[...] = nn(reorder("n", "s"), h_out.finish()).reshape(6, 12, 2, 192).astype(BF16)
    reduce2.step(1)
    g1 = nn(reorder("a", "s"), h_grad.finish()).astype(BF16)
    dx, saved1 = backward(s, 0, g1, gain1, s.wqkv, s.wproj, 1)
    reduce2.step(2)
    gradients(s, 0, g1, saved1, fold_first(s), 1)
    reduce1.step(0)
    dx_ref[...] = nn(reorder("n", "a"), dx).reshape(6, 12, 2, 192).astype(BF16)
    reduce1.step(1)
    reduce2.step(3)
    reduce1.step(2)
    reduce2.step(4)
    reduce1.step(3)
    reduce2.step(5)
    reduce1.step(4)
    reduce2.step(6)
    red_ref[1] = s.red[1]
    reduce1.step(5)
    reduce1.step(6)
    red_ref[0] = s.red[0]


def finish_kernel(red_ref, o_ref, d_ref, out_ref, dx_ref, gains_ref, dqkv_ref, dproj_ref, dtab_ref):
    out_ref[...] = o_ref[...]
    dx_ref[...] = d_ref[...]
    for j in range(2):
        for half in range(2):
            for slot in range(12):
                column, row = half * 3 + slot // 4, (slot % 4) * 48
                rows = slice(row, row + 48)
                value = red_ref[j, half, slot].astype(F32)
                if column < 4:
                    dqkv_ref[j, rows, 128 * column : 128 * column + 128] = value
                elif column == 4:
                    dqkv_ref[j, rows, 512:576] = value[:, 0:64]
                    dproj_ref[j, rows, 0:64] = value[:, 64:128]
                else:
                    dproj_ref[j, rows, 64:192] = value
            width = 128 if half == 0 else 16
            lanes = slice(128 * half, 128 * half + width)
            for third in range(3):
                value = red_ref[j, half, 16 + third].astype(F32)
                for i in range(2):
                    dtab_ref[j, 2 * third + i, :, 0, lanes] = value[24 * i : 24 * i + 23, 0:width]
        gains_ref[j : j + 1, 0:128] = red_ref[j, 0, 12].astype(F32)[0:1]
        gains_ref[j : j + 1, 128:192] = red_ref[j, 1, 12].astype(F32)[0:1, 0:64]


def body(inputs, cotangent, gains, qkv_weights, proj_weights, bias_tables, pad_rows):
    vmem = pl.BlockSpec(memory_space=pltpu.VMEM)
    hbm = pl.BlockSpec(memory_space=pltpu.HBM)
    field = jax.ShapeDtypeStruct((6, 12, 2, 192), BF16)
    out, dx, red = pl.pallas_call(
        main_kernel,
        out_shape=(field, field, jax.ShapeDtypeStruct((2, 2, 20, 48, 128), BF16)),
        in_specs=[hbm] * 7,
        out_specs=(vmem,) * 3,
        scratch_shapes=list(SCRATCH.values()),
        compiler_params=pltpu.CompilerParams(
            collective_id=0, has_side_effects=True, vmem_limit_bytes=48 * 2**20
        ),
        name="both_blocks",
    )(
        inputs.transpose(1, 2, 0, 3),
        cotangent.transpose(1, 2, 0, 3),
        gains,
        qkv_weights,
        proj_weights,
        bias_tables.transpose(0, 2, 3, 1, 4),
        pad_rows,
    )
    out, dx, d_gains, d_qkv, d_proj, d_tables = pl.pallas_call(
        finish_kernel,
        out_shape=(
            field,
            field,
            jax.ShapeDtypeStruct((2, 192), F32),
            jax.ShapeDtypeStruct((2, 192, 576), F32),
            jax.ShapeDtypeStruct((2, 192, 192), F32),
            jax.ShapeDtypeStruct((2, 6, 23, 1, 144), F32),
        ),
        in_specs=[vmem] * 3,
        out_specs=(vmem,) * 6,
        compiler_params=pltpu.CompilerParams(vmem_limit_bytes=32 * 2**20),
        name="unpack",
    )(red, out, dx)
    return (
        out.transpose(2, 0, 1, 3),
        dx.transpose(2, 0, 1, 3),
        d_gains,
        d_qkv,
        d_proj,
        d_tables.transpose(0, 3, 1, 2, 4),
    )


def solution(mesh):
    field = P(None, "lat", "lon", None)
    tables = P(None, "lat", None, None, None)
    return jax.shard_map(
        body,
        mesh=mesh,
        in_specs=(field, field, P(), P(), P(), tables, P()),
        out_specs=(field, field, P(), P(), P(), tables),
        check_vma=False,
    )
```

```python
import jax
import jax.numpy as jnp
from jax import lax
from jax.experimental import pallas as pl
from jax.experimental.pallas import tpu as pltpu
from jax.sharding import PartitionSpec as P

F32 = jnp.float32
BF16 = jnp.bfloat16
MESH = pl.DeviceIdType.MESH
HEADS = 6
VMEM_LIMIT = 62 * 2**20
SCALE = 32 ** (-0.5)


def div(x, d):
    return (x * (-(-(2**20) // d))) >> 20


def tokens_of(order, n):
    i = lax.broadcasted_iota(jnp.int32, (n, 1), 0)
    used = i < n
    if order == "n":
        r = div(i, 24)
        c = div(i - 24 * r, 2)
        l = i - 24 * r - 2 * c
    elif order == "a":
        c = div(i, 12)
        l = div(i - 12 * c, 6)
        r = i - 12 * c - 6 * l
    elif order == "b":
        l = div(i, 72)
        c = div(i - 72 * l, 6)
        r = i - 72 * l - 6 * c
    else:
        q = i >> 6
        inner = i - 64 * q
        used = inner < 36
        if order == "s1":
            inner, used = inner - 36, (inner >= 36) & (inner < 54)
        if order == "s2":
            inner, used = inner - 18, (inner >= 36) & (inner < 54)
        l = div(inner, 18)
        r = div(inner - 18 * l, 6)
        c = inner - 18 * l - 6 * r
        r, c = r + 3 * (q >> 1), c + 6 * (q & 1)
    return l, r, c, used


def place_in(order, l, r, c):
    if order == "n":
        return 24 * r + 2 * c + l
    if order == "a":
        return 12 * c + 6 * l + r
    if order == "b":
        return 72 * l + 6 * c + r
    lower, right = (r >= 3).astype(jnp.int32), (c >= 6).astype(jnp.int32)
    quarter = 64 * (2 * lower + right)
    inner = 18 * l + 6 * (r - 3 * lower) + c - 6 * right
    if order == "s":
        return quarter + inner
    if order == "s1":
        return jnp.where(inner < 18, quarter + 36 + inner, -1)
    return jnp.where(inner >= 18, quarter + 18 + inner, -1)


def reorder(to, of):
    n, m = [256 if order[0] == "s" else 144 for order in (to, of)]
    l, r, c, used = tokens_of(to, n)
    place = jnp.where(used, place_in(of, l, r, c), -1)
    return jnp.where(place == lax.broadcasted_iota(jnp.int32, (n, m), 1), 1.0, 0.0).astype(BF16)


def pack(x, order):
    wide, rest = x[:, 0:128], x[:, 128:192]
    pairs = [nn(reorder(to, order), rest) for to in ("s1", "s2")]
    return (nn(reorder("s", order), wide) + jnp.concatenate(pairs, 1)).astype(BF16)


def unpack(x, order):
    left, right = nn(reorder(order, "s1"), x), nn(reorder(order, "s2"), x)
    rest = left[:, 0:64] + right[:, 64:128]
    return jnp.concatenate([nn(reorder(order, "s"), x), rest], 1)


def spread(lanes, step, par, parts):
    i = lax.broadcasted_iota(jnp.int32, (72 * parts, 1), 0)
    part = div(i, 72)
    h = div(i - 72 * part, 24)
    o = i - 72 * part - 24 * h
    start = 12 * step * par + 24 * step * h + (22 - o) * step
    at = lax.broadcasted_iota(jnp.int32, (72 * parts, lanes), 1) - start
    return jnp.where((at >= 0) & (at < step), 1.0, 0.0).astype(BF16)


def lane_info(lanes, step):
    lane = lax.broadcasted_iota(jnp.int32, (1, lanes), 1)
    head = div(lane, 12 * step)
    parity = jnp.where(head < HEADS, head & 1, 2)
    return lane - step * div(lane, step), lane - 12 * step * head, parity


def nn(a, b):
    return lax.dot_general(a, b, (((1,), (0,)), ((), ())), preferred_element_type=F32)


def nt(a, b):
    return lax.dot_general(a, b, (((1,), (1,)), ((), ())), preferred_element_type=F32)


def tn(a, b):
    return lax.dot_general(a, b, (((0,), (0,)), ((), ())), preferred_element_type=F32)


def head_stack(x):
    lane = lax.broadcasted_iota(jnp.int32, (1, 192), 1)
    parts = [jnp.where((lane >= 32 * h) & (lane < 32 * h + 32), x, 0.0) for h in range(HEADS)]
    return jnp.concatenate(parts, 0).astype(BF16)


def head_diagonal(x, n):
    return jnp.concatenate(
        [x[32 * h : 32 * h + 32, n * h : n * h + n] for h in range(HEADS)], 0
    )


def split_table(s, block):
    out = []
    for h in range(HEADS):
        s.tab[h, 0:23, :] = s.tab_in[block, h, :, 0, :]
    for par in range(2):
        parts = [[], [], []]
        for h in range(3):
            t = s.tab[2 * h + par]
            hi = t.astype(BF16).astype(F32)
            rest = t - hi
            mid = rest.astype(BF16).astype(F32)
            for part, value in zip(parts, (hi, mid, rest - mid)):
                part.append(value)
        out.append(jnp.concatenate(sum(parts, []), 0).astype(BF16))
    return out


def row_flags(s, start):
    rows = lax.broadcasted_iota(jnp.int32, (6, 1), 0)
    flags = jnp.zeros((6, 1), jnp.int32)
    for r in range(6):
        flags = jnp.where(rows == r, s.pad[lax.rem(start + r, 48)], flags)
    return rows, flags == 1


def expand_first(s, lat):
    for par, parts in enumerate(split_table(s, 0)):
        s.wide[par] = tn(parts, spread(1024, 12, par, 3))
    entry, token, parity = lane_info(1024, 12)
    token, odd = token[:, 0:864], parity[:, 0:864] == 1
    rows, valid = row_flags(s, 6 * lat)
    for lk in range(2):
        strips = []
        for par in range(2):
            strip = jnp.zeros((6, 1024), F32)
            for e in range(12):
                at = 72 * (e // 6) + 36 * lk + 6 * (e % 6)
                strip = jnp.where(entry == e, s.wide[par, at : at + 6, :], strip)
            strips.append(strip)
        for ck in range(12):
            turn = (1024 - (11 - ck) * 12) % 1024
            even_part, odd_part = [
                (pltpu.roll(x, turn, 1) if turn else x)[:, 0:864] for x in strips
            ]
            at = 12 * ck + 6 * lk
            keep = valid | (token == rows + at)
            s.bias1[at : at + 6, :] = jnp.where(
                keep, jnp.where(odd, odd_part, even_part), -1e30
            )


def expand_second(s, lat):
    for par, parts in enumerate(split_table(s, 1)):
        s.wide[par, :, 0:512] = tn(parts, spread(512, 6, par, 3))
    entry, token, parity = lane_info(512, 6)
    token, odd = token[:, 0:432], parity[:, 0:432] == 1
    rows, valid = row_flags(s, 6 * lat + 3)
    q_band = jnp.where(lat == 7, (entry[:, 0:432] >= 3).astype(jnp.int32), 0)
    k_band = jnp.where(lat == 7, (rows >= 3).astype(jnp.int32), 0)
    same = q_band == k_band
    for lev in range(2):
        strips = []
        for par in range(2):
            strip = jnp.zeros((6, 512), F32)
            for e in range(6):
                at = 108 * (1 - lev) + 6 * e
                strip = jnp.where(entry == e, s.wide[par, at : at + 6, 0:512], strip)
            strips.append(strip)
        for ck in range(12):
            turn = (512 - (11 - ck) * 6) % 512
            even_part, odd_part = [
                (pltpu.roll(x, turn, 1) if turn else x)[:, 0:432] for x in strips
            ]
            at = 6 * ck
            keep = (valid | (token == rows + at)) & same
            s.bias2[lev, at : at + 6, :] = jnp.where(
                keep, jnp.where(odd, odd_part, even_part), -1e30
            )


def fold_first(s):
    entry, _, parity = lane_info(1024, 12)
    for par in range(2):
        mine = parity == par
        for lk in range(2):
            acc = jnp.zeros((6, 1024), F32)
            for ck in range(12):
                at = 12 * ck + 6 * lk
                piece = jnp.where(mine, s.ds[at : at + 6, :], 0.0)
                turn = (11 - ck) * 12
                acc = acc + (pltpu.roll(piece, turn, 1) if turn else piece)
            for e in range(12):
                at = 72 * (e // 6) + 36 * lk + 6 * (e % 6)
                s.wide[par, at : at + 6, :] = jnp.where(entry == e, acc, 0.0)
    return [nt(spread(1024, 12, par, 1), s.wide[par].astype(BF16)) for par in range(2)]


def fold_second(s):
    entry, _, parity = lane_info(512, 6)
    s.wide[:, :, 0:512] = jnp.zeros((2, 144, 512), F32)
    for par in range(2):
        mine = parity == par
        for lev in range(2):
            acc = jnp.zeros((6, 512), F32)
            for ck in range(12):
                at = 72 * lev + 6 * ck
                piece = jnp.where(mine, s.ds[at : at + 6, 0:512], 0.0)
                turn = (11 - ck) * 6
                acc = acc + (pltpu.roll(piece, turn, 1) if turn else piece)
            for e in range(6):
                at = 108 * (1 - lev) + 6 * e
                s.wide[par, at : at + 6, 0:512] = jnp.where(entry == e, acc, 0.0)
    return [nt(spread(512, 6, par, 1), s.wide[par, :, 0:512].astype(BF16)) for par in range(2)]


def forward(s, j, x, gain, wqkv_ref, wproj_ref, bias, groups):
    n = 144 // groups
    center = x - jnp.mean(x, -1, keepdims=True)
    inverse = lax.rsqrt(jnp.mean(center * center, -1, keepdims=True) + 1e-05)
    normed = center * inverse
    scaled = (normed * gain).astype(BF16)
    packed = nn(scaled, wqkv_ref[j])
    q, k, v = packed[:, 0:192], packed[:, 192:384], packed[:, 384:576]
    s.normed[j] = normed
    s.inverse[j] = inverse
    s.scaled[j] = scaled
    s.k[j] = k
    s.v[j] = v
    attended = []
    for g in range(groups):
        rows = slice(g * n, g * n + n)
        qm = head_stack(q[rows])
        s.qm[j, g * 6 * n : (g + 1) * 6 * n, :] = qm
        scores = nt(k[rows].astype(BF16), qm) * SCALE + bias(g)
        weight = jnp.exp(scores - jnp.max(scores, 0, keepdims=True))
        probs = weight * (1.0 / jnp.sum(weight, 0, keepdims=True))
        s.probs[j, rows, 0 : 6 * n] = probs
        mixed_t = head_diagonal(tn(v[rows].astype(BF16), probs.astype(BF16)), n)
        s.mixed_t[j, g, :, 0:n] = mixed_t
        attended.append(tn(mixed_t.astype(BF16), wproj_ref[j]))
    att = attended[0] if groups == 1 else jnp.concatenate(attended, 0)
    return (x + att).astype(BF16)


def backward(s, j, g_in, gain, wqkv_ref, wproj_ref, groups):
    n = 144 // groups
    back = nt(g_in, wproj_ref[j])
    dqs, dks, dvs = [], [], []
    for g in range(groups):
        rows = slice(g * n, g * n + n)
        backm = head_stack(back[rows])
        probs = s.probs[j, rows, 0 : 6 * n]
        k = s.k[j, rows, :].astype(BF16)
        v = s.v[j, rows, :].astype(BF16)
        qm = s.qm[j, g * 6 * n : (g + 1) * 6 * n, :]
        d_probs = nt(v, backm)
        dvs.append(nn(probs.astype(BF16), backm))
        d_scores = probs * (d_probs - jnp.sum(d_probs * probs, 0, keepdims=True))
        s.ds[rows, 0 : 6 * n] = d_scores
        d_rounded = (d_scores * SCALE).astype(BF16)
        dks.append(nn(d_rounded, qm))
        dqs.append(head_diagonal(tn(k, d_rounded), n).T)
    if groups == 1:
        dq, dk, dv = dqs[0], dks[0], dvs[0]
    else:
        dq, dk, dv = [jnp.concatenate(p, 0) for p in (dqs, dks, dvs)]
    dq, dk, dv = dq.astype(BF16), dk.astype(BF16), dv.astype(BF16)
    w = wqkv_ref[j]
    d_scaled = nt(dq, w[:, 0:192]) + nt(dk, w[:, 192:384]) + nt(dv, w[:, 384:576])
    normed = s.normed[j]
    d_normed = d_scaled * gain
    d_hidden = s.inverse[j] * (
        d_normed
        - jnp.mean(d_normed, -1, keepdims=True)
        - normed * jnp.mean(d_normed * normed, -1, keepdims=True)
    )
    result = (g_in.astype(F32) + d_hidden).astype(BF16)
    return result, (dq, dk, dv, d_scaled)


def gradients(s, j, g_in, saved, folded, groups):
    n = 144 // groups
    dq, dk, dv, d_scaled = saved
    scaled = s.scaled[j]
    s.grad[:, 0:192] = tn(scaled, dq)
    s.grad[:, 192:384] = tn(scaled, dk)
    s.grad[:, 384:576] = tn(scaled, dv)
    d_proj = jnp.zeros((192, 192), F32)
    for g in range(groups):
        d_proj = d_proj + nn(
            s.mixed_t[j, g, :, 0:n].astype(BF16), g_in[g * n : g * n + n]
        )
    s.grad[:, 576:768] = d_proj
    for h in range(HEADS):
        s.extra[24 * h : 24 * h + 24, 0:144] = folded[h % 2][24 * (h // 2) : 24 * (h // 2) + 24]
    s.extra[144:145, 0:192] = jnp.sum(d_scaled * s.normed[j], 0, keepdims=True)
    for half in range(2):
        for slot in range(12):
            column, row = half * 384 + (slot // 4) * 128, (slot % 4) * 48
            s.payload[j, half, slot] = s.grad[row : row + 48, column : column + 128].astype(BF16)
        for slot, row in ((12, 144), (13, 0), (14, 48), (15, 96)):
            s.payload[j, half, slot] = s.extra[
                row : row + 48, 128 * half : 128 * half + 128
            ].astype(BF16)


class Halo:
    def __init__(self, s, which, forward_shift):
        lat, lon = lax.axis_index("lat"), lax.axis_index("lon")
        nlat, nlon = lax.axis_size("lat"), lax.axis_size("lon")
        self.s, self.which = s, which
        self.copies = []
        self.stay = 3 if forward_shift else 0
        for i, quarter in enumerate(q for q in range(4) if q != self.stay):
            if forward_shift:
                by_lat, by_lon = quarter // 2 - 1 + nlat, quarter % 2 - 1 + nlon
            else:
                by_lat, by_lon = quarter // 2, quarter % 2
            self.copies.append(
                pltpu.make_async_remote_copy(
                    src_ref=s.halo_out.at[which, quarter],
                    dst_ref=s.halo_in.at[which, 3 - quarter],
                    send_sem=s.halo_send.at[which, i],
                    recv_sem=s.halo_recv.at[which, i],
                    device_id=(lax.rem(lat + by_lat, nlat), lax.rem(lon + by_lon, nlon)),
                    device_id_type=MESH,
                )
            )

    def start(self, quarters):
        for q in range(4):
            self.s.halo_out[self.which, q] = quarters[64 * q : 64 * q + 64]
        for copy in self.copies:
            copy.start()
        stay = self.stay
        self.s.halo_in[self.which, 3 - stay] = quarters[64 * stay : 64 * stay + 64]

    def finish(self):
        for copy in self.copies:
            copy.wait()
        return self.s.halo_in[self.which].reshape(256, 128)


def place():
    lat, lon = lax.axis_index("lat"), lax.axis_index("lon")
    line = lax.rem(lon, 8)
    return lat, lon, lat // 2, lax.rem(lat, 2), lon // 8, line // 2, lax.rem(line, 2)


def sibling():
    lat, lon, y, zh, zl, x, core = place()
    return lat, zl * 8 + x * 2 + 1 - core


def plane_peers():
    lat, lon, y, zh, zl, x, core = place()
    out = []
    for dy in range(4):
        for dx in range(4):
            if dx or dy:
                py, px = lax.rem(y + dy, 4), lax.rem(x + dx, 4)
                out.append((dx if dy == 0 else 0, (py * 2 + zh, zl * 8 + px * 2 + core), py * 4 + px))
    return out


def near_peers():
    lat, lon, y, zh, zl, x, core = place()
    quad = (zl // 4) * 4
    return [(lat, (quad + lax.rem(zl + d, 4)) * 8 + x * 2 + core) for d in range(1, 4)]


def far_peers():
    lat, lon, y, zh, zl, x, core = place()
    out = []
    for d in range(1, 4):
        z = lax.rem(zh * 8 + zl + 4 * d, 16)
        out.append((y * 2 + z // 8, lax.rem(z, 8) * 8 + x * 2 + core))
    return out


def half_peer():
    lat, lon, y, zh, zl, x, core = place()
    return lat, lax.rem(zl + 4, 8) * 8 + x * 2 + core


class Reduce:
    def __init__(self, s, j):
        lat, lon, y, zh, zl, x, core = place()
        self.s, self.j, self.core, self.x = s, j, core, x
        self.own = y * 4 + x
        self.near, self.far, self.half = lax.rem(zl, 4), zh * 2 + zl // 4, zl // 4
        self.used = 0
        own, table = self.own, 16 + x
        near, far, half = self.near, self.far, self.half
        stages = [[self.copy(s.payload.at[j, 1 - core], s.in_core.at[j], sibling())], [], [], [], []]
        for i, (dx, peer, slot) in enumerate(plane_peers()):
            stages[1].append(self.copy(s.half.at[j, slot], s.in_plane.at[j, i], peer))
            stages[4].append(self.copy(s.red.at[j, core, own], s.red.at[j, core, own], peer))
            if dx:
                px = lax.rem(x + dx, 4)
                stages[1].append(self.copy(s.half.at[j, 13 + px], s.in_plane.at[j, 14 + dx], peer))
                stages[4].append(
                    self.copy(s.red.at[j, core, table], s.red.at[j, core, table], peer)
                )
        for peer in near_peers():
            stages[2].append(self.copy(s.near.at[j, near], s.near.at[j, near], peer))
        for peer in far_peers():
            stages[3].append(self.copy(s.far.at[j, far], s.far.at[j, far], peer))
        stages[3].append(self.copy(s.far_tab.at[j, half], s.far_tab.at[j, half], half_peer()))
        stages.append([self.copy(s.red.at[j, core], s.red.at[j, core], sibling())])
        self.stages = stages

    def copy(self, src, dst, peer):
        number, self.used = self.used, self.used + 1
        return pltpu.make_async_remote_copy(
            src_ref=src,
            dst_ref=dst,
            send_sem=self.s.ar_send.at[self.j, number],
            recv_sem=self.s.ar_recv.at[self.j, number],
            device_id=peer,
            device_id_type=MESH,
        )

    def step(self, number):
        s, j, core = self.s, self.j, self.core
        if number > 0:
            for copy in self.stages[number - 1]:
                copy.wait()
        if number == 1:
            for slot in range(16):
                total = s.payload[j, core, slot].astype(F32) + s.in_core[j, slot].astype(F32)
                s.half[j, slot] = total.astype(BF16)
        if number == 2:
            total = s.half[j, self.own].astype(F32)
            for i in range(15):
                total = total + s.in_plane[j, i].astype(F32)
            table = s.half[j, 13 + self.x].astype(F32)
            for i in range(15, 18):
                table = table + s.in_plane[j, i].astype(F32)
            s.near[j, self.near, 0:48] = total.astype(BF16)
            s.near[j, self.near, 48:96] = table.astype(BF16)
        if number == 3:
            total = s.near[j, 0].astype(F32)
            for i in range(1, 4):
                total = total + s.near[j, i].astype(F32)
            s.far[j, self.far] = total[0:48].astype(BF16)
            s.far_tab[j, self.half] = total[48:96].astype(BF16)
        if number == 4:
            total = s.far[j, 0].astype(F32)
            for i in range(1, 4):
                total = total + s.far[j, i].astype(F32)
            s.red[j, core, self.own] = total.astype(BF16)
            table = s.far_tab[j, 0].astype(F32) + s.far_tab[j, 1].astype(F32)
            s.red[j, core, 16 + self.x] = table.astype(BF16)
        if number < 6:
            for copy in self.stages[number]:
                copy.start()


def signal_partners():
    barrier = pltpu.get_barrier_semaphore()
    lat, lon = lax.axis_index("lat"), lax.axis_index("lon")
    nlat, nlon = lax.axis_size("lat"), lax.axis_size("lon")
    partners = [sibling()] + near_peers() + far_peers() + [p for _, p, _ in plane_peers()]
    partners.append(half_peer())
    for da, db in ((0, 1), (1, 0), (1, 1)):
        partners.append((lax.rem(lat + da, nlat), lax.rem(lon + db, nlon)))
        partners.append((lax.rem(lat - da + nlat, nlat), lax.rem(lon - db + nlon, nlon)))
    for partner in partners:
        pl.semaphore_signal(barrier, inc=1, device_id=partner, device_id_type=MESH)
    return barrier, len(partners)


SCRATCH = dict(
    x_in=pltpu.VMEM((6, 12, 2, 192), BF16),
    cot_in=pltpu.VMEM((6, 12, 2, 192), BF16),
    gains=pltpu.VMEM((2, 192), F32),
    wqkv=pltpu.VMEM((2, 192, 576), BF16),
    wproj=pltpu.VMEM((2, 192, 192), BF16),
    tab_in=pltpu.VMEM((2, 6, 23, 1, 144), F32),
    pad=pltpu.SMEM((48,), jnp.int32),
    loads=pltpu.SemaphoreType.DMA((7,)),
    out=pltpu.VMEM((6, 12, 2, 192), BF16),
    dx=pltpu.VMEM((6, 12, 2, 192), BF16),
    stores=pltpu.SemaphoreType.DMA((4,)),
    tab=pltpu.VMEM((6, 24, 144), F32),
    wide=pltpu.VMEM((2, 144, 1024), F32),
    bias1=pltpu.VMEM((144, 864), F32),
    bias2=pltpu.VMEM((2, 72, 432), F32),
    ds=pltpu.VMEM((144, 1024), F32),
    normed=pltpu.VMEM((2, 144, 192), F32),
    inverse=pltpu.VMEM((2, 144, 1), F32),
    scaled=pltpu.VMEM((2, 144, 192), BF16),
    k=pltpu.VMEM((2, 144, 192), F32),
    v=pltpu.VMEM((2, 144, 192), F32),
    qm=pltpu.VMEM((2, 864, 192), BF16),
    probs=pltpu.VMEM((2, 144, 864), F32),
    mixed_t=pltpu.VMEM((2, 2, 192, 144), F32),
    grad=pltpu.VMEM((192, 768), F32),
    extra=pltpu.VMEM((192, 256), F32),
    halo_out=pltpu.VMEM((4, 4, 64, 128), BF16),
    halo_in=pltpu.VMEM((4, 4, 64, 128), BF16),
    payload=pltpu.VMEM((2, 2, 16, 48, 128), BF16),
    in_core=pltpu.VMEM((2, 16, 48, 128), BF16),
    half=pltpu.VMEM((2, 17, 48, 128), BF16),
    in_plane=pltpu.VMEM((2, 18, 48, 128), BF16),
    near=pltpu.VMEM((2, 4, 96, 128), BF16),
    far=pltpu.VMEM((2, 4, 48, 128), BF16),
    far_tab=pltpu.VMEM((2, 2, 48, 128), BF16),
    red=pltpu.VMEM((2, 2, 20, 48, 128), BF16),
    halo_send=pltpu.SemaphoreType.DMA((4, 3)),
    halo_recv=pltpu.SemaphoreType.DMA((4, 3)),
    ar_send=pltpu.SemaphoreType.DMA((2, 45)),
    ar_recv=pltpu.SemaphoreType.DMA((2, 45)),
)


class Names:
    pass


def main_kernel(
    x_ref, cot_ref, gains_ref, wqkv_ref, wproj_ref, tab_ref, pad_ref,
    out_ref, dx_ref, red_ref, *scratch,
):
    s = Names()
    for name, ref in zip(SCRATCH, scratch):
        setattr(s, name, ref)
    lat = lax.axis_index("lat")
    sources = dict(
        x_in=x_ref, tab_in=tab_ref, pad=pad_ref, gains=gains_ref, wqkv=wqkv_ref,
        wproj=wproj_ref, cot_in=cot_ref,
    )
    loads = {
        name: pltpu.make_async_copy(ref, getattr(s, name), s.loads.at[i])
        for i, (name, ref) in enumerate(sources.items())
    }
    for load in loads.values():
        load.start()
    barrier, expected = signal_partners()

    s.tab[...] = jnp.zeros((6, 24, 144), F32)
    s.ds[:, 768:1024] = jnp.zeros((144, 256), F32)
    s.extra[...] = jnp.zeros((192, 256), F32)
    s.half[:, 16] = jnp.zeros((2, 48, 128), BF16)
    s.red[:, :, 19] = jnp.zeros((2, 2, 48, 128), BF16)

    def field(ref):
        return ref[...].astype(F32).reshape(144, 192).astype(BF16)

    def store(number, value, ref):
        copy = pltpu.make_async_copy(value, ref, s.stores.at[number])
        copy.start()
        return copy

    for name in ("tab_in", "pad"):
        loads[name].wait()
    expand_first(s, lat)
    for name in ("x_in", "gains", "wqkv", "wproj", "cot_in"):
        loads[name].wait()
    gain1, gain2 = s.gains[0:1, :], s.gains[1:2, :]
    h_first, h_cot, h_out, h_grad = [Halo(s, i, i < 2) for i in range(4)]
    reduce2, reduce1 = Reduce(s, 1), Reduce(s, 0)
    cot = pack(field(s.cot_in), "n")
    x1 = nn(reorder("a", "n"), field(s.x_in))
    pl.semaphore_wait(barrier, expected)
    h_cot.start(cot)

    first = forward(s, 0, x1, gain1, s.wqkv, s.wproj, lambda g: s.bias1[...], 1)
    h_first.start(pack(first, "a"))
    expand_second(s, lat)
    x2 = unpack(h_first.finish(), "b")
    second = forward(s, 1, x2, gain2, s.wqkv, s.wproj, lambda g: s.bias2[g], 2)
    g2 = unpack(h_cot.finish(), "b").astype(BF16)
    dh2, saved2 = backward(s, 1, g2, gain2, s.wqkv, s.wproj, 2)
    h_grad.start(pack(dh2, "b"))
    h_out.start(pack(second, "b"))
    gradients(s, 1, g2, saved2, fold_second(s), 2)
    reduce2.step(0)
    reduce2.step(1)
    g1 = unpack(h_grad.finish(), "a").astype(BF16)
    dx, saved1 = backward(s, 0, g1, gain1, s.wqkv, s.wproj, 1)
    reduce2.step(2)
    gradients(s, 0, g1, saved1, fold_first(s), 1)
    reduce1.step(0)
    s.dx[...] = nn(reorder("n", "a"), dx).reshape(6, 12, 2, 192).astype(BF16)
    stores = [store(0, s.dx, dx_ref)]
    reduce1.step(1)
    s.out[...] = unpack(h_out.finish(), "n").reshape(6, 12, 2, 192).astype(BF16)
    stores.append(store(1, s.out, out_ref))
    reduce2.step(3)
    reduce1.step(2)
    reduce2.step(4)
    reduce1.step(3)
    reduce2.step(5)
    reduce1.step(4)
    reduce2.step(6)
    stores.append(store(2, s.red.at[1], red_ref.at[1]))
    reduce1.step(5)
    reduce1.step(6)
    stores.append(store(3, s.red.at[0], red_ref.at[0]))
    for copy in stores:
        copy.wait()


def finish_kernel(
    red_ref, o_ref, d_ref, out_ref, dx_ref, gains_ref, dqkv_ref, dproj_ref, dtab_ref, red, sems
):
    copies = [
        pltpu.make_async_copy(source, target, sems.at[i])
        for i, (source, target) in enumerate(
            ((red_ref.at[1], red.at[1]), (red_ref.at[0], red.at[0]), (o_ref, out_ref), (d_ref, dx_ref))
        )
    ]
    for copy in copies:
        copy.start()
    for j in (1, 0):
        copies[1 - j].wait()
        for half in range(2):
            for slot in range(12):
                column, row = half * 3 + slot // 4, (slot % 4) * 48
                rows = slice(row, row + 48)
                value = red[j, half, slot].astype(F32)
                if column < 4:
                    dqkv_ref[j, rows, 128 * column : 128 * column + 128] = value
                elif column == 4:
                    dqkv_ref[j, rows, 512:576] = value[:, 0:64]
                    dproj_ref[j, rows, 0:64] = value[:, 64:128]
                else:
                    dproj_ref[j, rows, 64:192] = value
            width = 128 if half == 0 else 16
            lanes = slice(128 * half, 128 * half + width)
            for third in range(3):
                value = red[j, half, 16 + third].astype(F32)
                for i in range(2):
                    dtab_ref[j, 2 * third + i, :, 0, lanes] = value[24 * i : 24 * i + 23, 0:width]
        gains_ref[j : j + 1, 0:128] = red[j, 0, 12].astype(F32)[0:1]
        gains_ref[j : j + 1, 128:192] = red[j, 1, 12].astype(F32)[0:1, 0:64]
    for copy in copies[2:]:
        copy.wait()


def body(inputs, cotangent, gains, qkv_weights, proj_weights, bias_tables, pad_rows):
    vmem = pl.BlockSpec(memory_space=pltpu.VMEM)
    hbm = pl.BlockSpec(memory_space=pltpu.HBM)
    field = jax.ShapeDtypeStruct((6, 12, 2, 192), BF16)
    out, dx, red = pl.pallas_call(
        main_kernel,
        out_shape=(field, field, jax.ShapeDtypeStruct((2, 2, 20, 48, 128), BF16)),
        in_specs=[hbm] * 7,
        out_specs=(hbm,) * 3,
        scratch_shapes=list(SCRATCH.values()),
        compiler_params=pltpu.CompilerParams(
            collective_id=0, has_side_effects=True, vmem_limit_bytes=VMEM_LIMIT
        ),
        name="both_blocks",
    )(
        inputs.transpose(1, 2, 0, 3),
        cotangent.transpose(1, 2, 0, 3),
        gains,
        qkv_weights,
        proj_weights,
        bias_tables.transpose(0, 2, 3, 1, 4),
        pad_rows,
    )
    out, dx, d_gains, d_qkv, d_proj, d_tables = pl.pallas_call(
        finish_kernel,
        out_shape=(
            field,
            field,
            jax.ShapeDtypeStruct((2, 192), F32),
            jax.ShapeDtypeStruct((2, 192, 576), F32),
            jax.ShapeDtypeStruct((2, 192, 192), F32),
            jax.ShapeDtypeStruct((2, 6, 23, 1, 144), F32),
        ),
        in_specs=[hbm] * 3,
        out_specs=(vmem,) * 6,
        scratch_shapes=[
            pltpu.VMEM((2, 2, 20, 48, 128), BF16),
            pltpu.SemaphoreType.DMA((4,)),
        ],
        compiler_params=pltpu.CompilerParams(vmem_limit_bytes=VMEM_LIMIT),
        name="unpack",
    )(red, out, dx)
    return (
        out.transpose(2, 0, 1, 3),
        dx.transpose(2, 0, 1, 3),
        d_gains,
        d_qkv,
        d_proj,
        d_tables.transpose(0, 3, 1, 2, 4),
    )


def solution(mesh):
    field = P(None, "lat", "lon", None)
    tables = P(None, "lat", None, None, None)
    return jax.shard_map(
        body,
        mesh=mesh,
        in_specs=(field, field, P(), P(), P(), tables, P()),
        out_specs=(field, field, P(), P(), P(), tables),
        check_vma=False,
    )
```

```python
import jax
import jax.numpy as jnp
from jax import lax
from jax.experimental import pallas as pl
from jax.experimental.pallas import tpu as pltpu
from jax.sharding import PartitionSpec as P

F32 = jnp.float32
BF16 = jnp.bfloat16
MESH = pl.DeviceIdType.MESH
HEADS = 6
VMEM_LIMIT = 62 * 2**20
SCALE = 32 ** (-0.5)


def div(x, d):
    return (x * (-(-(2**20) // d))) >> 20


def tokens_of(order, n):
    i = lax.broadcasted_iota(jnp.int32, (n, 1), 0)
    used = i < n
    if order == "n":
        r = div(i, 24)
        c = div(i - 24 * r, 2)
        l = i - 24 * r - 2 * c
    elif order == "a":
        c = div(i, 12)
        l = div(i - 12 * c, 6)
        r = i - 12 * c - 6 * l
    elif order == "b":
        l = div(i, 72)
        c = div(i - 72 * l, 6)
        r = i - 72 * l - 6 * c
    else:
        q = i >> 6
        inner = i - 64 * q
        used = inner < 36
        if order == "s1":
            inner, used = inner - 36, (inner >= 36) & (inner < 54)
        if order == "s2":
            inner, used = inner - 18, (inner >= 36) & (inner < 54)
        l = div(inner, 18)
        r = div(inner - 18 * l, 6)
        c = inner - 18 * l - 6 * r
        r, c = r + 3 * (q >> 1), c + 6 * (q & 1)
    return l, r, c, used


def place_in(order, l, r, c):
    if order == "n":
        return 24 * r + 2 * c + l
    if order == "a":
        return 12 * c + 6 * l + r
    if order == "b":
        return 72 * l + 6 * c + r
    lower, right = (r >= 3).astype(jnp.int32), (c >= 6).astype(jnp.int32)
    quarter = 64 * (2 * lower + right)
    inner = 18 * l + 6 * (r - 3 * lower) + c - 6 * right
    if order == "s":
        return quarter + inner
    if order == "s1":
        return jnp.where(inner < 18, quarter + 36 + inner, -1)
    return jnp.where(inner >= 18, quarter + 18 + inner, -1)


def reorder(to, of):
    n, m = [256 if order[0] == "s" else 144 for order in (to, of)]
    l, r, c, used = tokens_of(to, n)
    place = jnp.where(used, place_in(of, l, r, c), -1)
    return jnp.where(place == lax.broadcasted_iota(jnp.int32, (n, m), 1), 1.0, 0.0).astype(BF16)


def pack(x, order):
    wide, rest = x[:, 0:128], x[:, 128:192]
    pairs = [nn(reorder(to, order), rest) for to in ("s1", "s2")]
    return (nn(reorder("s", order), wide) + jnp.concatenate(pairs, 1)).astype(BF16)


def unpack(x, order):
    left, right = nn(reorder(order, "s1"), x), nn(reorder(order, "s2"), x)
    rest = left[:, 0:64] + right[:, 64:128]
    return jnp.concatenate([nn(reorder(order, "s"), x), rest], 1)


def spread(lanes, step, par, parts):
    i = lax.broadcasted_iota(jnp.int32, (72 * parts, 1), 0)
    part = div(i, 72)
    h = div(i - 72 * part, 24)
    o = i - 72 * part - 24 * h
    start = 12 * step * par + 24 * step * h + (22 - o) * step
    at = lax.broadcasted_iota(jnp.int32, (72 * parts, lanes), 1) - start
    return jnp.where((at >= 0) & (at < step), 1.0, 0.0).astype(BF16)


def lane_info(lanes, step):
    lane = lax.broadcasted_iota(jnp.int32, (1, lanes), 1)
    head = div(lane, 12 * step)
    parity = jnp.where(head < HEADS, head & 1, 2)
    return lane - step * div(lane, step), lane - 12 * step * head, parity


def nn(a, b):
    return lax.dot_general(a, b, (((1,), (0,)), ((), ())), preferred_element_type=F32)


def nt(a, b):
    return lax.dot_general(a, b, (((1,), (1,)), ((), ())), preferred_element_type=F32)


def tn(a, b):
    return lax.dot_general(a, b, (((0,), (0,)), ((), ())), preferred_element_type=F32)


def head_stack(x):
    lane = lax.broadcasted_iota(jnp.int32, (1, 192), 1)
    parts = [jnp.where((lane >= 32 * h) & (lane < 32 * h + 32), x, 0.0) for h in range(HEADS)]
    return jnp.concatenate(parts, 0).astype(BF16)


def head_diagonal(x, n):
    return jnp.concatenate(
        [x[32 * h : 32 * h + 32, n * h : n * h + n] for h in range(HEADS)], 0
    )


def split_table(tab):
    out = []
    for par in range(2):
        parts = [[], [], []]
        for h in range(3):
            t = tab[2 * h + par]
            hi = t.astype(BF16).astype(F32)
            rest = t - hi
            mid = rest.astype(BF16).astype(F32)
            for part, value in zip(parts, (hi, mid, rest - mid)):
                part.append(value)
        out.append(jnp.concatenate(sum(parts, []), 0).astype(BF16))
    return out


def row_flags(s, start):
    rows = lax.broadcasted_iota(jnp.int32, (6, 1), 0)
    flags = jnp.zeros((6, 1), jnp.int32)
    for r in range(6):
        flags = jnp.where(rows == r, s.pad[lax.rem(start + r, 48)], flags)
    return rows, flags == 1


def expand_first(s, lat):
    for h in range(HEADS):
        s.tab[h, 0:23, :] = s.tab_in[0, h, :, 0, :]
    for par, parts in enumerate(split_table(s.tab)):
        s.wide[par] = tn(parts, spread(1024, 12, par, 3))
    entry, token, parity = lane_info(1024, 12)
    token, odd = token[:, 0:864], parity[:, 0:864] == 1
    rows, valid = row_flags(s, 6 * lat)
    for lk in range(2):
        strips = []
        for par in range(2):
            strip = jnp.zeros((6, 1024), F32)
            for e in range(12):
                at = 72 * (e // 6) + 36 * lk + 6 * (e % 6)
                strip = jnp.where(entry == e, s.wide[par, at : at + 6, :], strip)
            strips.append(strip)
        for ck in range(12):
            turn = (1024 - (11 - ck) * 12) % 1024
            even_part, odd_part = [
                (pltpu.roll(x, turn, 1) if turn else x)[:, 0:864] for x in strips
            ]
            at = 12 * ck + 6 * lk
            keep = valid | (token == rows + at)
            s.bias1[at : at + 6, :] = jnp.where(
                keep, jnp.where(odd, odd_part, even_part), -1e30
            )


def expand_second(s, lat):
    for par, parts in enumerate(split_table(s.tab2)):
        s.wide[par, 0:128, 0:512] = tn(parts, spread(512, 6, par, 3))
    entry, token, parity = lane_info(512, 6)
    token, odd = token[:, 0:432], parity[:, 0:432] == 1
    rows, valid = row_flags(s, 6 * lat + 3)
    q_band = jnp.where(lat == 7, (entry[:, 0:432] >= 3).astype(jnp.int32), 0)
    k_band = jnp.where(lat == 7, (rows >= 3).astype(jnp.int32), 0)
    same = q_band == k_band
    for lev in range(2):
        strips = []
        for par in range(2):
            strip = jnp.zeros((6, 512), F32)
            for e in range(6):
                at = 36 * (1 - lev) + 6 * e
                strip = jnp.where(entry == e, s.wide[par, at : at + 6, 0:512], strip)
            strips.append(strip)
        for ck in range(12):
            turn = (512 - (11 - ck) * 6) % 512
            even_part, odd_part = [
                (pltpu.roll(x, turn, 1) if turn else x)[:, 0:432] for x in strips
            ]
            at = 6 * ck
            keep = (valid | (token == rows + at)) & same
            s.bias2[lev, at : at + 6, :] = jnp.where(
                keep, jnp.where(odd, odd_part, even_part), -1e30
            )


def fold_first(s):
    entry, _, parity = lane_info(1024, 12)
    for par in range(2):
        mine = parity == par
        for lk in range(2):
            acc = jnp.zeros((6, 1024), F32)
            for ck in range(12):
                at = 12 * ck + 6 * lk
                piece = jnp.where(mine, s.ds[at : at + 6, :], 0.0)
                turn = (11 - ck) * 12
                acc = acc + (pltpu.roll(piece, turn, 1) if turn else piece)
            for e in range(12):
                at = 72 * (e // 6) + 36 * lk + 6 * (e % 6)
                s.wide[par, at : at + 6, :] = jnp.where(entry == e, acc, 0.0)
    return [nt(spread(1024, 12, par, 1), s.wide[par].astype(BF16)) for par in range(2)]


def fold_second(s):
    entry, _, parity = lane_info(512, 6)
    s.wide[:, :, 0:512] = jnp.zeros((2, 144, 512), F32)
    for par in range(2):
        mine = parity == par
        for lev in range(2):
            acc = jnp.zeros((6, 512), F32)
            for ck in range(12):
                at = 72 * lev + 6 * ck
                piece = jnp.where(mine, s.ds[at : at + 6, 0:512], 0.0)
                turn = (11 - ck) * 6
                acc = acc + (pltpu.roll(piece, turn, 1) if turn else piece)
            for e in range(6):
                at = 108 * (1 - lev) + 6 * e
                s.wide[par, at : at + 6, 0:512] = jnp.where(entry == e, acc, 0.0)
    return [nt(spread(512, 6, par, 1), s.wide[par, :, 0:512].astype(BF16)) for par in range(2)]


def attend(s, j, x, gain, wqkv_ref, bias, groups):
    n = 144 // groups
    center = x - jnp.mean(x, -1, keepdims=True)
    inverse = lax.rsqrt(jnp.mean(center * center, -1, keepdims=True) + 1e-05)
    normed = center * inverse
    scaled = (normed * gain).astype(BF16)
    packed = nn(scaled, wqkv_ref[j])
    q, k, v = packed[:, 0:192], packed[:, 192:384], packed[:, 384:576]
    s.normed[j] = normed
    s.inverse[j] = inverse
    s.scaled[j] = scaled
    s.k[j] = k
    s.v[j] = v
    for g in range(groups):
        rows = slice(g * n, g * n + n)
        qm = head_stack(q[rows])
        s.qm[j, g * 6 * n : (g + 1) * 6 * n, :] = qm
        scores = nt(k[rows].astype(BF16), qm) * SCALE + bias(g)
        weight = jnp.exp(scores - jnp.max(scores, 0, keepdims=True))
        probs = weight * (1.0 / jnp.sum(weight, 0, keepdims=True))
        s.probs[j, rows, 0 : 6 * n] = probs


def project(s, j, x, wproj_ref, groups):
    n = 144 // groups
    attended = []
    for g in range(groups):
        rows = slice(g * n, g * n + n)
        v, probs = s.v[j, rows, :], s.probs[j, rows, 0 : 6 * n]
        mixed_t = head_diagonal(tn(v.astype(BF16), probs.astype(BF16)), n)
        s.mixed_t[j, g, :, 0:n] = mixed_t
        attended.append(tn(mixed_t.astype(BF16), wproj_ref[j]))
    att = attended[0] if groups == 1 else jnp.concatenate(attended, 0)
    return (x + att).astype(BF16)


def head_backs(s, j, g_in, wproj_ref, groups):
    n = 144 // groups
    back = nt(g_in, wproj_ref[j])
    for g in range(groups):
        s.backm[j, g * 6 * n : (g + 1) * 6 * n, :] = head_stack(back[g * n : g * n + n])


def backward(s, j, g_in, gain, wqkv_ref, groups):
    n = 144 // groups
    dqs, dks, dvs = [], [], []
    for g in range(groups):
        rows = slice(g * n, g * n + n)
        backm = s.backm[j, g * 6 * n : (g + 1) * 6 * n, :]
        probs = s.probs[j, rows, 0 : 6 * n]
        k = s.k[j, rows, :].astype(BF16)
        v = s.v[j, rows, :].astype(BF16)
        qm = s.qm[j, g * 6 * n : (g + 1) * 6 * n, :]
        d_probs = nt(v, backm)
        dvs.append(nn(probs.astype(BF16), backm))
        d_scores = probs * (d_probs - jnp.sum(d_probs * probs, 0, keepdims=True))
        s.ds[rows, 0 : 6 * n] = d_scores
        d_rounded = (d_scores * SCALE).astype(BF16)
        dks.append(nn(d_rounded, qm))
        dqs.append(head_diagonal(tn(k, d_rounded), n).T)
    if groups == 1:
        dq, dk, dv = dqs[0], dks[0], dvs[0]
    else:
        dq, dk, dv = [jnp.concatenate(p, 0) for p in (dqs, dks, dvs)]
    dq, dk, dv = dq.astype(BF16), dk.astype(BF16), dv.astype(BF16)
    w = wqkv_ref[j]
    d_scaled = nt(dq, w[:, 0:192]) + nt(dk, w[:, 192:384]) + nt(dv, w[:, 384:576])
    normed = s.normed[j]
    d_normed = d_scaled * gain
    d_hidden = s.inverse[j] * (
        d_normed
        - jnp.mean(d_normed, -1, keepdims=True)
        - normed * jnp.mean(d_normed * normed, -1, keepdims=True)
    )
    result = (g_in.astype(F32) + d_hidden).astype(BF16)
    return result, (dq, dk, dv, d_scaled)


def gradients(s, j, g_in, saved, folded, groups):
    n = 144 // groups
    dq, dk, dv, d_scaled = saved
    scaled = s.scaled[j]
    s.grad[:, 0:192] = tn(scaled, dq)
    s.grad[:, 192:384] = tn(scaled, dk)
    s.grad[:, 384:576] = tn(scaled, dv)
    d_proj = jnp.zeros((192, 192), F32)
    for g in range(groups):
        d_proj = d_proj + nn(
            s.mixed_t[j, g, :, 0:n].astype(BF16), g_in[g * n : g * n + n]
        )
    s.grad[:, 576:768] = d_proj
    for h in range(HEADS):
        s.extra[24 * h : 24 * h + 24, 0:144] = folded[h % 2][24 * (h // 2) : 24 * (h // 2) + 24]
    s.extra[144:145, 0:192] = jnp.sum(d_scaled * s.normed[j], 0, keepdims=True)
    for half in range(2):
        for slot in range(12):
            column, row = half * 384 + (slot // 4) * 128, (slot % 4) * 48
            s.payload[j, half, slot] = s.grad[row : row + 48, column : column + 128].astype(BF16)
        for slot, row in ((12, 144), (13, 0), (14, 48), (15, 96)):
            s.payload[j, half, slot] = s.extra[
                row : row + 48, 128 * half : 128 * half + 128
            ].astype(BF16)


class Halo:
    def __init__(self, s, which, forward_shift):
        lat, lon = lax.axis_index("lat"), lax.axis_index("lon")
        home_lat, home_lon = home()
        nlat, nlon = lax.axis_size("lat"), lax.axis_size("lon")
        self.s, self.which = s, which
        self.copies, self.partners = [], []
        for quarter in range(4):
            down, right = quarter // 2, quarter % 2
            if forward_shift:
                peer = runs_at(
                    lax.rem(lat + down - 1 + nlat, nlat), lax.rem(lon + right - 1 + nlon, nlon)
                )
            else:
                peer = lax.rem(home_lat + down, nlat), lax.rem(home_lon + right, nlon)
            self.partners.append(peer)
            self.copies.append(
                pltpu.make_async_remote_copy(
                    src_ref=s.halo_out.at[which, quarter],
                    dst_ref=s.halo_in.at[which, 3 - quarter],
                    send_sem=s.halo_send.at[which, quarter],
                    recv_sem=s.halo_recv.at[which, quarter],
                    device_id=peer,
                    device_id_type=MESH,
                )
            )

    def start(self, quarters):
        self.s.halo_out[self.which] = quarters.reshape(4, 64, 128)
        for copy in self.copies:
            copy.start()

    def finish(self):
        for copy in self.copies:
            copy.wait()
        return self.s.halo_in[self.which].reshape(256, 128)


class TableShare:
    def __init__(self, s):
        lat, lon, y, zh, zl, x, core = place()
        self.s, self.core = s, core
        self.leaves, self.arrives = zl >= 4, zl < 4
        heads, others = pl.ds(3 * core, 3), pl.ds(3 - 3 * core, 3)
        self.far = self.copy(s.tab2_own.at[heads], s.tab2.at[heads], far_peers()[0], 0)
        self.pair = self.copy(s.tab2.at[heads], s.tab2.at[heads], sibling(), 1)

    def copy(self, src, dst, peer, number):
        return pltpu.make_async_remote_copy(
            src_ref=src,
            dst_ref=dst,
            send_sem=self.s.tab_send.at[number],
            recv_sem=self.s.tab_recv.at[number],
            device_id=peer,
            device_id_type=MESH,
        )

    def start(self):
        @pl.when(self.leaves)
        def _():
            self.far.start()

    def forward(self):
        @pl.when(self.arrives)
        def _():
            self.far.wait_recv()
            self.pair.start()

    def finish(self):
        @pl.when(self.leaves)
        def _():
            self.far.wait_send()
            self.s.tab2[...] = self.s.tab2_own[...]

        @pl.when(self.arrives)
        def _():
            self.pair.wait()


def place():
    lat, lon = lax.axis_index("lat"), lax.axis_index("lon")
    line = lax.rem(lon, 8)
    return lat, lon, lat // 2, lax.rem(lat, 2), lon // 8, line // 2, lax.rem(line, 2)


def runs_at(lat, lon):
    z = lax.rem(lax.rem(lat, 2) * 8 + lon // 8 + 4, 16)
    return (lat // 2) * 2 + z // 8, lax.rem(z, 8) * 8 + lax.rem(lon, 8)


def home():
    lat, lon, y, zh, zl, x, core = place()
    z = lax.rem(zh * 8 + zl + 12, 16)
    return y * 2 + z // 8, lax.rem(z, 8) * 8 + lax.rem(lon, 8)


def sibling():
    lat, lon, y, zh, zl, x, core = place()
    return lat, zl * 8 + x * 2 + 1 - core


def plane_peers():
    lat, lon, y, zh, zl, x, core = place()
    out = []
    for dy in range(4):
        for dx in range(4):
            if dx or dy:
                py, px = lax.rem(y + dy, 4), lax.rem(x + dx, 4)
                out.append((dx if dy == 0 else 0, (py * 2 + zh, zl * 8 + px * 2 + core), py * 4 + px))
    return out


def near_peers():
    lat, lon, y, zh, zl, x, core = place()
    quad = (zl // 4) * 4
    return [(lat, (quad + lax.rem(zl + d, 4)) * 8 + x * 2 + core) for d in range(1, 4)]


def far_peers():
    lat, lon, y, zh, zl, x, core = place()
    out = []
    for d in range(1, 4):
        z = lax.rem(zh * 8 + zl + 4 * d, 16)
        out.append((y * 2 + z // 8, lax.rem(z, 8) * 8 + x * 2 + core))
    return out


def half_peer():
    lat, lon, y, zh, zl, x, core = place()
    return lat, lax.rem(zl + 4, 8) * 8 + x * 2 + core


class Reduce:
    def __init__(self, s, j):
        lat, lon, y, zh, zl, x, core = place()
        self.s, self.j, self.core, self.x = s, j, core, x
        self.own = y * 4 + x
        self.near, self.far, self.half = lax.rem(zl, 4), zh * 2 + zl // 4, zl // 4
        self.used = 0
        own, table = self.own, 16 + x
        near, far, half = self.near, self.far, self.half
        stages = [[self.copy(s.payload.at[j, 1 - core], s.in_core.at[j], sibling())], [], [], [], []]
        for i, (dx, peer, slot) in enumerate(plane_peers()):
            stages[1].append(self.copy(s.half.at[j, slot], s.in_plane.at[j, i], peer))
            stages[4].append(self.copy(s.red.at[j, core, own], s.red.at[j, core, own], peer))
            if dx:
                px = lax.rem(x + dx, 4)
                stages[1].append(self.copy(s.half.at[j, 13 + px], s.in_plane.at[j, 14 + dx], peer))
                stages[4].append(
                    self.copy(s.red.at[j, core, table], s.red.at[j, core, table], peer)
                )
        for peer in near_peers():
            stages[2].append(self.copy(s.near.at[j, near], s.near.at[j, near], peer))
        for peer in far_peers():
            stages[3].append(self.copy(s.far.at[j, far], s.far.at[j, far], peer))
        if j == 0:
            stages[3].append(self.copy(s.far_tab.at[0, half], s.far_tab.at[0, half], half_peer()))
        else:
            for steps in (1, 2):
                stages[3].append(
                    self.copy(s.far_tab.at[1, 0], s.far_tab.at[1, steps], far_peers()[3 - steps])
                )
        stages.append([self.copy(s.red.at[j, core], s.red.at[j, core], sibling())])
        self.stages = stages

    def copy(self, src, dst, peer):
        number, self.used = self.used, self.used + 1
        return pltpu.make_async_remote_copy(
            src_ref=src,
            dst_ref=dst,
            send_sem=self.s.ar_send.at[self.j, number],
            recv_sem=self.s.ar_recv.at[self.j, number],
            device_id=peer,
            device_id_type=MESH,
        )

    def step(self, number):
        s, j, core = self.s, self.j, self.core
        if number > 0:
            for copy in self.stages[number - 1]:
                copy.wait()
        if number == 1:
            for slot in range(16):
                total = s.payload[j, core, slot].astype(F32) + s.in_core[j, slot].astype(F32)
                s.half[j, slot] = total.astype(BF16)
        if number == 2:
            total = s.half[j, self.own].astype(F32)
            for i in range(15):
                total = total + s.in_plane[j, i].astype(F32)
            table = s.half[j, 13 + self.x].astype(F32)
            for i in range(15, 18):
                table = table + s.in_plane[j, i].astype(F32)
            s.near[j, self.near, 0:48] = total.astype(BF16)
            s.near[j, self.near, 48:96] = table.astype(BF16)
        if number == 3:
            total = s.near[j, 0].astype(F32)
            for i in range(1, 4):
                total = total + s.near[j, i].astype(F32)
            s.far[j, self.far] = total[0:48].astype(BF16)
            s.far_tab[j, self.half if j == 0 else 0] = total[48:96].astype(BF16)
        if number == 4:
            total = s.far[j, 0].astype(F32)
            for i in range(1, 4):
                total = total + s.far[j, i].astype(F32)
            s.red[j, core, self.own] = total.astype(BF16)
            if j == 0:
                table = s.far_tab[0, 0].astype(F32) + s.far_tab[0, 1].astype(F32)
            else:
                own, one, two = [s.far_tab[1, i].astype(F32) for i in range(3)]
                table = jnp.where(self.half == 1, own + one, one + two)
            s.red[j, core, 16 + self.x] = table.astype(BF16)
        if number < 6:
            for copy in self.stages[number]:
                copy.start()


def signal_partners(halos):
    barrier = pltpu.get_barrier_semaphore()
    partners = halos[0].partners + halos[-1].partners
    partners += far_peers() + near_peers() + [p for _, p, _ in plane_peers()]
    partners += [sibling(), half_peer()]
    for partner in partners:
        pl.semaphore_signal(barrier, inc=1, device_id=partner, device_id_type=MESH)
    return barrier, len(partners)


SCRATCH = dict(
    x_in=pltpu.VMEM((6, 12, 2, 192), BF16),
    cot_in=pltpu.VMEM((6, 12, 2, 192), BF16),
    gains=pltpu.VMEM((2, 192), F32),
    wqkv=pltpu.VMEM((2, 192, 576), BF16),
    wproj=pltpu.VMEM((2, 192, 192), BF16),
    tab_in=pltpu.VMEM((2, 6, 23, 1, 144), F32),
    pad=pltpu.SMEM((48,), jnp.int32),
    loads=pltpu.SemaphoreType.DMA((7,)),
    out=pltpu.VMEM((6, 12, 2, 192), BF16),
    dx=pltpu.VMEM((6, 12, 2, 192), BF16),
    stores=pltpu.SemaphoreType.DMA((4,)),
    tab=pltpu.VMEM((6, 24, 144), F32),
    tab2_own=pltpu.VMEM((6, 24, 128), F32),
    tab2=pltpu.VMEM((6, 24, 128), F32),
    wide=pltpu.VMEM((2, 144, 1024), F32),
    bias1=pltpu.VMEM((144, 864), F32),
    bias2=pltpu.VMEM((2, 72, 432), F32),
    ds=pltpu.VMEM((144, 1024), F32),
    normed=pltpu.VMEM((2, 144, 192), F32),
    inverse=pltpu.VMEM((2, 144, 1), F32),
    scaled=pltpu.VMEM((2, 144, 192), BF16),
    k=pltpu.VMEM((2, 144, 192), F32),
    v=pltpu.VMEM((2, 144, 192), F32),
    qm=pltpu.VMEM((2, 864, 192), BF16),
    backm=pltpu.VMEM((2, 864, 192), BF16),
    probs=pltpu.VMEM((2, 144, 864), F32),
    mixed_t=pltpu.VMEM((2, 2, 192, 144), F32),
    grad=pltpu.VMEM((192, 768), F32),
    extra=pltpu.VMEM((192, 256), F32),
    halo_out=pltpu.VMEM((4, 4, 64, 128), BF16),
    halo_in=pltpu.VMEM((4, 4, 64, 128), BF16),
    payload=pltpu.VMEM((2, 2, 16, 48, 128), BF16),
    in_core=pltpu.VMEM((2, 16, 48, 128), BF16),
    half=pltpu.VMEM((2, 17, 48, 128), BF16),
    in_plane=pltpu.VMEM((2, 18, 48, 128), BF16),
    near=pltpu.VMEM((2, 4, 96, 128), BF16),
    far=pltpu.VMEM((2, 4, 48, 128), BF16),
    far_tab=pltpu.VMEM((2, 3, 48, 128), BF16),
    red=pltpu.VMEM((2, 2, 20, 48, 128), BF16),
    halo_send=pltpu.SemaphoreType.DMA((4, 4)),
    halo_recv=pltpu.SemaphoreType.DMA((4, 4)),
    tab_send=pltpu.SemaphoreType.DMA((2,)),
    tab_recv=pltpu.SemaphoreType.DMA((2,)),
    ar_send=pltpu.SemaphoreType.DMA((2, 48)),
    ar_recv=pltpu.SemaphoreType.DMA((2, 48)),
)


class Names:
    pass


def main_kernel(
    x_ref, cot_ref, gains_ref, wqkv_ref, wproj_ref, tab_ref, pad_ref,
    out_ref, dx_ref, red_ref, *scratch,
):
    s = Names()
    for name, ref in zip(SCRATCH, scratch):
        setattr(s, name, ref)
    lat = lax.axis_index("lat")
    sources = dict(
        x_in=x_ref, tab_in=tab_ref, pad=pad_ref, gains=gains_ref, wqkv=wqkv_ref,
        wproj=wproj_ref, cot_in=cot_ref,
    )
    loads = {
        name: pltpu.make_async_copy(ref, getattr(s, name), s.loads.at[i])
        for i, (name, ref) in enumerate(sources.items())
    }
    for load in loads.values():
        load.start()
    h_first, h_cot, h_out, h_grad = halos = [Halo(s, i, i < 2) for i in range(4)]
    barrier, expected = signal_partners(halos)

    s.tab[...] = jnp.zeros((6, 24, 144), F32)
    s.tab2_own[...] = jnp.zeros((6, 24, 128), F32)
    s.ds[:, 768:1024] = jnp.zeros((144, 256), F32)
    s.extra[...] = jnp.zeros((192, 256), F32)
    s.half[:, 16] = jnp.zeros((2, 48, 128), BF16)
    s.red[:, :, 19] = jnp.zeros((2, 2, 48, 128), BF16)

    def field(ref):
        return ref[...].astype(F32).reshape(144, 192).astype(BF16)

    def store(number, value, ref):
        copy = pltpu.make_async_copy(value, ref, s.stores.at[number])
        copy.start()
        return copy

    for name in ("tab_in", "pad"):
        loads[name].wait()
    for h in range(HEADS):
        for lev in range(2):
            s.tab2_own[h, 0:23, 36 * lev : 36 * lev + 36] = s.tab_in[
                1, h, :, 0, 108 * lev : 108 * lev + 36
            ]
    expand_first(s, lat)
    for name in ("x_in", "gains", "wqkv", "wproj", "cot_in"):
        loads[name].wait()
    gain1, gain2 = s.gains[0:1, :], s.gains[1:2, :]
    share = TableShare(s)
    reduce2, reduce1 = Reduce(s, 1), Reduce(s, 0)
    cot = pack(field(s.cot_in), "n")
    x1 = nn(reorder("a", "n"), field(s.x_in))
    pl.semaphore_wait(barrier, expected)
    share.start()
    h_cot.start(cot)

    attend(s, 0, x1, gain1, s.wqkv, lambda g: s.bias1[...], 1)
    first = project(s, 0, x1, s.wproj, 1)
    h_first.start(pack(first, "a"))
    share.forward()
    g2 = unpack(h_cot.finish(), "b").astype(BF16)
    head_backs(s, 1, g2, s.wproj, 2)
    share.finish()
    expand_second(s, home()[0])
    x2 = unpack(h_first.finish(), "b")
    attend(s, 1, x2, gain2, s.wqkv, lambda g: s.bias2[g], 2)
    dh2, saved2 = backward(s, 1, g2, gain2, s.wqkv, 2)
    h_grad.start(pack(dh2, "b"))
    h_out.start(pack(project(s, 1, x2, s.wproj, 2), "b"))
    gradients(s, 1, g2, saved2, fold_second(s), 2)
    reduce2.step(0)
    reduce2.step(1)
    g1 = unpack(h_grad.finish(), "a").astype(BF16)
    head_backs(s, 0, g1, s.wproj, 1)
    dx, saved1 = backward(s, 0, g1, gain1, s.wqkv, 1)
    reduce2.step(2)
    gradients(s, 0, g1, saved1, fold_first(s), 1)
    reduce1.step(0)
    s.dx[...] = nn(reorder("n", "a"), dx).reshape(6, 12, 2, 192).astype(BF16)
    stores = [store(0, s.dx, dx_ref)]
    reduce1.step(1)
    s.out[...] = unpack(h_out.finish(), "n").reshape(6, 12, 2, 192).astype(BF16)
    stores.append(store(1, s.out, out_ref))
    reduce2.step(3)
    reduce1.step(2)
    reduce2.step(4)
    reduce1.step(3)
    reduce2.step(5)
    reduce1.step(4)
    reduce2.step(6)
    stores.append(store(2, s.red.at[1], red_ref.at[1]))
    reduce1.step(5)
    reduce1.step(6)
    stores.append(store(3, s.red.at[0], red_ref.at[0]))
    for copy in stores:
        copy.wait()


def finish_kernel(
    red_ref, o_ref, d_ref, out_ref, dx_ref, gains_ref, dqkv_ref, dproj_ref, dtab_ref, red, sems
):
    copies = [
        pltpu.make_async_copy(source, target, sems.at[i])
        for i, (source, target) in enumerate(
            ((red_ref.at[1], red.at[1]), (red_ref.at[0], red.at[0]), (o_ref, out_ref), (d_ref, dx_ref))
        )
    ]
    for copy in copies:
        copy.start()
    for j in (1, 0):
        copies[1 - j].wait()
        for half in range(2):
            for slot in range(12):
                column, row = half * 3 + slot // 4, (slot % 4) * 48
                rows = slice(row, row + 48)
                value = red[j, half, slot].astype(F32)
                if column < 4:
                    dqkv_ref[j, rows, 128 * column : 128 * column + 128] = value
                elif column == 4:
                    dqkv_ref[j, rows, 512:576] = value[:, 0:64]
                    dproj_ref[j, rows, 0:64] = value[:, 64:128]
                else:
                    dproj_ref[j, rows, 64:192] = value
            width = 128 if half == 0 else 16
            lanes = slice(128 * half, 128 * half + width)
            for third in range(3):
                value = red[j, half, 16 + third].astype(F32)
                for i in range(2):
                    dtab_ref[j, 2 * third + i, :, 0, lanes] = value[24 * i : 24 * i + 23, 0:width]
        gains_ref[j : j + 1, 0:128] = red[j, 0, 12].astype(F32)[0:1]
        gains_ref[j : j + 1, 128:192] = red[j, 1, 12].astype(F32)[0:1, 0:64]
    for copy in copies[2:]:
        copy.wait()


def body(inputs, cotangent, gains, qkv_weights, proj_weights, bias_tables, pad_rows):
    vmem = pl.BlockSpec(memory_space=pltpu.VMEM)
    hbm = pl.BlockSpec(memory_space=pltpu.HBM)
    field = jax.ShapeDtypeStruct((6, 12, 2, 192), BF16)
    out, dx, red = pl.pallas_call(
        main_kernel,
        out_shape=(field, field, jax.ShapeDtypeStruct((2, 2, 20, 48, 128), BF16)),
        in_specs=[hbm] * 7,
        out_specs=(hbm,) * 3,
        scratch_shapes=list(SCRATCH.values()),
        compiler_params=pltpu.CompilerParams(
            collective_id=0, has_side_effects=True, vmem_limit_bytes=VMEM_LIMIT
        ),
        name="both_blocks",
    )(
        inputs.transpose(1, 2, 0, 3),
        cotangent.transpose(1, 2, 0, 3),
        gains,
        qkv_weights,
        proj_weights,
        bias_tables.transpose(0, 2, 3, 1, 4),
        pad_rows,
    )
    out, dx, d_gains, d_qkv, d_proj, d_tables = pl.pallas_call(
        finish_kernel,
        out_shape=(
            field,
            field,
            jax.ShapeDtypeStruct((2, 192), F32),
            jax.ShapeDtypeStruct((2, 192, 576), F32),
            jax.ShapeDtypeStruct((2, 192, 192), F32),
            jax.ShapeDtypeStruct((2, 6, 23, 1, 144), F32),
        ),
        in_specs=[hbm] * 3,
        out_specs=(vmem,) * 6,
        scratch_shapes=[
            pltpu.VMEM((2, 2, 20, 48, 128), BF16),
            pltpu.SemaphoreType.DMA((4,)),
        ],
        compiler_params=pltpu.CompilerParams(vmem_limit_bytes=VMEM_LIMIT),
        name="unpack",
    )(red, out, dx)
    return (
        out.transpose(2, 0, 1, 3),
        dx.transpose(2, 0, 1, 3),
        d_gains,
        d_qkv,
        d_proj,
        d_tables.transpose(0, 3, 1, 2, 4),
    )


def solution(mesh):
    field = P(None, "lat", "lon", None)
    tables = P(None, "lat", None, None, None)
    return jax.shard_map(
        body,
        mesh=mesh,
        in_specs=(field, field, P(), P(), P(), tables, P()),
        out_specs=(field, field, P(), P(), P(), tables),
        check_vma=False,
    )
```

```python
import jax
import jax.numpy as jnp
from jax import lax
from jax.experimental import pallas as pl
from jax.experimental.pallas import tpu as pltpu
from jax.sharding import PartitionSpec as P

F32 = jnp.float32
BF16 = jnp.bfloat16
MESH = pl.DeviceIdType.MESH
HEADS = 6
VMEM_LIMIT = 62 * 2**20
SCALE = 32 ** (-0.5)


def div(x, d):
    return (x * (-(-(2**20) // d))) >> 20


def tokens_of(order, n):
    i = lax.broadcasted_iota(jnp.int32, (n, 1), 0)
    used = i < n
    if order == "n":
        r = div(i, 24)
        c = div(i - 24 * r, 2)
        l = i - 24 * r - 2 * c
    elif order == "a":
        c = div(i, 12)
        l = div(i - 12 * c, 6)
        r = i - 12 * c - 6 * l
    elif order == "b":
        l = div(i, 72)
        c = div(i - 72 * l, 6)
        r = i - 72 * l - 6 * c
    else:
        q = i >> 6
        inner = i - 64 * q
        used = inner < 36
        if order == "s1":
            inner, used = inner - 36, (inner >= 36) & (inner < 54)
        if order == "s2":
            inner, used = inner - 18, (inner >= 36) & (inner < 54)
        l = div(inner, 18)
        r = div(inner - 18 * l, 6)
        c = inner - 18 * l - 6 * r
        r, c = r + 3 * (q >> 1), c + 6 * (q & 1)
    return l, r, c, used


def place_in(order, l, r, c):
    if order == "n":
        return 24 * r + 2 * c + l
    if order == "a":
        return 12 * c + 6 * l + r
    if order == "b":
        return 72 * l + 6 * c + r
    lower, right = (r >= 3).astype(jnp.int32), (c >= 6).astype(jnp.int32)
    quarter = 64 * (2 * lower + right)
    inner = 18 * l + 6 * (r - 3 * lower) + c - 6 * right
    if order == "s":
        return quarter + inner
    if order == "s1":
        return jnp.where(inner < 18, quarter + 36 + inner, -1)
    return jnp.where(inner >= 18, quarter + 18 + inner, -1)


def reorder(to, of):
    n, m = [256 if order[0] == "s" else 144 for order in (to, of)]
    l, r, c, used = tokens_of(to, n)
    place = jnp.where(used, place_in(of, l, r, c), -1)
    return jnp.where(place == lax.broadcasted_iota(jnp.int32, (n, m), 1), 1.0, 0.0).astype(BF16)


def pack(x, order):
    wide, rest = x[:, 0:128], x[:, 128:192]
    pairs = [nn(reorder(to, order), rest) for to in ("s1", "s2")]
    return (nn(reorder("s", order), wide) + jnp.concatenate(pairs, 1)).astype(BF16)


def unpack(x, order):
    left, right = nn(reorder(order, "s1"), x), nn(reorder(order, "s2"), x)
    rest = left[:, 0:64] + right[:, 64:128]
    return jnp.concatenate([nn(reorder(order, "s"), x), rest], 1)


def spread(lanes, step, par, parts):
    i = lax.broadcasted_iota(jnp.int32, (72 * parts, 1), 0)
    part = div(i, 72)
    h = div(i - 72 * part, 24)
    o = i - 72 * part - 24 * h
    start = 12 * step * par + 24 * step * h + (22 - o) * step
    at = lax.broadcasted_iota(jnp.int32, (72 * parts, lanes), 1) - start
    return jnp.where((at >= 0) & (at < step), 1.0, 0.0).astype(BF16)


def lane_info(lanes, step):
    lane = lax.broadcasted_iota(jnp.int32, (1, lanes), 1)
    head = div(lane, 12 * step)
    parity = jnp.where(head < HEADS, head & 1, 2)
    return lane - step * div(lane, step), lane - 12 * step * head, parity


def nn(a, b):
    return lax.dot_general(a, b, (((1,), (0,)), ((), ())), preferred_element_type=F32)


def nt(a, b):
    return lax.dot_general(a, b, (((1,), (1,)), ((), ())), preferred_element_type=F32)


def tn(a, b):
    return lax.dot_general(a, b, (((0,), (0,)), ((), ())), preferred_element_type=F32)


def head_stack(x):
    lane = lax.broadcasted_iota(jnp.int32, (1, 192), 1)
    parts = [jnp.where((lane >= 32 * h) & (lane < 32 * h + 32), x, 0.0) for h in range(HEADS)]
    return jnp.concatenate(parts, 0).astype(BF16)


def head_diagonal(x, n):
    return jnp.concatenate(
        [x[32 * h : 32 * h + 32, n * h : n * h + n] for h in range(HEADS)], 0
    )


def split_table(s, block):
    out = []
    for h in range(HEADS):
        s.tab[h, 0:23, :] = s.tab_in[block, h, :, 0, :]
    for par in range(2):
        parts = [[], [], []]
        for h in range(3):
            t = s.tab[2 * h + par]
            hi = t.astype(BF16).astype(F32)
            rest = t - hi
            mid = rest.astype(BF16).astype(F32)
            for part, value in zip(parts, (hi, mid, rest - mid)):
                part.append(value)
        out.append(jnp.concatenate(sum(parts, []), 0).astype(BF16))
    return out


def row_flags(s, start):
    rows = lax.broadcasted_iota(jnp.int32, (6, 1), 0)
    flags = jnp.zeros((6, 1), jnp.int32)
    for r in range(6):
        flags = jnp.where(rows == r, s.pad[lax.rem(start + r, 48)], flags)
    return rows, flags == 1


def expand_first(s, lat):
    for par, parts in enumerate(split_table(s, 0)):
        s.wide[par] = tn(parts, spread(1024, 12, par, 3))
    entry, token, parity = lane_info(1024, 12)
    token, odd = token[:, 0:864], parity[:, 0:864] == 1
    rows, valid = row_flags(s, 6 * lat)
    for lk in range(2):
        strips = []
        for par in range(2):
            strip = jnp.zeros((6, 1024), F32)
            for e in range(12):
                at = 72 * (e // 6) + 36 * lk + 6 * (e % 6)
                strip = jnp.where(entry == e, s.wide[par, at : at + 6, :], strip)
            strips.append(strip)
        for ck in range(12):
            turn = (1024 - (11 - ck) * 12) % 1024
            even_part, odd_part = [
                (pltpu.roll(x, turn, 1) if turn else x)[:, 0:864] for x in strips
            ]
            at = 12 * ck + 6 * lk
            keep = valid | (token == rows + at)
            s.bias1[at : at + 6, :] = jnp.where(
                keep, jnp.where(odd, odd_part, even_part), -1e30
            )


def expand_second(s, lat):
    for par, parts in enumerate(split_table(s, 1)):
        s.wide[par, :, 0:512] = tn(parts, spread(512, 6, par, 3))
    entry, token, parity = lane_info(512, 6)
    token, odd = token[:, 0:432], parity[:, 0:432] == 1
    rows, valid = row_flags(s, 6 * lat + 3)
    q_band = jnp.where(lat == 7, (entry[:, 0:432] >= 3).astype(jnp.int32), 0)
    k_band = jnp.where(lat == 7, (rows >= 3).astype(jnp.int32), 0)
    same = q_band == k_band
    for lev in range(2):
        strips = []
        for par in range(2):
            strip = jnp.zeros((6, 512), F32)
            for e in range(6):
                at = 108 * (1 - lev) + 6 * e
                strip = jnp.where(entry == e, s.wide[par, at : at + 6, 0:512], strip)
            strips.append(strip)
        for ck in range(12):
            turn = (512 - (11 - ck) * 6) % 512
            even_part, odd_part = [
                (pltpu.roll(x, turn, 1) if turn else x)[:, 0:432] for x in strips
            ]
            at = 6 * ck
            keep = (valid | (token == rows + at)) & same
            s.bias2[lev, at : at + 6, :] = jnp.where(
                keep, jnp.where(odd, odd_part, even_part), -1e30
            )


def fold_first(s):
    entry, _, parity = lane_info(1024, 12)
    for par in range(2):
        mine = parity == par
        for lk in range(2):
            acc = jnp.zeros((6, 1024), F32)
            for ck in range(12):
                at = 12 * ck + 6 * lk
                piece = jnp.where(mine, s.ds[at : at + 6, :], 0.0)
                turn = (11 - ck) * 12
                acc = acc + (pltpu.roll(piece, turn, 1) if turn else piece)
            for e in range(12):
                at = 72 * (e // 6) + 36 * lk + 6 * (e % 6)
                s.wide[par, at : at + 6, :] = jnp.where(entry == e, acc, 0.0)
    return [nt(spread(1024, 12, par, 1), s.wide[par].astype(BF16)) for par in range(2)]


def fold_second(s):
    entry, _, parity = lane_info(512, 6)
    s.wide[:, :, 0:512] = jnp.zeros((2, 144, 512), F32)
    for par in range(2):
        mine = parity == par
        for lev in range(2):
            acc = jnp.zeros((6, 512), F32)
            for ck in range(12):
                at = 72 * lev + 6 * ck
                piece = jnp.where(mine, s.ds[at : at + 6, 0:512], 0.0)
                turn = (11 - ck) * 6
                acc = acc + (pltpu.roll(piece, turn, 1) if turn else piece)
            for e in range(6):
                at = 108 * (1 - lev) + 6 * e
                s.wide[par, at : at + 6, 0:512] = jnp.where(entry == e, acc, 0.0)
    return [nt(spread(512, 6, par, 1), s.wide[par, :, 0:512].astype(BF16)) for par in range(2)]


def attend(s, j, x, gain, wqkv_ref, bias, groups):
    n = 144 // groups
    center = x - jnp.mean(x, -1, keepdims=True)
    inverse = lax.rsqrt(jnp.mean(center * center, -1, keepdims=True) + 1e-05)
    normed = center * inverse
    scaled = (normed * gain).astype(BF16)
    packed = nn(scaled, wqkv_ref[j])
    q, k, v = packed[:, 0:192], packed[:, 192:384], packed[:, 384:576]
    s.normed[j] = normed
    s.inverse[j] = inverse
    s.scaled[j] = scaled
    s.k[j] = k
    s.v[j] = v
    for g in range(groups):
        rows = slice(g * n, g * n + n)
        qm = head_stack(q[rows])
        s.qm[j, g * 6 * n : (g + 1) * 6 * n, :] = qm
        scores = nt(k[rows].astype(BF16), qm) * SCALE + bias(g)
        weight = jnp.exp(scores - jnp.max(scores, 0, keepdims=True))
        probs = weight * (1.0 / jnp.sum(weight, 0, keepdims=True))
        s.probs[j, rows, 0 : 6 * n] = probs


def project(s, j, x, wproj_ref, groups):
    n = 144 // groups
    attended = []
    for g in range(groups):
        rows = slice(g * n, g * n + n)
        v, probs = s.v[j, rows, :], s.probs[j, rows, 0 : 6 * n]
        mixed_t = head_diagonal(tn(v.astype(BF16), probs.astype(BF16)), n)
        s.mixed_t[j, g, :, 0:n] = mixed_t
        attended.append(tn(mixed_t.astype(BF16), wproj_ref[j]))
    att = attended[0] if groups == 1 else jnp.concatenate(attended, 0)
    return (x + att).astype(BF16)


def head_backs(s, j, g_in, wproj_ref, groups):
    n = 144 // groups
    back = nt(g_in, wproj_ref[j])
    for g in range(groups):
        s.backm[j, g * 6 * n : (g + 1) * 6 * n, :] = head_stack(back[g * n : g * n + n])


def backward(s, j, groups):
    n = 144 // groups
    dqs, dks, dvs = [], [], []
    for g in range(groups):
        rows = slice(g * n, g * n + n)
        backm = s.backm[j, g * 6 * n : (g + 1) * 6 * n, :]
        probs = s.probs[j, rows, 0 : 6 * n]
        k = s.k[j, rows, :].astype(BF16)
        v = s.v[j, rows, :].astype(BF16)
        qm = s.qm[j, g * 6 * n : (g + 1) * 6 * n, :]
        d_probs = nt(v, backm)
        dvs.append(nn(probs.astype(BF16), backm))
        d_scores = probs * (d_probs - jnp.sum(d_probs * probs, 0, keepdims=True))
        s.ds[rows, 0 : 6 * n] = d_scores
        d_rounded = (d_scores * SCALE).astype(BF16)
        dks.append(nn(d_rounded, qm))
        dqs.append(head_diagonal(tn(k, d_rounded), n).T)
    if groups == 1:
        dq, dk, dv = dqs[0], dks[0], dvs[0]
    else:
        dq, dk, dv = [jnp.concatenate(p, 0) for p in (dqs, dks, dvs)]
    return dq.astype(BF16), dk.astype(BF16), dv.astype(BF16)


def norm_backward(s, j, g_in, d_packed, gain, wqkv_ref):
    w = wqkv_ref[j]
    d_scaled = sum(nt(d_packed[i], w[:, 192 * i : 192 * i + 192]) for i in range(3))
    normed = s.normed[j]
    d_normed = d_scaled * gain
    d_hidden = s.inverse[j] * (
        d_normed
        - jnp.mean(d_normed, -1, keepdims=True)
        - normed * jnp.mean(d_normed * normed, -1, keepdims=True)
    )
    return (g_in.astype(F32) + d_hidden).astype(BF16), d_scaled


def weight_gradients(s, j, g_in, d_packed, groups):
    n = 144 // groups
    scaled = s.scaled[j]
    for i, part in enumerate(d_packed):
        s.grad[:, 192 * i : 192 * i + 192] = tn(scaled, part)
    d_proj = jnp.zeros((192, 192), F32)
    for g in range(groups):
        d_proj = d_proj + nn(
            s.mixed_t[j, g, :, 0:n].astype(BF16), g_in[g * n : g * n + n]
        )
    s.grad[:, 576:768] = d_proj
    for half in range(2):
        for slot in range(12):
            column, row = half * 384 + (slot // 4) * 128, (slot % 4) * 48
            s.payload[j, half, slot] = s.grad[row : row + 48, column : column + 128].astype(BF16)


def other_gradients(s, j, d_scaled, folded):
    for h in range(HEADS):
        s.extra[24 * h : 24 * h + 24, 0:144] = folded[h % 2][24 * (h // 2) : 24 * (h // 2) + 24]
    s.extra[144:145, 0:192] = jnp.sum(d_scaled * s.normed[j], 0, keepdims=True)
    for half in range(2):
        for slot, row in ((12, 144), (13, 0), (14, 48), (15, 96)):
            s.payload[j, half, slot] = s.extra[
                row : row + 48, 128 * half : 128 * half + 128
            ].astype(BF16)


class Halo:
    def __init__(self, s, which, forward_shift):
        lat, lon = lax.axis_index("lat"), lax.axis_index("lon")
        home_lat, home_lon = runs_at(lat, lon)
        nlat, nlon = lax.axis_size("lat"), lax.axis_size("lon")
        self.s, self.which = s, which
        self.copies, self.partners = [], []
        for quarter in range(4):
            down, right = quarter // 2, quarter % 2
            if forward_shift:
                peer = runs_at(
                    lax.rem(lat + down - 1 + nlat, nlat), lax.rem(lon + right - 1 + nlon, nlon)
                )
            else:
                peer = lax.rem(home_lat + down, nlat), lax.rem(home_lon + right, nlon)
            self.partners.append(peer)
            self.copies.append(
                pltpu.make_async_remote_copy(
                    src_ref=s.halo_out.at[which, quarter],
                    dst_ref=s.halo_in.at[which, 3 - quarter],
                    send_sem=s.halo_send.at[which, quarter],
                    recv_sem=s.halo_recv.at[which, quarter],
                    device_id=peer,
                    device_id_type=MESH,
                )
            )

    def start(self, quarters):
        self.s.halo_out[self.which] = quarters.reshape(4, 64, 128)
        for copy in self.copies:
            copy.start()

    def finish(self):
        for copy in self.copies:
            copy.wait_recv()
        return self.s.halo_in[self.which].reshape(256, 128)

    def sent(self):
        for copy in self.copies:
            copy.wait_send()


def place():
    lat, lon = lax.axis_index("lat"), lax.axis_index("lon")
    line = lax.rem(lon, 8)
    return lat, lon, lat // 2, lax.rem(lat, 2), lon // 8, line // 2, lax.rem(line, 2)


def runs_at(lat, lon):
    return lat, lax.rem(lon + 32, 64)


def sibling():
    lat, lon, y, zh, zl, x, core = place()
    return lat, zl * 8 + x * 2 + 1 - core


def plane_peers():
    lat, lon, y, zh, zl, x, core = place()
    hops = lambda step: min(step, 4 - step)
    steps = [(dx, dy) for dy in range(4) for dx in range(4) if dx or dy]
    out = []
    for dx, dy in sorted(steps, key=lambda step: -hops(step[0]) - hops(step[1])):
        py, px = lax.rem(y + dy, 4), lax.rem(x + dx, 4)
        out.append((dx if dy == 0 else 0, (py * 2 + zh, zl * 8 + px * 2 + core), py * 4 + px))
    return out


def near_peers():
    lat, lon, y, zh, zl, x, core = place()
    quad = (zl // 4) * 4
    return [(lat, (quad + lax.rem(zl + d, 4)) * 8 + x * 2 + core) for d in range(1, 4)]


def far_peers():
    lat, lon, y, zh, zl, x, core = place()
    out = []
    for d in range(1, 4):
        z = lax.rem(zh * 8 + zl + 4 * d, 16)
        out.append((y * 2 + z // 8, lax.rem(z, 8) * 8 + x * 2 + core))
    return out


def half_peer():
    lat, lon, y, zh, zl, x, core = place()
    return lat, lax.rem(zl + 4, 8) * 8 + x * 2 + core


class Reduce:
    def __init__(self, s, j):
        lat, lon, y, zh, zl, x, core = place()
        self.s, self.j, self.core, self.x = s, j, core, x
        self.own = y * 4 + x
        self.near, self.far, self.half = lax.rem(zl, 4), zh * 2 + zl // 4, zl // 4
        self.used = 0
        own, table = self.own, 16 + x
        near, far, half = self.near, self.far, self.half
        stages = [[], [], [], [], []]
        for first, count in ((0, 12), (12, 4)):
            slots = pl.ds(first, count)
            stages[0].append(
                self.copy(s.payload.at[j, 1 - core, slots], s.in_core.at[j, slots], sibling())
            )
        for i, (dx, peer, slot) in enumerate(plane_peers()):
            stages[1].append(self.copy(s.half.at[j, slot], s.in_plane.at[j, i], peer))
            stages[4].append(self.copy(s.red.at[j, core, own], s.red.at[j, core, own], peer))
            if dx:
                px = lax.rem(x + dx, 4)
                stages[1].append(self.copy(s.half.at[j, 13 + px], s.in_plane.at[j, 14 + dx], peer))
                stages[4].append(
                    self.copy(s.red.at[j, core, table], s.red.at[j, core, table], peer)
                )
        for peer in near_peers():
            stages[2].append(self.copy(s.near.at[j, near], s.near.at[j, near], peer))
        for peer in far_peers():
            stages[3].append(self.copy(s.far.at[j, far], s.far.at[j, far], peer))
        stages[3].append(self.copy(s.far_tab.at[j, half], s.far_tab.at[j, half], half_peer()))
        stages.append([self.copy(s.red.at[j, core], s.red.at[j, core], sibling())])
        self.stages = stages

    def copy(self, src, dst, peer):
        number, self.used = self.used, self.used + 1
        return pltpu.make_async_remote_copy(
            src_ref=src,
            dst_ref=dst,
            send_sem=self.s.ar_send.at[self.j, number],
            recv_sem=self.s.ar_recv.at[self.j, number],
            device_id=peer,
            device_id_type=MESH,
        )

    def step(self, number):
        s, j, core = self.s, self.j, self.core
        if number > 0:
            for copy in self.stages[number - 1]:
                copy.wait_recv()
        if number == 1:
            for slot in range(16):
                total = s.payload[j, core, slot].astype(F32) + s.in_core[j, slot].astype(F32)
                s.half[j, slot] = total.astype(BF16)
        if number == 2:
            total = s.half[j, self.own].astype(F32)
            for i in range(15):
                total = total + s.in_plane[j, i].astype(F32)
            table = s.half[j, 13 + self.x].astype(F32)
            for i in range(15, 18):
                table = table + s.in_plane[j, i].astype(F32)
            s.near[j, self.near, 0:48] = total.astype(BF16)
            s.near[j, self.near, 48:96] = table.astype(BF16)
        if number == 3:
            total = s.near[j, 0].astype(F32)
            for i in range(1, 4):
                total = total + s.near[j, i].astype(F32)
            s.far[j, self.far] = total[0:48].astype(BF16)
            s.far_tab[j, self.half] = total[48:96].astype(BF16)
        if number == 4:
            total = s.far[j, 0].astype(F32)
            for i in range(1, 4):
                total = total + s.far[j, i].astype(F32)
            s.red[j, core, self.own] = total.astype(BF16)
            table = s.far_tab[j, 0].astype(F32) + s.far_tab[j, 1].astype(F32)
            s.red[j, core, 16 + self.x] = table.astype(BF16)
        if 0 < number < 6:
            for copy in self.stages[number]:
                copy.start()
        if number > 0:
            for copy in self.stages[number - 1]:
                copy.wait_send()


def signal_partners(halos):
    barrier = pltpu.get_barrier_semaphore()
    partners = halos[0].partners + halos[-1].partners
    partners += far_peers() + near_peers() + [p for _, p, _ in plane_peers()]
    partners += [sibling(), half_peer()]
    for partner in partners:
        pl.semaphore_signal(barrier, inc=1, device_id=partner, device_id_type=MESH)
    return barrier, len(partners)


SCRATCH = dict(
    x_in=pltpu.VMEM((6, 12, 2, 192), BF16),
    cot_in=pltpu.VMEM((6, 12, 2, 192), BF16),
    gains=pltpu.VMEM((2, 192), F32),
    wqkv=pltpu.VMEM((2, 192, 576), BF16),
    wproj=pltpu.VMEM((2, 192, 192), BF16),
    tab_in=pltpu.VMEM((2, 6, 23, 1, 144), F32),
    pad=pltpu.SMEM((48,), jnp.int32),
    loads=pltpu.SemaphoreType.DMA((7,)),
    out=pltpu.VMEM((6, 12, 2, 192), BF16),
    dx=pltpu.VMEM((6, 12, 2, 192), BF16),
    stores=pltpu.SemaphoreType.DMA((4,)),
    tab=pltpu.VMEM((6, 24, 144), F32),
    wide=pltpu.VMEM((2, 144, 1024), F32),
    bias1=pltpu.VMEM((144, 864), F32),
    bias2=pltpu.VMEM((2, 72, 432), F32),
    ds=pltpu.VMEM((144, 1024), F32),
    normed=pltpu.VMEM((2, 144, 192), F32),
    inverse=pltpu.VMEM((2, 144, 1), F32),
    scaled=pltpu.VMEM((2, 144, 192), BF16),
    k=pltpu.VMEM((2, 144, 192), F32),
    v=pltpu.VMEM((2, 144, 192), F32),
    qm=pltpu.VMEM((2, 864, 192), BF16),
    backm=pltpu.VMEM((2, 864, 192), BF16),
    probs=pltpu.VMEM((2, 144, 864), F32),
    mixed_t=pltpu.VMEM((2, 2, 192, 144), F32),
    grad=pltpu.VMEM((192, 768), F32),
    extra=pltpu.VMEM((192, 256), F32),
    halo_out=pltpu.VMEM((4, 4, 64, 128), BF16),
    halo_in=pltpu.VMEM((4, 4, 64, 128), BF16),
    payload=pltpu.VMEM((2, 2, 16, 48, 128), BF16),
    in_core=pltpu.VMEM((2, 16, 48, 128), BF16),
    half=pltpu.VMEM((2, 17, 48, 128), BF16),
    in_plane=pltpu.VMEM((2, 18, 48, 128), BF16),
    near=pltpu.VMEM((2, 4, 96, 128), BF16),
    far=pltpu.VMEM((2, 4, 48, 128), BF16),
    far_tab=pltpu.VMEM((2, 2, 48, 128), BF16),
    red=pltpu.VMEM((2, 2, 20, 48, 128), BF16),
    halo_send=pltpu.SemaphoreType.DMA((4, 4)),
    halo_recv=pltpu.SemaphoreType.DMA((4, 4)),
    ar_send=pltpu.SemaphoreType.DMA((2, 48)),
    ar_recv=pltpu.SemaphoreType.DMA((2, 48)),
)


class Names:
    pass


def main_kernel(
    x_ref, cot_ref, gains_ref, wqkv_ref, wproj_ref, tab_ref, pad_ref,
    out_ref, dx_ref, red_ref, *scratch,
):
    s = Names()
    for name, ref in zip(SCRATCH, scratch):
        setattr(s, name, ref)
    lat = lax.axis_index("lat")
    sources = dict(
        x_in=x_ref, tab_in=tab_ref, pad=pad_ref, gains=gains_ref, wqkv=wqkv_ref,
        wproj=wproj_ref, cot_in=cot_ref,
    )
    loads = {
        name: pltpu.make_async_copy(ref, getattr(s, name), s.loads.at[i])
        for i, (name, ref) in enumerate(sources.items())
    }
    for load in loads.values():
        load.start()
    h_first, h_cot, h_out, h_grad = halos = [Halo(s, i, i < 2) for i in range(4)]
    barrier, expected = signal_partners(halos)
    reduce2, reduce1 = Reduce(s, 1), Reduce(s, 0)

    s.tab[...] = jnp.zeros((6, 24, 144), F32)
    s.ds[:, 768:1024] = jnp.zeros((144, 256), F32)
    s.extra[...] = jnp.zeros((192, 256), F32)
    s.half[:, 16] = jnp.zeros((2, 48, 128), BF16)
    s.red[:, :, 19] = jnp.zeros((2, 2, 48, 128), BF16)

    def field(ref):
        return ref[...].astype(F32).reshape(144, 192).astype(BF16)

    def store(number, value, ref):
        copy = pltpu.make_async_copy(value, ref, s.stores.at[number])
        copy.start()
        return copy

    for load in loads.values():
        load.wait()
    gain1, gain2 = s.gains[0:1, :], s.gains[1:2, :]
    x1 = nn(reorder("a", "n"), field(s.x_in))
    expand_first(s, lat)
    attend(s, 0, x1, gain1, s.wqkv, lambda g: s.bias1[...], 1)
    first = pack(project(s, 0, x1, s.wproj, 1), "a")
    cot = pack(field(s.cot_in), "n")
    pl.semaphore_wait(barrier, expected)
    h_first.start(first)
    h_cot.start(cot)

    expand_second(s, lat)
    g2 = unpack(h_cot.finish(), "b").astype(BF16)
    head_backs(s, 1, g2, s.wproj, 2)
    x2 = unpack(h_first.finish(), "b")
    attend(s, 1, x2, gain2, s.wqkv, lambda g: s.bias2[g], 2)
    d_packed = backward(s, 1, 2)
    dh2, d_scaled = norm_backward(s, 1, g2, d_packed, gain2, s.wqkv)
    h_grad.start(pack(dh2, "b"))
    h_out.start(pack(project(s, 1, x2, s.wproj, 2), "b"))
    weight_gradients(s, 1, g2, d_packed, 2)
    reduce2.stages[0][0].start()
    other_gradients(s, 1, d_scaled, fold_second(s))
    reduce2.stages[0][1].start()
    h_cot.sent()
    h_first.sent()
    reduce2.step(1)
    g1 = unpack(h_grad.finish(), "a").astype(BF16)
    head_backs(s, 0, g1, s.wproj, 1)
    d_packed = backward(s, 0, 1)
    weight_gradients(s, 0, g1, d_packed, 1)
    reduce1.stages[0][0].start()
    dx, d_scaled = norm_backward(s, 0, g1, d_packed, gain1, s.wqkv)
    other_gradients(s, 0, d_scaled, fold_first(s))
    reduce1.stages[0][1].start()
    reduce2.step(2)
    reduce1.step(1)
    s.dx[...] = nn(reorder("n", "a"), dx).reshape(6, 12, 2, 192).astype(BF16)
    stores = [store(0, s.dx, dx_ref)]
    s.out[...] = unpack(h_out.finish(), "n").reshape(6, 12, 2, 192).astype(BF16)
    stores.append(store(1, s.out, out_ref))
    h_grad.sent()
    h_out.sent()
    reduce2.step(3)
    reduce1.step(2)
    reduce2.step(4)
    reduce1.step(3)
    reduce2.step(5)
    reduce1.step(4)
    reduce2.step(6)
    stores.append(store(2, s.red.at[1], red_ref.at[1]))
    reduce1.step(5)
    reduce1.step(6)
    stores.append(store(3, s.red.at[0], red_ref.at[0]))
    for copy in stores:
        copy.wait()


def finish_kernel(
    red_ref, o_ref, d_ref, out_ref, dx_ref, gains_ref, dqkv_ref, dproj_ref, dtab_ref, red, sems
):
    copies = [
        pltpu.make_async_copy(source, target, sems.at[i])
        for i, (source, target) in enumerate(
            ((red_ref.at[1], red.at[1]), (red_ref.at[0], red.at[0]), (o_ref, out_ref), (d_ref, dx_ref))
        )
    ]
    for copy in copies:
        copy.start()
    for j in (1, 0):
        copies[1 - j].wait()
        for half in range(2):
            for slot in range(12):
                column, row = half * 3 + slot // 4, (slot % 4) * 48
                rows = slice(row, row + 48)
                value = red[j, half, slot].astype(F32)
                if column < 4:
                    dqkv_ref[j, rows, 128 * column : 128 * column + 128] = value
                elif column == 4:
                    dqkv_ref[j, rows, 512:576] = value[:, 0:64]
                    dproj_ref[j, rows, 0:64] = value[:, 64:128]
                else:
                    dproj_ref[j, rows, 64:192] = value
            width = 128 if half == 0 else 16
            lanes = slice(128 * half, 128 * half + width)
            for third in range(3):
                value = red[j, half, 16 + third].astype(F32)
                for i in range(2):
                    dtab_ref[j, 2 * third + i, :, 0, lanes] = value[24 * i : 24 * i + 23, 0:width]
        gains_ref[j : j + 1, 0:128] = red[j, 0, 12].astype(F32)[0:1]
        gains_ref[j : j + 1, 128:192] = red[j, 1, 12].astype(F32)[0:1, 0:64]
    for copy in copies[2:]:
        copy.wait()


def body(inputs, cotangent, gains, qkv_weights, proj_weights, bias_tables, pad_rows):
    vmem = pl.BlockSpec(memory_space=pltpu.VMEM)
    hbm = pl.BlockSpec(memory_space=pltpu.HBM)
    field = jax.ShapeDtypeStruct((6, 12, 2, 192), BF16)
    out, dx, red = pl.pallas_call(
        main_kernel,
        out_shape=(field, field, jax.ShapeDtypeStruct((2, 2, 20, 48, 128), BF16)),
        in_specs=[hbm] * 7,
        out_specs=(hbm,) * 3,
        scratch_shapes=list(SCRATCH.values()),
        compiler_params=pltpu.CompilerParams(
            collective_id=0, has_side_effects=True, vmem_limit_bytes=VMEM_LIMIT
        ),
        name="both_blocks",
    )(
        inputs.transpose(1, 2, 0, 3),
        cotangent.transpose(1, 2, 0, 3),
        gains,
        qkv_weights,
        proj_weights,
        bias_tables.transpose(0, 2, 3, 1, 4),
        pad_rows,
    )
    out, dx, d_gains, d_qkv, d_proj, d_tables = pl.pallas_call(
        finish_kernel,
        out_shape=(
            field,
            field,
            jax.ShapeDtypeStruct((2, 192), F32),
            jax.ShapeDtypeStruct((2, 192, 576), F32),
            jax.ShapeDtypeStruct((2, 192, 192), F32),
            jax.ShapeDtypeStruct((2, 6, 23, 1, 144), F32),
        ),
        in_specs=[hbm] * 3,
        out_specs=(vmem,) * 6,
        scratch_shapes=[
            pltpu.VMEM((2, 2, 20, 48, 128), BF16),
            pltpu.SemaphoreType.DMA((4,)),
        ],
        compiler_params=pltpu.CompilerParams(vmem_limit_bytes=VMEM_LIMIT),
        name="unpack",
    )(red, out, dx)
    return (
        out.transpose(2, 0, 1, 3),
        dx.transpose(2, 0, 1, 3),
        d_gains,
        d_qkv,
        d_proj,
        d_tables.transpose(0, 3, 1, 2, 4),
    )


def solution(mesh):
    field = P(None, "lat", "lon", None)
    tables = P(None, "lat", None, None, None)
    return jax.shard_map(
        body,
        mesh=mesh,
        in_specs=(field, field, P(), P(), P(), tables, P()),
        out_specs=(field, field, P(), P(), P(), tables),
        check_vma=False,
    )
```

```python
import jax
import jax.numpy as jnp
from jax import lax
from jax.experimental import pallas as pl
from jax.experimental.pallas import tpu as pltpu
from jax.sharding import PartitionSpec as P

F32 = jnp.float32
BF16 = jnp.bfloat16
MESH = pl.DeviceIdType.MESH
HEADS = 6
VMEM_LIMIT = 62 * 2**20
SCALE = 32 ** (-0.5)


def div(x, d):
    return (x * (-(-(2**20) // d))) >> 20


def tokens_of(order, n):
    i = lax.broadcasted_iota(jnp.int32, (n, 1), 0)
    used = i < n
    if order == "n":
        r = div(i, 24)
        c = div(i - 24 * r, 2)
        l = i - 24 * r - 2 * c
    elif order == "a":
        c = div(i, 12)
        l = div(i - 12 * c, 6)
        r = i - 12 * c - 6 * l
    elif order == "b":
        l = div(i, 72)
        c = div(i - 72 * l, 6)
        r = i - 72 * l - 6 * c
    else:
        q = i >> 6
        inner = i - 64 * q
        used = inner < 36
        if order == "s1":
            inner, used = inner - 36, (inner >= 36) & (inner < 54)
        if order == "s2":
            inner, used = inner - 18, (inner >= 36) & (inner < 54)
        l = div(inner, 18)
        r = div(inner - 18 * l, 6)
        c = inner - 18 * l - 6 * r
        r, c = r + 3 * (q >> 1), c + 6 * (q & 1)
    return l, r, c, used


def place_in(order, l, r, c):
    if order == "n":
        return 24 * r + 2 * c + l
    if order == "a":
        return 12 * c + 6 * l + r
    if order == "b":
        return 72 * l + 6 * c + r
    lower, right = (r >= 3).astype(jnp.int32), (c >= 6).astype(jnp.int32)
    quarter = 64 * (2 * lower + right)
    inner = 18 * l + 6 * (r - 3 * lower) + c - 6 * right
    if order == "s":
        return quarter + inner
    if order == "s1":
        return jnp.where(inner < 18, quarter + 36 + inner, -1)
    return jnp.where(inner >= 18, quarter + 18 + inner, -1)


def reorder(to, of):
    n, m = [256 if order[0] == "s" else 144 for order in (to, of)]
    l, r, c, used = tokens_of(to, n)
    place = jnp.where(used, place_in(of, l, r, c), -1)
    return jnp.where(place == lax.broadcasted_iota(jnp.int32, (n, m), 1), 1.0, 0.0).astype(BF16)


def pack(x, order):
    wide, rest = x[:, 0:128], x[:, 128:192]
    pairs = [nn(reorder(to, order), rest) for to in ("s1", "s2")]
    return (nn(reorder("s", order), wide) + jnp.concatenate(pairs, 1)).astype(BF16)


def unpack(x, order):
    left, right = nn(reorder(order, "s1"), x), nn(reorder(order, "s2"), x)
    rest = left[:, 0:64] + right[:, 64:128]
    return jnp.concatenate([nn(reorder(order, "s"), x), rest], 1)


def spread(lanes, step, par, parts):
    i = lax.broadcasted_iota(jnp.int32, (72 * parts, 1), 0)
    part = div(i, 72)
    h = div(i - 72 * part, 24)
    o = i - 72 * part - 24 * h
    start = 12 * step * par + 24 * step * h + (22 - o) * step
    at = lax.broadcasted_iota(jnp.int32, (72 * parts, lanes), 1) - start
    return jnp.where((at >= 0) & (at < step), 1.0, 0.0).astype(BF16)


def lane_info(lanes, step):
    lane = lax.broadcasted_iota(jnp.int32, (1, lanes), 1)
    head = div(lane, 12 * step)
    parity = jnp.where(head < HEADS, head & 1, 2)
    return lane - step * div(lane, step), lane - 12 * step * head, parity


def nn(a, b):
    return lax.dot_general(a, b, (((1,), (0,)), ((), ())), preferred_element_type=F32)


def nt(a, b):
    return lax.dot_general(a, b, (((1,), (1,)), ((), ())), preferred_element_type=F32)


def tn(a, b):
    return lax.dot_general(a, b, (((0,), (0,)), ((), ())), preferred_element_type=F32)


def head_stack(x):
    lane = lax.broadcasted_iota(jnp.int32, (1, 192), 1)
    parts = [jnp.where((lane >= 32 * h) & (lane < 32 * h + 32), x, 0.0) for h in range(HEADS)]
    return jnp.concatenate(parts, 0).astype(BF16)


def head_diagonal(x, n):
    return jnp.concatenate(
        [x[32 * h : 32 * h + 32, n * h : n * h + n] for h in range(HEADS)], 0
    )


def split_table(s, block):
    out = []
    for h in range(HEADS):
        s.tab[h, 0:23, :] = s.tab_in[block, h, :, 0, :]
    for par in range(2):
        parts = [[], [], []]
        for h in range(3):
            t = s.tab[2 * h + par]
            hi = t.astype(BF16).astype(F32)
            rest = t - hi
            mid = rest.astype(BF16).astype(F32)
            for part, value in zip(parts, (hi, mid, rest - mid)):
                part.append(value)
        out.append(jnp.concatenate(sum(parts, []), 0).astype(BF16))
    return out


def row_flags(s, start):
    rows = lax.broadcasted_iota(jnp.int32, (6, 1), 0)
    flags = jnp.zeros((6, 1), jnp.int32)
    for r in range(6):
        flags = jnp.where(rows == r, s.pad[lax.rem(start + r, 48)], flags)
    return rows, flags == 1


def expand_first(s, lat):
    for par, parts in enumerate(split_table(s, 0)):
        s.wide[par] = tn(parts, spread(1024, 12, par, 3))
    entry, token, parity = lane_info(1024, 12)
    token, odd = token[:, 0:864], parity[:, 0:864] == 1
    rows, valid = row_flags(s, 6 * lat)
    for lk in range(2):
        strips = []
        for par in range(2):
            strip = jnp.zeros((6, 1024), F32)
            for e in range(12):
                at = 72 * (e // 6) + 36 * lk + 6 * (e % 6)
                strip = jnp.where(entry == e, s.wide[par, at : at + 6, :], strip)
            strips.append(strip)
        for ck in range(12):
            turn = (1024 - (11 - ck) * 12) % 1024
            even_part, odd_part = [
                (pltpu.roll(x, turn, 1) if turn else x)[:, 0:864] for x in strips
            ]
            at = 12 * ck + 6 * lk
            keep = valid | (token == rows + at)
            s.bias1[at : at + 6, :] = jnp.where(
                keep, jnp.where(odd, odd_part, even_part), -1e30
            )


def expand_second(s, lat):
    for par, parts in enumerate(split_table(s, 1)):
        s.wide[par, :, 0:512] = tn(parts, spread(512, 6, par, 3))
    entry, token, parity = lane_info(512, 6)
    token, odd = token[:, 0:432], parity[:, 0:432] == 1
    rows, valid = row_flags(s, 6 * lat + 3)
    q_band = jnp.where(lat == 7, (entry[:, 0:432] >= 3).astype(jnp.int32), 0)
    k_band = jnp.where(lat == 7, (rows >= 3).astype(jnp.int32), 0)
    same = q_band == k_band
    for lev in range(2):
        strips = []
        for par in range(2):
            strip = jnp.zeros((6, 512), F32)
            for e in range(6):
                at = 108 * (1 - lev) + 6 * e
                strip = jnp.where(entry == e, s.wide[par, at : at + 6, 0:512], strip)
            strips.append(strip)
        for ck in range(12):
            turn = (512 - (11 - ck) * 6) % 512
            even_part, odd_part = [
                (pltpu.roll(x, turn, 1) if turn else x)[:, 0:432] for x in strips
            ]
            at = 6 * ck
            keep = (valid | (token == rows + at)) & same
            s.bias2[lev, at : at + 6, :] = jnp.where(
                keep, jnp.where(odd, odd_part, even_part), -1e30
            )


def fold_first(s):
    entry, _, parity = lane_info(1024, 12)
    for par in range(2):
        mine = parity == par
        for lk in range(2):
            acc = jnp.zeros((6, 1024), F32)
            for ck in range(12):
                at = 12 * ck + 6 * lk
                piece = jnp.where(mine, s.ds[at : at + 6, :], 0.0)
                turn = (11 - ck) * 12
                acc = acc + (pltpu.roll(piece, turn, 1) if turn else piece)
            for e in range(12):
                at = 72 * (e // 6) + 36 * lk + 6 * (e % 6)
                s.wide[par, at : at + 6, :] = jnp.where(entry == e, acc, 0.0)
    return [nt(spread(1024, 12, par, 1), s.wide[par].astype(BF16)) for par in range(2)]


def fold_second(s):
    entry, _, parity = lane_info(512, 6)
    s.wide[:, :, 0:512] = jnp.zeros((2, 144, 512), F32)
    for par in range(2):
        mine = parity == par
        for lev in range(2):
            acc = jnp.zeros((6, 512), F32)
            for ck in range(12):
                at = 72 * lev + 6 * ck
                piece = jnp.where(mine, s.ds[at : at + 6, 0:512], 0.0)
                turn = (11 - ck) * 6
                acc = acc + (pltpu.roll(piece, turn, 1) if turn else piece)
            for e in range(6):
                at = 108 * (1 - lev) + 6 * e
                s.wide[par, at : at + 6, 0:512] = jnp.where(entry == e, acc, 0.0)
    return [nt(spread(512, 6, par, 1), s.wide[par, :, 0:512].astype(BF16)) for par in range(2)]


def attend(s, j, x, gain, wqkv_ref, bias, groups):
    n = 144 // groups
    center = x - jnp.mean(x, -1, keepdims=True)
    inverse = lax.rsqrt(jnp.mean(center * center, -1, keepdims=True) + 1e-05)
    normed = center * inverse
    scaled = (normed * gain).astype(BF16)
    packed = nn(scaled, wqkv_ref[j])
    q, k, v = packed[:, 0:192], packed[:, 192:384], packed[:, 384:576]
    s.normed[j] = normed
    s.inverse[j] = inverse
    s.scaled[j] = scaled
    s.k[j] = k
    s.v[j] = v
    for g in range(groups):
        rows = slice(g * n, g * n + n)
        qm = head_stack(q[rows])
        s.qm[j, g * 6 * n : (g + 1) * 6 * n, :] = qm
        scores = nt(k[rows].astype(BF16), qm) * SCALE + bias(g)
        weight = jnp.exp(scores - jnp.max(scores, 0, keepdims=True))
        probs = weight * (1.0 / jnp.sum(weight, 0, keepdims=True))
        s.probs[j, rows, 0 : 6 * n] = probs


def project(s, j, x, wproj_ref, groups):
    n = 144 // groups
    attended = []
    for g in range(groups):
        rows = slice(g * n, g * n + n)
        v, probs = s.v[j, rows, :], s.probs[j, rows, 0 : 6 * n]
        mixed_t = head_diagonal(tn(v.astype(BF16), probs.astype(BF16)), n)
        s.mixed_t[j, g, :, 0:n] = mixed_t
        attended.append(tn(mixed_t.astype(BF16), wproj_ref[j]))
    att = attended[0] if groups == 1 else jnp.concatenate(attended, 0)
    return (x + att).astype(BF16)


def head_backs(s, j, g_in, wproj_ref, groups):
    n = 144 // groups
    back = nt(g_in, wproj_ref[j])
    for g in range(groups):
        s.backm[j, g * 6 * n : (g + 1) * 6 * n, :] = head_stack(back[g * n : g * n + n])


def backward(s, j, groups):
    n = 144 // groups
    dqs, dks, dvs = [], [], []
    for g in range(groups):
        rows = slice(g * n, g * n + n)
        backm = s.backm[j, g * 6 * n : (g + 1) * 6 * n, :]
        probs = s.probs[j, rows, 0 : 6 * n]
        k = s.k[j, rows, :].astype(BF16)
        v = s.v[j, rows, :].astype(BF16)
        qm = s.qm[j, g * 6 * n : (g + 1) * 6 * n, :]
        d_probs = nt(v, backm)
        dvs.append(nn(probs.astype(BF16), backm))
        d_scores = probs * (d_probs - jnp.sum(d_probs * probs, 0, keepdims=True))
        s.ds[rows, 0 : 6 * n] = d_scores
        d_rounded = (d_scores * SCALE).astype(BF16)
        dks.append(nn(d_rounded, qm))
        dqs.append(head_diagonal(tn(k, d_rounded), n).T)
    if groups == 1:
        dq, dk, dv = dqs[0], dks[0], dvs[0]
    else:
        dq, dk, dv = [jnp.concatenate(p, 0) for p in (dqs, dks, dvs)]
    return dq.astype(BF16), dk.astype(BF16), dv.astype(BF16)


def norm_backward(s, j, g_in, d_packed, gain, wqkv_ref):
    w = wqkv_ref[j]
    d_scaled = sum(nt(d_packed[i], w[:, 192 * i : 192 * i + 192]) for i in range(3))
    normed = s.normed[j]
    d_normed = d_scaled * gain
    d_hidden = s.inverse[j] * (
        d_normed
        - jnp.mean(d_normed, -1, keepdims=True)
        - normed * jnp.mean(d_normed * normed, -1, keepdims=True)
    )
    return (g_in.astype(F32) + d_hidden).astype(BF16), d_scaled


def weight_gradients(s, j, g_in, d_packed, groups):
    n = 144 // groups
    scaled = s.scaled[j]
    for i, part in enumerate(d_packed):
        s.grad[:, 192 * i : 192 * i + 192] = tn(scaled, part)
    d_proj = jnp.zeros((192, 192), F32)
    for g in range(groups):
        d_proj = d_proj + nn(
            s.mixed_t[j, g, :, 0:n].astype(BF16), g_in[g * n : g * n + n]
        )
    s.grad[:, 576:768] = d_proj
    for half in range(2):
        for slot in range(12):
            column, row = half * 384 + (slot // 4) * 128, (slot % 4) * 48
            s.payload[j, half, slot] = s.grad[row : row + 48, column : column + 128].astype(BF16)


def other_gradients(s, j, d_scaled, folded):
    for h in range(HEADS):
        s.extra[24 * h : 24 * h + 24, 0:144] = folded[h % 2][24 * (h // 2) : 24 * (h // 2) + 24]
    s.extra[144:145, 0:192] = jnp.sum(d_scaled * s.normed[j], 0, keepdims=True)
    for half in range(2):
        for slot, row in ((12, 144), (13, 0), (14, 48), (15, 96)):
            s.payload[j, half, slot] = s.extra[
                row : row + 48, 128 * half : 128 * half + 128
            ].astype(BF16)


class Halo:
    def __init__(self, s, which, forward_shift):
        lat, lon = lax.axis_index("lat"), lax.axis_index("lon")
        home_lat, home_lon = runs_at(lat, lon)
        nlat, nlon = lax.axis_size("lat"), lax.axis_size("lon")
        self.s, self.which = s, which
        self.copies, self.partners = [], []
        for quarter in range(4):
            down, right = quarter // 2, quarter % 2
            if forward_shift:
                peer = runs_at(
                    lax.rem(lat + down - 1 + nlat, nlat), lax.rem(lon + right - 1 + nlon, nlon)
                )
            else:
                peer = lax.rem(home_lat + down, nlat), lax.rem(home_lon + right, nlon)
            self.partners.append(peer)
            self.copies.append(
                pltpu.make_async_remote_copy(
                    src_ref=s.halo_out.at[which, quarter],
                    dst_ref=s.halo_in.at[which, 3 - quarter],
                    send_sem=s.halo_send.at[which],
                    recv_sem=s.halo_recv.at[which],
                    device_id=peer,
                    device_id_type=MESH,
                )
            )
        self.all = pltpu.make_async_remote_copy(
            src_ref=s.halo_out.at[which],
            dst_ref=s.halo_in.at[which],
            send_sem=s.halo_send.at[which],
            recv_sem=s.halo_recv.at[which],
            device_id=self.partners[0],
            device_id_type=MESH,
        )

    def start(self, quarters):
        self.s.halo_out[self.which] = quarters.reshape(4, 64, 128)
        for copy in self.copies:
            copy.start()

    def finish(self):
        self.all.wait_recv()
        return self.s.halo_in[self.which].reshape(256, 128)

    def sent(self):
        self.all.wait_send()


def place():
    lat, lon = lax.axis_index("lat"), lax.axis_index("lon")
    line = lax.rem(lon, 8)
    return lat, lon, lat // 2, lax.rem(lat, 2), lon // 8, line // 2, lax.rem(line, 2)


def runs_at(lat, lon):
    return lat, lax.rem(lon + 32, 64)


def sibling():
    lat, lon, y, zh, zl, x, core = place()
    return lat, zl * 8 + x * 2 + 1 - core


def plane_peers():
    lat, lon, y, zh, zl, x, core = place()
    hops = lambda step: min(step, 4 - step)
    steps = [(dx, dy) for dy in range(4) for dx in range(4) if dx or dy]
    out = []
    for dx, dy in sorted(steps, key=lambda step: -hops(step[0]) - hops(step[1])):
        py, px = lax.rem(y + dy, 4), lax.rem(x + dx, 4)
        out.append((dx if dy == 0 else 0, (py * 2 + zh, zl * 8 + px * 2 + core), py * 4 + px))
    return out


def near_peers():
    lat, lon, y, zh, zl, x, core = place()
    quad = (zl // 4) * 4
    return [(lat, (quad + lax.rem(zl + d, 4)) * 8 + x * 2 + core) for d in range(1, 4)]


def far_peers():
    lat, lon, y, zh, zl, x, core = place()
    out = []
    for d in range(1, 4):
        z = lax.rem(zh * 8 + zl + 4 * d, 16)
        out.append((y * 2 + z // 8, lax.rem(z, 8) * 8 + x * 2 + core))
    return out


def half_peer():
    lat, lon, y, zh, zl, x, core = place()
    return lat, lax.rem(zl + 4, 8) * 8 + x * 2 + core


class Reduce:
    def __init__(self, s, j):
        lat, lon, y, zh, zl, x, core = place()
        self.s, self.j, self.core, self.x = s, j, core, x
        self.own = y * 4 + x
        self.near, self.far, self.half = lax.rem(zl, 4), zh * 2 + zl // 4, zl // 4
        own, table = self.own, 16 + x
        near, far, half = self.near, self.far, self.half
        stages = [[] for _ in range(6)]

        def add(number, src, dst, peer):
            stages[number].append(self.copy(number, src, dst, peer))

        for first, count in ((0, 12), (12, 4)):
            slots = pl.ds(first, count)
            add(0, s.payload.at[j, 1 - core, slots], s.in_core.at[j, slots], sibling())
        for i, (dx, peer, slot) in enumerate(plane_peers()):
            add(1, s.half.at[j, slot], s.in_plane.at[j, i], peer)
            add(4, s.red.at[j, core, own], s.red.at[j, core, own], peer)
            if dx:
                px = lax.rem(x + dx, 4)
                add(1, s.half.at[j, 13 + px], s.in_plane.at[j, 14 + dx], peer)
                add(4, s.red.at[j, core, table], s.red.at[j, core, table], peer)
        for peer in near_peers():
            add(2, s.near.at[j, near], s.near.at[j, near], peer)
        for peer in far_peers():
            add(3, s.far.at[j, far], s.far.at[j, far], peer)
        add(3, s.far_tab.at[j, half], s.far_tab.at[j, half], half_peer())
        for first, count in ((0, 13), (16, 3)):
            slots = pl.ds(first, count)
            add(5, s.red.at[j, core, slots], s.red.at[j, core, slots], sibling())
        self.stages = stages
        sizes = (
            s.in_core.at[j], s.in_plane.at[j], s.near.at[j, pl.ds(0, 3)], s.far.at[j],
            s.red.at[j, core, pl.ds(0, 18)], s.red.at[j, core, pl.ds(0, 16)],
        )
        self.all = [self.copy(i, size, size, sibling()) for i, size in enumerate(sizes)]

    def copy(self, number, src, dst, peer):
        return pltpu.make_async_remote_copy(
            src_ref=src,
            dst_ref=dst,
            send_sem=self.s.ar_send.at[self.j, number],
            recv_sem=self.s.ar_recv.at[self.j, number],
            device_id=peer,
            device_id_type=MESH,
        )

    def step(self, number):
        s, j, core = self.s, self.j, self.core
        if number > 0:
            self.all[number - 1].wait_recv()
        if number == 1:
            for slot in range(16):
                total = s.payload[j, core, slot].astype(F32) + s.in_core[j, slot].astype(F32)
                s.half[j, slot] = total.astype(BF16)
        if number == 2:
            total = s.half[j, self.own].astype(F32)
            for i in range(15):
                total = total + s.in_plane[j, i].astype(F32)
            table = s.half[j, 13 + self.x].astype(F32)
            for i in range(15, 18):
                table = table + s.in_plane[j, i].astype(F32)
            s.near[j, self.near, 0:48] = total.astype(BF16)
            s.near[j, self.near, 48:96] = table.astype(BF16)
        if number == 3:
            total = s.near[j, 0].astype(F32)
            for i in range(1, 4):
                total = total + s.near[j, i].astype(F32)
            s.far[j, self.far] = total[0:48].astype(BF16)
            s.far_tab[j, self.half] = total[48:96].astype(BF16)
        if number == 4:
            total = s.far[j, 0].astype(F32)
            for i in range(1, 4):
                total = total + s.far[j, i].astype(F32)
            s.red[j, core, self.own] = total.astype(BF16)
            table = s.far_tab[j, 0].astype(F32) + s.far_tab[j, 1].astype(F32)
            s.red[j, core, 16 + self.x] = table.astype(BF16)
        if 0 < number < 6:
            for copy in self.stages[number]:
                copy.start()
        if number > 0:
            self.all[number - 1].wait_send()


def signal_partners(halos):
    barrier = pltpu.get_barrier_semaphore()
    partners = halos[0].partners + halos[-1].partners
    ahead, opposite, behind = far_peers()
    partners += [ahead, behind] + [p for _, p, _ in plane_peers()] + near_peers()
    partners += [half_peer(), sibling()]
    for partner in partners:
        pl.semaphore_signal(barrier, inc=1, device_id=partner, device_id_type=MESH)
    return barrier, len(partners)


SCRATCH = dict(
    x_in=pltpu.VMEM((6, 12, 2, 192), BF16),
    cot_in=pltpu.VMEM((6, 12, 2, 192), BF16),
    gains=pltpu.VMEM((2, 192), F32),
    wqkv=pltpu.VMEM((2, 192, 576), BF16),
    wproj=pltpu.VMEM((2, 192, 192), BF16),
    tab_in=pltpu.VMEM((2, 6, 23, 1, 144), F32),
    pad=pltpu.SMEM((48,), jnp.int32),
    loads=pltpu.SemaphoreType.DMA((7,)),
    out=pltpu.VMEM((6, 12, 2, 192), BF16),
    dx=pltpu.VMEM((6, 12, 2, 192), BF16),
    stores=pltpu.SemaphoreType.DMA((5,)),
    tab=pltpu.VMEM((6, 24, 144), F32),
    wide=pltpu.VMEM((2, 144, 1024), F32),
    bias1=pltpu.VMEM((144, 864), F32),
    bias2=pltpu.VMEM((2, 72, 432), F32),
    ds=pltpu.VMEM((144, 1024), F32),
    normed=pltpu.VMEM((2, 144, 192), F32),
    inverse=pltpu.VMEM((2, 144, 1), F32),
    scaled=pltpu.VMEM((2, 144, 192), BF16),
    k=pltpu.VMEM((2, 144, 192), F32),
    v=pltpu.VMEM((2, 144, 192), F32),
    qm=pltpu.VMEM((2, 864, 192), BF16),
    backm=pltpu.VMEM((2, 864, 192), BF16),
    probs=pltpu.VMEM((2, 144, 864), F32),
    mixed_t=pltpu.VMEM((2, 2, 192, 144), F32),
    grad=pltpu.VMEM((192, 768), F32),
    extra=pltpu.VMEM((192, 256), F32),
    halo_out=pltpu.VMEM((4, 4, 64, 128), BF16),
    halo_in=pltpu.VMEM((4, 4, 64, 128), BF16),
    payload=pltpu.VMEM((2, 2, 16, 48, 128), BF16),
    in_core=pltpu.VMEM((2, 16, 48, 128), BF16),
    half=pltpu.VMEM((2, 17, 48, 128), BF16),
    in_plane=pltpu.VMEM((2, 18, 48, 128), BF16),
    near=pltpu.VMEM((2, 4, 96, 128), BF16),
    far=pltpu.VMEM((2, 4, 48, 128), BF16),
    far_tab=pltpu.VMEM((2, 2, 48, 128), BF16),
    red=pltpu.VMEM((2, 2, 20, 48, 128), BF16),
    relay=pltpu.SemaphoreType.REGULAR,
    halo_send=pltpu.SemaphoreType.DMA((4,)),
    halo_recv=pltpu.SemaphoreType.DMA((4,)),
    ar_send=pltpu.SemaphoreType.DMA((2, 6)),
    ar_recv=pltpu.SemaphoreType.DMA((2, 6)),
)


class Names:
    pass


def main_kernel(
    x_ref, cot_ref, gains_ref, wqkv_ref, wproj_ref, tab_ref, pad_ref,
    out_ref, dx_ref, red_ref, *scratch,
):
    s = Names()
    for name, ref in zip(SCRATCH, scratch):
        setattr(s, name, ref)
    lat = lax.axis_index("lat")
    sources = dict(
        x_in=x_ref, tab_in=tab_ref, pad=pad_ref, gains=gains_ref, wqkv=wqkv_ref,
        wproj=wproj_ref, cot_in=cot_ref,
    )
    loads = {
        name: pltpu.make_async_copy(ref, getattr(s, name), s.loads.at[i])
        for i, (name, ref) in enumerate(sources.items())
    }
    for load in loads.values():
        load.start()
    h_first, h_cot, h_out, h_grad = halos = [Halo(s, i, i < 2) for i in range(4)]
    barrier, expected = signal_partners(halos)
    reduce2, reduce1 = Reduce(s, 1), Reduce(s, 0)

    s.tab[...] = jnp.zeros((6, 24, 144), F32)
    s.ds[:, 768:1024] = jnp.zeros((144, 256), F32)
    s.extra[...] = jnp.zeros((192, 256), F32)
    s.half[:, 16] = jnp.zeros((2, 48, 128), BF16)
    s.red[:, :, 19] = jnp.zeros((2, 2, 48, 128), BF16)

    def field(ref):
        return ref[...].astype(F32).reshape(144, 192).astype(BF16)

    def store(number, value, ref):
        copy = pltpu.make_async_copy(value, ref, s.stores.at[number])
        copy.start()
        return copy

    for load in loads.values():
        load.wait()
    gain1, gain2 = s.gains[0:1, :], s.gains[1:2, :]
    x1 = nn(reorder("a", "n"), field(s.x_in))
    expand_first(s, lat)
    attend(s, 0, x1, gain1, s.wqkv, lambda g: s.bias1[...], 1)
    first = pack(project(s, 0, x1, s.wproj, 1), "a")
    pl.semaphore_wait(barrier, expected)
    h_first.start(first)
    pl.semaphore_signal(s.relay, inc=1, device_id=far_peers()[2], device_id_type=MESH)
    h_cot.start(pack(field(s.cot_in), "n"))

    expand_second(s, lat)
    g2 = unpack(h_cot.finish(), "b").astype(BF16)
    head_backs(s, 1, g2, s.wproj, 2)
    x2 = unpack(h_first.finish(), "b")
    pl.semaphore_wait(s.relay, 1)
    attend(s, 1, x2, gain2, s.wqkv, lambda g: s.bias2[g], 2)
    d_packed = backward(s, 1, 2)
    dh2, d_scaled = norm_backward(s, 1, g2, d_packed, gain2, s.wqkv)
    h_grad.start(pack(dh2, "b"))
    h_out.start(pack(project(s, 1, x2, s.wproj, 2), "b"))
    weight_gradients(s, 1, g2, d_packed, 2)
    reduce2.stages[0][0].start()
    other_gradients(s, 1, d_scaled, fold_second(s))
    reduce2.stages[0][1].start()
    h_cot.sent()
    h_first.sent()
    reduce2.step(1)
    g1 = unpack(h_grad.finish(), "a").astype(BF16)
    head_backs(s, 0, g1, s.wproj, 1)
    d_packed = backward(s, 0, 1)
    weight_gradients(s, 0, g1, d_packed, 1)
    reduce1.stages[0][0].start()
    dx, d_scaled = norm_backward(s, 0, g1, d_packed, gain1, s.wqkv)
    other_gradients(s, 0, d_scaled, fold_first(s))
    reduce1.stages[0][1].start()
    reduce1.step(1)
    reduce2.step(2)
    s.dx[...] = nn(reorder("n", "a"), dx).reshape(6, 12, 2, 192).astype(BF16)
    stores = [store(0, s.dx, dx_ref)]
    s.out[...] = unpack(h_out.finish(), "n").reshape(6, 12, 2, 192).astype(BF16)
    stores.append(store(1, s.out, out_ref))
    h_grad.sent()
    h_out.sent()
    reduce2.step(3)
    reduce1.step(2)
    reduce1.step(3)
    reduce2.step(4)
    reduce1.step(4)
    reduce2.step(5)
    reduce2.step(6)
    stores.append(store(2, s.red.at[1], red_ref.at[1]))
    reduce1.step(5)
    core = reduce1.core
    stores.append(store(3, s.red.at[0, core], red_ref.at[0, core]))
    reduce1.step(6)
    stores.append(store(4, s.red.at[0, 1 - core], red_ref.at[0, 1 - core]))
    for copy in stores:
        copy.wait()


def finish_kernel(
    red_ref, o_ref, d_ref, out_ref, dx_ref, gains_ref, dqkv_ref, dproj_ref, dtab_ref, red, sems
):
    copies = [
        pltpu.make_async_copy(source, target, sems.at[i])
        for i, (source, target) in enumerate(
            ((red_ref.at[1], red.at[1]), (red_ref.at[0], red.at[0]), (o_ref, out_ref), (d_ref, dx_ref))
        )
    ]
    for copy in copies:
        copy.start()
    for j in (1, 0):
        copies[1 - j].wait()
        for half in range(2):
            for slot in range(12):
                column, row = half * 3 + slot // 4, (slot % 4) * 48
                rows = slice(row, row + 48)
                value = red[j, half, slot].astype(F32)
                if column < 4:
                    dqkv_ref[j, rows, 128 * column : 128 * column + 128] = value
                elif column == 4:
                    dqkv_ref[j, rows, 512:576] = value[:, 0:64]
                    dproj_ref[j, rows, 0:64] = value[:, 64:128]
                else:
                    dproj_ref[j, rows, 64:192] = value
            width = 128 if half == 0 else 16
            lanes = slice(128 * half, 128 * half + width)
            for third in range(3):
                value = red[j, half, 16 + third].astype(F32)
                for i in range(2):
                    dtab_ref[j, 2 * third + i, :, 0, lanes] = value[24 * i : 24 * i + 23, 0:width]
        gains_ref[j : j + 1, 0:128] = red[j, 0, 12].astype(F32)[0:1]
        gains_ref[j : j + 1, 128:192] = red[j, 1, 12].astype(F32)[0:1, 0:64]
    for copy in copies[2:]:
        copy.wait()


def body(inputs, cotangent, gains, qkv_weights, proj_weights, bias_tables, pad_rows):
    vmem = pl.BlockSpec(memory_space=pltpu.VMEM)
    hbm = pl.BlockSpec(memory_space=pltpu.HBM)
    field = jax.ShapeDtypeStruct((6, 12, 2, 192), BF16)
    out, dx, red = pl.pallas_call(
        main_kernel,
        out_shape=(field, field, jax.ShapeDtypeStruct((2, 2, 20, 48, 128), BF16)),
        in_specs=[hbm] * 7,
        out_specs=(hbm,) * 3,
        scratch_shapes=list(SCRATCH.values()),
        compiler_params=pltpu.CompilerParams(
            collective_id=0, has_side_effects=True, vmem_limit_bytes=VMEM_LIMIT
        ),
        name="both_blocks",
    )(
        inputs.transpose(1, 2, 0, 3),
        cotangent.transpose(1, 2, 0, 3),
        gains,
        qkv_weights,
        proj_weights,
        bias_tables.transpose(0, 2, 3, 1, 4),
        pad_rows,
    )
    out, dx, d_gains, d_qkv, d_proj, d_tables = pl.pallas_call(
        finish_kernel,
        out_shape=(
            field,
            field,
            jax.ShapeDtypeStruct((2, 192), F32),
            jax.ShapeDtypeStruct((2, 192, 576), F32),
            jax.ShapeDtypeStruct((2, 192, 192), F32),
            jax.ShapeDtypeStruct((2, 6, 23, 1, 144), F32),
        ),
        in_specs=[hbm] * 3,
        out_specs=(vmem,) * 6,
        scratch_shapes=[
            pltpu.VMEM((2, 2, 20, 48, 128), BF16),
            pltpu.SemaphoreType.DMA((4,)),
        ],
        compiler_params=pltpu.CompilerParams(vmem_limit_bytes=VMEM_LIMIT),
        name="unpack",
    )(red, out, dx)
    return (
        out.transpose(2, 0, 1, 3),
        dx.transpose(2, 0, 1, 3),
        d_gains,
        d_qkv,
        d_proj,
        d_tables.transpose(0, 3, 1, 2, 4),
    )


def solution(mesh):
    field = P(None, "lat", "lon", None)
    tables = P(None, "lat", None, None, None)
    return jax.shard_map(
        body,
        mesh=mesh,
        in_specs=(field, field, P(), P(), P(), tables, P()),
        out_specs=(field, field, P(), P(), P(), tables),
        check_vma=False,
    )
```

```python
import jax
import jax.numpy as jnp
from jax import lax
from jax.experimental import pallas as pl
from jax.experimental.pallas import tpu as pltpu
from jax.sharding import PartitionSpec as P

F32 = jnp.float32
BF16 = jnp.bfloat16
MESH = pl.DeviceIdType.MESH
HEADS = 6
VMEM_LIMIT = 62 * 2**20
SCALE = 32 ** (-0.5)


def div(x, d):
    return (x * (-(-(2**20) // d))) >> 20


def tokens_of(order, n):
    i = lax.broadcasted_iota(jnp.int32, (n, 1), 0)
    used = i < n
    if order == "n":
        r = div(i, 24)
        c = div(i - 24 * r, 2)
        l = i - 24 * r - 2 * c
    elif order == "a":
        c = div(i, 12)
        l = div(i - 12 * c, 6)
        r = i - 12 * c - 6 * l
    elif order == "b":
        l = div(i, 72)
        c = div(i - 72 * l, 6)
        r = i - 72 * l - 6 * c
    else:
        q = i >> 6
        inner = i - 64 * q
        used = inner < 36
        if order == "s1":
            inner, used = inner - 36, (inner >= 36) & (inner < 54)
        if order == "s2":
            inner, used = inner - 18, (inner >= 36) & (inner < 54)
        l = div(inner, 18)
        r = div(inner - 18 * l, 6)
        c = inner - 18 * l - 6 * r
        r, c = r + 3 * (q >> 1), c + 6 * (q & 1)
    return l, r, c, used


def place_in(order, l, r, c):
    if order == "n":
        return 24 * r + 2 * c + l
    if order == "a":
        return 12 * c + 6 * l + r
    if order == "b":
        return 72 * l + 6 * c + r
    lower, right = (r >= 3).astype(jnp.int32), (c >= 6).astype(jnp.int32)
    quarter = 64 * (2 * lower + right)
    inner = 18 * l + 6 * (r - 3 * lower) + c - 6 * right
    if order == "s":
        return quarter + inner
    if order == "s1":
        return jnp.where(inner < 18, quarter + 36 + inner, -1)
    return jnp.where(inner >= 18, quarter + 18 + inner, -1)


SLOTS = ("s", "s1", "s2")


def reorder(to, of):
    n, m = [256 if order[0] == "s" else 144 for order in (to, of)]
    l, r, c, used = tokens_of(to, n)
    place = jnp.where(used, place_in(of, l, r, c), -1)
    return jnp.where(place == lax.broadcasted_iota(jnp.int32, (n, m), 1), 1.0, 0.0).astype(BF16)


def pack(x, order, ready=None):
    wide, rest = x[:, 0:128], x[:, 128:192]
    whole, first, second = ready or [reorder(to, order) for to in SLOTS]
    pairs = jnp.concatenate([nn(first, rest), nn(second, rest)], 1)
    return (nn(whole, wide) + pairs).astype(BF16)


def unpack(x, order, ready=None):
    whole, first, second = ready or [reorder(order, of) for of in SLOTS]
    rest = nn(first, x)[:, 0:64] + nn(second, x)[:, 64:128]
    return jnp.concatenate([nn(whole, x), rest], 1)


def spread(lanes, step, par, parts):
    i = lax.broadcasted_iota(jnp.int32, (72 * parts, 1), 0)
    part = div(i, 72)
    h = div(i - 72 * part, 24)
    o = i - 72 * part - 24 * h
    start = 12 * step * par + 24 * step * h + (22 - o) * step
    at = lax.broadcasted_iota(jnp.int32, (72 * parts, lanes), 1) - start
    return jnp.where((at >= 0) & (at < step), 1.0, 0.0).astype(BF16)


def lane_info(lanes, step):
    lane = lax.broadcasted_iota(jnp.int32, (1, lanes), 1)
    head = div(lane, 12 * step)
    parity = jnp.where(head < HEADS, head & 1, 2)
    return lane - step * div(lane, step), lane - 12 * step * head, parity


def nn(a, b):
    return lax.dot_general(a, b, (((1,), (0,)), ((), ())), preferred_element_type=F32)


def nt(a, b):
    return lax.dot_general(a, b, (((1,), (1,)), ((), ())), preferred_element_type=F32)


def tn(a, b):
    return lax.dot_general(a, b, (((0,), (0,)), ((), ())), preferred_element_type=F32)


def head_stack(x):
    lane = lax.broadcasted_iota(jnp.int32, (1, 192), 1)
    parts = [jnp.where((lane >= 32 * h) & (lane < 32 * h + 32), x, 0.0) for h in range(HEADS)]
    return jnp.concatenate(parts, 0).astype(BF16)


def head_diagonal(x, n):
    return jnp.concatenate(
        [x[32 * h : 32 * h + 32, n * h : n * h + n] for h in range(HEADS)], 0
    )


def split_table(s, block):
    out = []
    for h in range(HEADS):
        s.tab[h, 0:23, :] = s.tab_in[block, h, :, 0, :]
    for par in range(2):
        parts = [[], [], []]
        for h in range(3):
            t = s.tab[2 * h + par]
            hi = t.astype(BF16).astype(F32)
            rest = t - hi
            mid = rest.astype(BF16).astype(F32)
            for part, value in zip(parts, (hi, mid, rest - mid)):
                part.append(value)
        out.append(jnp.concatenate(sum(parts, []), 0).astype(BF16))
    return out


def row_flags(s, start):
    rows = lax.broadcasted_iota(jnp.int32, (6, 1), 0)
    flags = jnp.zeros((6, 1), jnp.int32)
    for r in range(6):
        flags = jnp.where(rows == r, s.pad[lax.rem(start + r, 48)], flags)
    return rows, flags == 1


def expand_first(s, lat):
    for par, parts in enumerate(split_table(s, 0)):
        s.wide[par] = tn(parts, spread(1024, 12, par, 3))
    entry, token, parity = lane_info(1024, 12)
    token, odd = token[:, 0:864], parity[:, 0:864] == 1
    rows, valid = row_flags(s, 6 * lat)
    for lk in range(2):
        strips = []
        for par in range(2):
            strip = jnp.zeros((6, 1024), F32)
            for e in range(12):
                at = 72 * (e // 6) + 36 * lk + 6 * (e % 6)
                strip = jnp.where(entry == e, s.wide[par, at : at + 6, :], strip)
            strips.append(strip)
        for ck in range(12):
            turn = (1024 - (11 - ck) * 12) % 1024
            even_part, odd_part = [
                (pltpu.roll(x, turn, 1) if turn else x)[:, 0:864] for x in strips
            ]
            at = 12 * ck + 6 * lk
            keep = valid | (token == rows + at)
            s.bias1[at : at + 6, :] = jnp.where(
                keep, jnp.where(odd, odd_part, even_part), -1e30
            )


def expand_second(s, lat):
    for par, parts in enumerate(split_table(s, 1)):
        s.wide[par, :, 0:512] = tn(parts, spread(512, 6, par, 3))
    entry, token, parity = lane_info(512, 6)
    token, odd = token[:, 0:432], parity[:, 0:432] == 1
    rows, valid = row_flags(s, 6 * lat + 3)
    q_band = jnp.where(lat == 7, (entry[:, 0:432] >= 3).astype(jnp.int32), 0)
    k_band = jnp.where(lat == 7, (rows >= 3).astype(jnp.int32), 0)
    same = q_band == k_band
    for lev in range(2):
        strips = []
        for par in range(2):
            strip = jnp.zeros((6, 512), F32)
            for e in range(6):
                at = 108 * (1 - lev) + 6 * e
                strip = jnp.where(entry == e, s.wide[par, at : at + 6, 0:512], strip)
            strips.append(strip)
        for ck in range(12):
            turn = (512 - (11 - ck) * 6) % 512
            even_part, odd_part = [
                (pltpu.roll(x, turn, 1) if turn else x)[:, 0:432] for x in strips
            ]
            at = 6 * ck
            keep = (valid | (token == rows + at)) & same
            s.bias2[lev, at : at + 6, :] = jnp.where(
                keep, jnp.where(odd, odd_part, even_part), -1e30
            )


def fold_first(s):
    entry, _, parity = lane_info(1024, 12)
    for par in range(2):
        mine = parity == par
        for lk in range(2):
            acc = jnp.zeros((6, 1024), F32)
            for ck in range(12):
                at = 12 * ck + 6 * lk
                piece = jnp.where(mine, s.ds[at : at + 6, :], 0.0)
                turn = (11 - ck) * 12
                acc = acc + (pltpu.roll(piece, turn, 1) if turn else piece)
            for e in range(12):
                at = 72 * (e // 6) + 36 * lk + 6 * (e % 6)
                s.wide[par, at : at + 6, :] = jnp.where(entry == e, acc, 0.0)
    return [nt(spread(1024, 12, par, 1), s.wide[par].astype(BF16)) for par in range(2)]


def fold_second(s):
    entry, _, parity = lane_info(512, 6)
    s.wide[:, :, 0:512] = jnp.zeros((2, 144, 512), F32)
    for par in range(2):
        mine = parity == par
        for lev in range(2):
            acc = jnp.zeros((6, 512), F32)
            for ck in range(12):
                at = 72 * lev + 6 * ck
                piece = jnp.where(mine, s.ds[at : at + 6, 0:512], 0.0)
                turn = (11 - ck) * 6
                acc = acc + (pltpu.roll(piece, turn, 1) if turn else piece)
            for e in range(6):
                at = 108 * (1 - lev) + 6 * e
                s.wide[par, at : at + 6, 0:512] = jnp.where(entry == e, acc, 0.0)
    return [nt(spread(512, 6, par, 1), s.wide[par, :, 0:512].astype(BF16)) for par in range(2)]


def attend(s, j, x, gain, wqkv_ref, bias, groups):
    n = 144 // groups
    center = x - jnp.mean(x, -1, keepdims=True)
    inverse = lax.rsqrt(jnp.mean(center * center, -1, keepdims=True) + 1e-05)
    normed = center * inverse
    scaled = (normed * gain).astype(BF16)
    packed = nn(scaled, wqkv_ref[j])
    q, k, v = packed[:, 0:192], packed[:, 192:384], packed[:, 384:576]
    s.normed[j] = normed
    s.inverse[j] = inverse
    s.scaled[j] = scaled
    s.k[j] = k
    s.v[j] = v
    for g in range(groups):
        rows = slice(g * n, g * n + n)
        qm = head_stack(q[rows])
        s.qm[j, g * 6 * n : (g + 1) * 6 * n, :] = qm
        scores = nt(k[rows].astype(BF16), qm) * SCALE + bias(g)
        weight = jnp.exp(scores - jnp.max(scores, 0, keepdims=True))
        probs = weight * (1.0 / jnp.sum(weight, 0, keepdims=True))
        s.probs[j, rows, 0 : 6 * n] = probs


def project(s, j, x, wproj_ref, groups):
    n = 144 // groups
    attended = []
    for g in range(groups):
        rows = slice(g * n, g * n + n)
        v, probs = s.v[j, rows, :], s.probs[j, rows, 0 : 6 * n]
        mixed_t = head_diagonal(tn(v.astype(BF16), probs.astype(BF16)), n)
        s.mixed_t[j, g, :, 0:n] = mixed_t
        attended.append(tn(mixed_t.astype(BF16), wproj_ref[j]))
    att = attended[0] if groups == 1 else jnp.concatenate(attended, 0)
    return (x + att).astype(BF16)


def head_backs(s, j, g_in, wproj_ref, groups):
    n = 144 // groups
    back = nt(g_in, wproj_ref[j])
    for g in range(groups):
        s.backm[j, g * 6 * n : (g + 1) * 6 * n, :] = head_stack(back[g * n : g * n + n])


def backward(s, j, groups):
    n = 144 // groups
    dqs, dks, dvs = [], [], []
    for g in range(groups):
        rows = slice(g * n, g * n + n)
        backm = s.backm[j, g * 6 * n : (g + 1) * 6 * n, :]
        probs = s.probs[j, rows, 0 : 6 * n]
        k = s.k[j, rows, :].astype(BF16)
        v = s.v[j, rows, :].astype(BF16)
        qm = s.qm[j, g * 6 * n : (g + 1) * 6 * n, :]
        d_probs = nt(v, backm)
        dvs.append(nn(probs.astype(BF16), backm))
        d_scores = probs * (d_probs - jnp.sum(d_probs * probs, 0, keepdims=True))
        s.ds[rows, 0 : 6 * n] = d_scores
        d_rounded = (d_scores * SCALE).astype(BF16)
        dks.append(nn(d_rounded, qm))
        dqs.append(head_diagonal(tn(k, d_rounded), n).T)
    if groups == 1:
        dq, dk, dv = dqs[0], dks[0], dvs[0]
    else:
        dq, dk, dv = [jnp.concatenate(p, 0) for p in (dqs, dks, dvs)]
    return dq.astype(BF16), dk.astype(BF16), dv.astype(BF16)


def norm_backward(s, j, g_in, d_packed, gain, wqkv_ref):
    w = wqkv_ref[j]
    d_scaled = sum(nt(d_packed[i], w[:, 192 * i : 192 * i + 192]) for i in range(3))
    normed = s.normed[j]
    d_normed = d_scaled * gain
    d_hidden = s.inverse[j] * (
        d_normed
        - jnp.mean(d_normed, -1, keepdims=True)
        - normed * jnp.mean(d_normed * normed, -1, keepdims=True)
    )
    return (g_in.astype(F32) + d_hidden).astype(BF16), d_scaled


def weight_gradients(s, j, g_in, d_packed, groups):
    n = 144 // groups
    scaled = s.scaled[j]
    for i, part in enumerate(d_packed):
        s.grad[:, 192 * i : 192 * i + 192] = tn(scaled, part)
    d_proj = jnp.zeros((192, 192), F32)
    for g in range(groups):
        d_proj = d_proj + nn(
            s.mixed_t[j, g, :, 0:n].astype(BF16), g_in[g * n : g * n + n]
        )
    s.grad[:, 576:768] = d_proj
    for half in range(2):
        for slot in range(12):
            column, row = half * 384 + (slot // 4) * 128, (slot % 4) * 48
            s.payload[j, half, slot] = s.grad[row : row + 48, column : column + 128].astype(BF16)


def other_gradients(s, j, d_scaled, folded):
    for h in range(HEADS):
        s.extra[24 * h : 24 * h + 24, 0:144] = folded[h % 2][24 * (h // 2) : 24 * (h // 2) + 24]
    s.extra[144:145, 0:192] = jnp.sum(d_scaled * s.normed[j], 0, keepdims=True)
    for half in range(2):
        for slot, row in ((12, 144), (13, 0), (14, 48), (15, 96)):
            s.payload[j, half, slot] = s.extra[
                row : row + 48, 128 * half : 128 * half + 128
            ].astype(BF16)


class Halo:
    def __init__(self, s, which, forward_shift):
        lat, lon = lax.axis_index("lat"), lax.axis_index("lon")
        home_lat, home_lon = runs_at(lat, lon)
        nlat, nlon = lax.axis_size("lat"), lax.axis_size("lon")
        self.s, self.which = s, which
        self.copies, self.partners = [], []
        for quarter in range(4):
            down, right = quarter // 2, quarter % 2
            if forward_shift:
                peer = runs_at(
                    lax.rem(lat + down - 1 + nlat, nlat), lax.rem(lon + right - 1 + nlon, nlon)
                )
            else:
                peer = lax.rem(home_lat + down, nlat), lax.rem(home_lon + right, nlon)
            self.partners.append(peer)
            self.copies.append(
                pltpu.make_async_remote_copy(
                    src_ref=s.halo_out.at[which, quarter],
                    dst_ref=s.halo_in.at[which, 3 - quarter],
                    send_sem=s.halo_send.at[which],
                    recv_sem=s.halo_recv.at[which],
                    device_id=peer,
                    device_id_type=MESH,
                )
            )
        self.all = pltpu.make_async_remote_copy(
            src_ref=s.halo_out.at[which],
            dst_ref=s.halo_in.at[which],
            send_sem=s.halo_send.at[which],
            recv_sem=s.halo_recv.at[which],
            device_id=self.partners[0],
            device_id_type=MESH,
        )

    def start(self, quarters):
        self.s.halo_out[self.which] = quarters.reshape(4, 64, 128)
        for copy in self.copies:
            copy.start()

    def finish(self):
        self.all.wait_recv()
        return self.s.halo_in[self.which].reshape(256, 128)

    def sent(self):
        self.all.wait_send()


def place():
    lat, lon = lax.axis_index("lat"), lax.axis_index("lon")
    line = lax.rem(lon, 8)
    return lat, lon, lat // 2, lax.rem(lat, 2), lon // 8, line // 2, lax.rem(line, 2)


def runs_at(lat, lon):
    return lat, lax.rem(lon + 32, 64)


def sibling():
    lat, lon, y, zh, zl, x, core = place()
    return lat, zl * 8 + x * 2 + 1 - core


def plane_peers():
    lat, lon, y, zh, zl, x, core = place()
    hops = lambda step: min(step, 4 - step)
    steps = [(dx, dy) for dy in range(4) for dx in range(4) if dx or dy]
    out = []
    for dx, dy in sorted(steps, key=lambda step: -hops(step[0]) - hops(step[1])):
        py, px = lax.rem(y + dy, 4), lax.rem(x + dx, 4)
        out.append((dx if dy == 0 else 0, (py * 2 + zh, zl * 8 + px * 2 + core), py * 4 + px))
    return out


def near_peers():
    lat, lon, y, zh, zl, x, core = place()
    quad = (zl // 4) * 4
    return [(lat, (quad + lax.rem(zl + d, 4)) * 8 + x * 2 + core) for d in range(1, 4)]


def at_z(z):
    lat, lon, y, zh, zl, x, core = place()
    z = lax.rem(z, 16)
    return y * 2 + z // 8, lax.rem(z, 8) * 8 + x * 2 + core


def quad_ends():
    lat, lon, y, zh, zl, x, core = place()
    quad, member = zh * 2 + zl // 4, lax.rem(zl, 4)
    low = member == 0
    is_end = low | (member == 3)
    beside, across = quad + jnp.where(low, 3, 1), quad + 2
    sends = [at_z(4 * beside + i) for i in range(4)]
    sends += [at_z(4 * across + jnp.where(low, 2, 0) + i) for i in range(2)]
    takes = [
        at_z(4 * across + jnp.where(member < 2, 3, 0)),
        at_z(4 * (quad + 1)),
        at_z(4 * (quad + 3) + 3),
    ]
    return is_end, sends, takes


def half_peer():
    lat, lon, y, zh, zl, x, core = place()
    return lat, lax.rem(zl + 4, 8) * 8 + x * 2 + core


class Reduce:
    def __init__(self, s, j):
        lat, lon, y, zh, zl, x, core = place()
        self.s, self.j, self.core, self.x = s, j, core, x
        self.own = y * 4 + x
        self.near, self.far, self.half = lax.rem(zl, 4), zh * 2 + zl // 4, zl // 4
        own, table = self.own, 16 + x
        near, far, half = self.near, self.far, self.half
        stages = [[] for _ in range(6)]

        def add(number, src, dst, peer):
            stages[number].append(self.copy(number, src, dst, peer))

        for first, count in ((0, 12), (12, 4)):
            slots = pl.ds(first, count)
            add(0, s.payload.at[j, 1 - core, slots], s.in_core.at[j, slots], sibling())
        for i, (dx, peer, slot) in enumerate(plane_peers()):
            add(1, s.half.at[j, slot], s.in_plane.at[j, i], peer)
            add(4, s.red.at[j, core, own], s.red.at[j, core, own], peer)
            if dx:
                px = lax.rem(x + dx, 4)
                add(1, s.half.at[j, 13 + px], s.in_plane.at[j, 14 + dx], peer)
                add(4, s.red.at[j, core, table], s.red.at[j, core, table], peer)
        for peer in near_peers():
            add(2, s.near.at[j, near], s.near.at[j, near], peer)
        self.is_end, sends, _ = quad_ends()
        for peer in sends:
            add(3, s.far.at[j, far], s.far.at[j, far], peer)
        self.far_tab = self.copy(6, s.far_tab.at[j, half], s.far_tab.at[j, half], half_peer())
        for first, count in ((0, 13), (16, 3)):
            slots = pl.ds(first, count)
            add(5, s.red.at[j, core, slots], s.red.at[j, core, slots], sibling())
        self.stages = stages
        sizes = (
            s.in_core.at[j], s.in_plane.at[j], s.near.at[j, pl.ds(0, 3)], s.far.at[j, pl.ds(0, 3)],
            s.red.at[j, core, pl.ds(0, 18)], s.red.at[j, core, pl.ds(0, 16)],
        )
        self.all = [self.copy(i, size, size, sibling()) for i, size in enumerate(sizes)]

    def copy(self, number, src, dst, peer):
        return pltpu.make_async_remote_copy(
            src_ref=src,
            dst_ref=dst,
            send_sem=self.s.ar_send.at[self.j, number],
            recv_sem=self.s.ar_recv.at[self.j, number],
            device_id=peer,
            device_id_type=MESH,
        )

    def step(self, number):
        s, j, core = self.s, self.j, self.core
        if number > 0:
            self.all[number - 1].wait_recv()
        if number == 4:
            self.far_tab.wait_recv()
        if number == 1:
            for slot in range(16):
                total = s.payload[j, core, slot].astype(F32) + s.in_core[j, slot].astype(F32)
                s.half[j, slot] = total.astype(BF16)
        if number == 2:
            total = s.half[j, self.own].astype(F32)
            for i in range(15):
                total = total + s.in_plane[j, i].astype(F32)
            table = s.half[j, 13 + self.x].astype(F32)
            for i in range(15, 18):
                table = table + s.in_plane[j, i].astype(F32)
            s.near[j, self.near, 0:48] = total.astype(BF16)
            s.near[j, self.near, 48:96] = table.astype(BF16)
        if number == 3:
            total = s.near[j, 0].astype(F32)
            for i in range(1, 4):
                total = total + s.near[j, i].astype(F32)
            s.far[j, self.far] = total[0:48].astype(BF16)
            s.far_tab[j, self.half] = total[48:96].astype(BF16)
        if number == 4:
            total = s.far[j, 0].astype(F32)
            for i in range(1, 4):
                total = total + s.far[j, i].astype(F32)
            s.red[j, core, self.own] = total.astype(BF16)
            table = s.far_tab[j, 0].astype(F32) + s.far_tab[j, 1].astype(F32)
            s.red[j, core, 16 + self.x] = table.astype(BF16)
        if number == 3:
            self.far_tab.start()

            @pl.when(self.is_end)
            def _():
                for copy in self.stages[3]:
                    copy.start()

        elif 0 < number < 6:
            for copy in self.stages[number]:
                copy.start()
        if number == 4:
            self.far_tab.wait_send()
            size = s.in_plane.at[j, pl.ds(0, 6)]

            @pl.when(self.is_end)
            def _():
                self.copy(3, size, size, sibling()).wait_send()

        elif number > 0:
            self.all[number - 1].wait_send()


def signal_partners(halos):
    barrier = pltpu.get_barrier_semaphore()
    partners = halos[0].partners + halos[-1].partners
    is_end, sends, takes = quad_ends()
    partners += [p for _, p, _ in plane_peers()] + near_peers() + [half_peer(), sibling()]
    expected = len(partners) + jnp.where(is_end, len(sends), 0)
    partners += takes
    for partner in partners:
        pl.semaphore_signal(barrier, inc=1, device_id=partner, device_id_type=MESH)
    return barrier, expected


SCRATCH = dict(
    x_in=pltpu.VMEM((6, 12, 2, 192), BF16),
    cot_in=pltpu.VMEM((6, 12, 2, 192), BF16),
    gains=pltpu.VMEM((2, 192), F32),
    wqkv=pltpu.VMEM((2, 192, 576), BF16),
    wproj=pltpu.VMEM((2, 192, 192), BF16),
    tab_in=pltpu.VMEM((2, 6, 23, 1, 144), F32),
    pad=pltpu.SMEM((48,), jnp.int32),
    loads=pltpu.SemaphoreType.DMA((7,)),
    out=pltpu.VMEM((6, 12, 2, 192), BF16),
    dx=pltpu.VMEM((6, 12, 2, 192), BF16),
    stores=pltpu.SemaphoreType.DMA((5,)),
    tab=pltpu.VMEM((6, 24, 144), F32),
    wide=pltpu.VMEM((2, 144, 1024), F32),
    bias1=pltpu.VMEM((144, 864), F32),
    bias2=pltpu.VMEM((2, 72, 432), F32),
    ds=pltpu.VMEM((144, 1024), F32),
    normed=pltpu.VMEM((2, 144, 192), F32),
    inverse=pltpu.VMEM((2, 144, 1), F32),
    scaled=pltpu.VMEM((2, 144, 192), BF16),
    k=pltpu.VMEM((2, 144, 192), F32),
    v=pltpu.VMEM((2, 144, 192), F32),
    qm=pltpu.VMEM((2, 864, 192), BF16),
    backm=pltpu.VMEM((2, 864, 192), BF16),
    probs=pltpu.VMEM((2, 144, 864), F32),
    mixed_t=pltpu.VMEM((2, 2, 192, 144), F32),
    grad=pltpu.VMEM((192, 768), F32),
    extra=pltpu.VMEM((192, 256), F32),
    to_slots=pltpu.VMEM((3, 256, 144), BF16),
    from_slots=pltpu.VMEM((6, 144, 256), BF16),
    halo_out=pltpu.VMEM((4, 4, 64, 128), BF16),
    halo_in=pltpu.VMEM((4, 4, 64, 128), BF16),
    payload=pltpu.VMEM((2, 2, 16, 48, 128), BF16),
    in_core=pltpu.VMEM((2, 16, 48, 128), BF16),
    half=pltpu.VMEM((2, 17, 48, 128), BF16),
    in_plane=pltpu.VMEM((2, 18, 48, 128), BF16),
    near=pltpu.VMEM((2, 4, 96, 128), BF16),
    far=pltpu.VMEM((2, 4, 48, 128), BF16),
    far_tab=pltpu.VMEM((2, 2, 48, 128), BF16),
    red=pltpu.VMEM((2, 2, 20, 48, 128), BF16),
    halo_send=pltpu.SemaphoreType.DMA((4,)),
    halo_recv=pltpu.SemaphoreType.DMA((4,)),
    ar_send=pltpu.SemaphoreType.DMA((2, 7)),
    ar_recv=pltpu.SemaphoreType.DMA((2, 7)),
)


class Names:
    pass


def main_kernel(
    x_ref, cot_ref, gains_ref, wqkv_ref, wproj_ref, tab_ref, pad_ref,
    out_ref, dx_ref, red_ref, *scratch,
):
    s = Names()
    for name, ref in zip(SCRATCH, scratch):
        setattr(s, name, ref)
    lat = lax.axis_index("lat")
    sources = dict(
        x_in=x_ref, tab_in=tab_ref, pad=pad_ref, gains=gains_ref, wqkv=wqkv_ref,
        wproj=wproj_ref, cot_in=cot_ref,
    )
    loads = {
        name: pltpu.make_async_copy(ref, getattr(s, name), s.loads.at[i])
        for i, (name, ref) in enumerate(sources.items())
    }
    for load in loads.values():
        load.start()
    h_first, h_cot, h_out, h_grad = halos = [Halo(s, i, i < 2) for i in range(4)]
    barrier, expected = signal_partners(halos)
    reduce2, reduce1 = Reduce(s, 1), Reduce(s, 0)

    s.tab[...] = jnp.zeros((6, 24, 144), F32)
    s.ds[:, 768:1024] = jnp.zeros((144, 256), F32)
    s.extra[...] = jnp.zeros((192, 256), F32)
    s.half[:, 16] = jnp.zeros((2, 48, 128), BF16)
    s.red[:, :, 19] = jnp.zeros((2, 2, 48, 128), BF16)

    def field(ref):
        return ref[...].astype(F32).reshape(144, 192).astype(BF16)

    def store(number, value, ref):
        copy = pltpu.make_async_copy(value, ref, s.stores.at[number])
        copy.start()
        return copy

    for name in ("x_in", "tab_in", "pad", "gains", "wqkv", "wproj"):
        loads[name].wait()
    gain1, gain2 = s.gains[0:1, :], s.gains[1:2, :]
    x1 = nn(reorder("a", "n"), field(s.x_in))
    expand_first(s, lat)
    attend(s, 0, x1, gain1, s.wqkv, lambda g: s.bias1[...], 1)
    first = pack(project(s, 0, x1, s.wproj, 1), "a")
    pl.semaphore_wait(barrier, expected)
    h_first.start(first)
    loads["cot_in"].wait()
    h_cot.start(pack(field(s.cot_in), "n"))

    expand_second(s, lat)
    for i, slots in enumerate(SLOTS):
        s.to_slots[i] = reorder(slots, "b")
        s.from_slots[i] = reorder("b", slots)
        s.from_slots[3 + i] = reorder("a", slots)
    x2 = unpack(h_first.finish(), "b", [s.from_slots[i] for i in range(3)])
    attend(s, 1, x2, gain2, s.wqkv, lambda g: s.bias2[g], 2)
    g2 = unpack(h_cot.finish(), "b", [s.from_slots[i] for i in range(3)]).astype(BF16)
    head_backs(s, 1, g2, s.wproj, 2)
    d_packed = backward(s, 1, 2)
    dh2, d_scaled = norm_backward(s, 1, g2, d_packed, gain2, s.wqkv)
    h_grad.start(pack(dh2, "b", [s.to_slots[i] for i in range(3)]))
    second = project(s, 1, x2, s.wproj, 2)
    second = pack(second, "b", [s.to_slots[i] for i in range(3)])
    weight_gradients(s, 1, g2, d_packed, 2)
    reduce2.stages[0][0].start()
    other_gradients(s, 1, d_scaled, fold_second(s))
    reduce2.stages[0][1].start()
    h_cot.sent()
    h_first.sent()
    reduce2.step(1)
    g1 = unpack(h_grad.finish(), "a", [s.from_slots[3 + i] for i in range(3)]).astype(BF16)
    h_out.start(second)
    head_backs(s, 0, g1, s.wproj, 1)
    d_packed = backward(s, 0, 1)
    weight_gradients(s, 0, g1, d_packed, 1)
    reduce1.stages[0][0].start()
    dx, d_scaled = norm_backward(s, 0, g1, d_packed, gain1, s.wqkv)
    other_gradients(s, 0, d_scaled, fold_first(s))
    reduce1.stages[0][1].start()
    reduce1.step(1)
    reduce2.step(2)
    s.dx[...] = nn(reorder("n", "a"), dx).reshape(6, 12, 2, 192).astype(BF16)
    stores = [store(0, s.dx, dx_ref)]
    h_grad.sent()
    reduce2.step(3)
    s.out[...] = unpack(h_out.finish(), "n").reshape(6, 12, 2, 192).astype(BF16)
    stores.append(store(1, s.out, out_ref))
    h_out.sent()
    reduce1.step(2)
    reduce1.step(3)
    reduce2.step(4)
    reduce1.step(4)
    reduce2.step(5)
    reduce2.step(6)
    stores.append(store(2, s.red.at[1], red_ref.at[1]))
    reduce1.step(5)
    core = reduce1.core
    stores.append(store(3, s.red.at[0, core], red_ref.at[0, core]))
    reduce1.step(6)
    stores.append(store(4, s.red.at[0, 1 - core], red_ref.at[0, 1 - core]))
    for copy in stores:
        copy.wait()


def finish_kernel(
    red_ref, o_ref, d_ref, out_ref, dx_ref, gains_ref, dqkv_ref, dproj_ref, dtab_ref, red, sems
):
    copies = [
        pltpu.make_async_copy(source, target, sems.at[i])
        for i, (source, target) in enumerate(
            ((red_ref.at[1], red.at[1]), (red_ref.at[0], red.at[0]), (o_ref, out_ref), (d_ref, dx_ref))
        )
    ]
    for copy in copies:
        copy.start()
    for j in (1, 0):
        copies[1 - j].wait()
        for half in range(2):
            for slot in range(12):
                column, row = half * 3 + slot // 4, (slot % 4) * 48
                rows = slice(row, row + 48)
                value = red[j, half, slot].astype(F32)
                if column < 4:
                    dqkv_ref[j, rows, 128 * column : 128 * column + 128] = value
                elif column == 4:
                    dqkv_ref[j, rows, 512:576] = value[:, 0:64]
                    dproj_ref[j, rows, 0:64] = value[:, 64:128]
                else:
                    dproj_ref[j, rows, 64:192] = value
            width = 128 if half == 0 else 16
            lanes = slice(128 * half, 128 * half + width)
            for third in range(3):
                value = red[j, half, 16 + third].astype(F32)
                for i in range(2):
                    dtab_ref[j, 2 * third + i, :, 0, lanes] = value[24 * i : 24 * i + 23, 0:width]
        gains_ref[j : j + 1, 0:128] = red[j, 0, 12].astype(F32)[0:1]
        gains_ref[j : j + 1, 128:192] = red[j, 1, 12].astype(F32)[0:1, 0:64]
    for copy in copies[2:]:
        copy.wait()


def body(inputs, cotangent, gains, qkv_weights, proj_weights, bias_tables, pad_rows):
    vmem = pl.BlockSpec(memory_space=pltpu.VMEM)
    hbm = pl.BlockSpec(memory_space=pltpu.HBM)
    field = jax.ShapeDtypeStruct((6, 12, 2, 192), BF16)
    out, dx, red = pl.pallas_call(
        main_kernel,
        out_shape=(field, field, jax.ShapeDtypeStruct((2, 2, 20, 48, 128), BF16)),
        in_specs=[hbm] * 7,
        out_specs=(hbm,) * 3,
        scratch_shapes=list(SCRATCH.values()),
        compiler_params=pltpu.CompilerParams(
            collective_id=0, has_side_effects=True, vmem_limit_bytes=VMEM_LIMIT
        ),
        name="both_blocks",
    )(
        inputs.transpose(1, 2, 0, 3),
        cotangent.transpose(1, 2, 0, 3),
        gains,
        qkv_weights,
        proj_weights,
        bias_tables.transpose(0, 2, 3, 1, 4),
        pad_rows,
    )
    out, dx, d_gains, d_qkv, d_proj, d_tables = pl.pallas_call(
        finish_kernel,
        out_shape=(
            field,
            field,
            jax.ShapeDtypeStruct((2, 192), F32),
            jax.ShapeDtypeStruct((2, 192, 576), F32),
            jax.ShapeDtypeStruct((2, 192, 192), F32),
            jax.ShapeDtypeStruct((2, 6, 23, 1, 144), F32),
        ),
        in_specs=[hbm] * 3,
        out_specs=(vmem,) * 6,
        scratch_shapes=[
            pltpu.VMEM((2, 2, 20, 48, 128), BF16),
            pltpu.SemaphoreType.DMA((4,)),
        ],
        compiler_params=pltpu.CompilerParams(vmem_limit_bytes=VMEM_LIMIT),
        name="unpack",
    )(red, out, dx)
    return (
        out.transpose(2, 0, 1, 3),
        dx.transpose(2, 0, 1, 3),
        d_gains,
        d_qkv,
        d_proj,
        d_tables.transpose(0, 3, 1, 2, 4),
    )


def solution(mesh):
    field = P(None, "lat", "lon", None)
    tables = P(None, "lat", None, None, None)
    return jax.shard_map(
        body,
        mesh=mesh,
        in_specs=(field, field, P(), P(), P(), tables, P()),
        out_specs=(field, field, P(), P(), P(), tables),
        check_vma=False,
    )
```

```python
import jax
import jax.numpy as jnp
from jax import lax
from jax.experimental import pallas as pl
from jax.experimental.pallas import tpu as pltpu
from jax.sharding import PartitionSpec as P

F32 = jnp.float32
BF16 = jnp.bfloat16
MESH = pl.DeviceIdType.MESH
HEADS = 6
VMEM_LIMIT = 62 * 2**20
SCALE = 32 ** (-0.5)


def div(x, d):
    return (x * (-(-(2**20) // d))) >> 20


def tokens_of(order, n):
    i = lax.broadcasted_iota(jnp.int32, (n, 1), 0)
    used = i < n
    if order == "n":
        r = div(i, 24)
        c = div(i - 24 * r, 2)
        l = i - 24 * r - 2 * c
    elif order == "a":
        c = div(i, 12)
        l = div(i - 12 * c, 6)
        r = i - 12 * c - 6 * l
    elif order == "b":
        l = div(i, 72)
        c = div(i - 72 * l, 6)
        r = i - 72 * l - 6 * c
    else:
        q = i >> 6
        inner = i - 64 * q
        used = inner < 36
        if order == "s1":
            inner, used = inner - 36, (inner >= 36) & (inner < 54)
        if order == "s2":
            inner, used = inner - 18, (inner >= 36) & (inner < 54)
        l = div(inner, 18)
        r = div(inner - 18 * l, 6)
        c = inner - 18 * l - 6 * r
        r, c = r + 3 * (q >> 1), c + 6 * (q & 1)
    return l, r, c, used


def place_in(order, l, r, c):
    if order == "n":
        return 24 * r + 2 * c + l
    if order == "a":
        return 12 * c + 6 * l + r
    if order == "b":
        return 72 * l + 6 * c + r
    lower, right = (r >= 3).astype(jnp.int32), (c >= 6).astype(jnp.int32)
    quarter = 64 * (2 * lower + right)
    inner = 18 * l + 6 * (r - 3 * lower) + c - 6 * right
    if order == "s":
        return quarter + inner
    if order == "s1":
        return jnp.where(inner < 18, quarter + 36 + inner, -1)
    return jnp.where(inner >= 18, quarter + 18 + inner, -1)


SLOTS = ("s", "s1", "s2")


def reorder(to, of):
    n, m = [256 if order[0] == "s" else 144 for order in (to, of)]
    l, r, c, used = tokens_of(to, n)
    place = jnp.where(used, place_in(of, l, r, c), -1)
    return jnp.where(place == lax.broadcasted_iota(jnp.int32, (n, m), 1), 1.0, 0.0).astype(BF16)


def pack(x, order, ready=None):
    wide, rest = x[:, 0:128], x[:, 128:192]
    whole, first, second = ready or [reorder(to, order) for to in SLOTS]
    pairs = jnp.concatenate([nn(first, rest), nn(second, rest)], 1)
    return (nn(whole, wide) + pairs).astype(BF16)


def unpack(x, order, ready=None):
    whole, first, second = ready or [reorder(order, of) for of in SLOTS]
    rest = nn(first, x)[:, 0:64] + nn(second, x)[:, 64:128]
    return jnp.concatenate([nn(whole, x), rest], 1)


def spread(lanes, step, par, parts):
    i = lax.broadcasted_iota(jnp.int32, (72 * parts, 1), 0)
    part = div(i, 72)
    h = div(i - 72 * part, 24)
    o = i - 72 * part - 24 * h
    start = 12 * step * par + 24 * step * h + (22 - o) * step
    at = lax.broadcasted_iota(jnp.int32, (72 * parts, lanes), 1) - start
    return jnp.where((at >= 0) & (at < step), 1.0, 0.0).astype(BF16)


def lane_info(lanes, step):
    lane = lax.broadcasted_iota(jnp.int32, (1, lanes), 1)
    head = div(lane, 12 * step)
    parity = jnp.where(head < HEADS, head & 1, 2)
    return lane - step * div(lane, step), lane - 12 * step * head, parity


def nn(a, b):
    return lax.dot_general(a, b, (((1,), (0,)), ((), ())), preferred_element_type=F32)


def nt(a, b):
    return lax.dot_general(a, b, (((1,), (1,)), ((), ())), preferred_element_type=F32)


def tn(a, b):
    return lax.dot_general(a, b, (((0,), (0,)), ((), ())), preferred_element_type=F32)


def head_stack(x):
    lane = lax.broadcasted_iota(jnp.int32, (1, 192), 1)
    parts = [jnp.where((lane >= 32 * h) & (lane < 32 * h + 32), x, 0.0) for h in range(HEADS)]
    return jnp.concatenate(parts, 0).astype(BF16)


def head_diagonal(x, n):
    return jnp.concatenate(
        [x[32 * h : 32 * h + 32, n * h : n * h + n] for h in range(HEADS)], 0
    )


def split_table(s, block):
    out = []
    for h in range(HEADS):
        s.tab[h, 0:23, :] = s.tab_in[block, h, :, 0, :]
    for par in range(2):
        parts = [[], [], []]
        for h in range(3):
            t = s.tab[2 * h + par]
            hi = t.astype(BF16).astype(F32)
            rest = t - hi
            mid = rest.astype(BF16).astype(F32)
            for part, value in zip(parts, (hi, mid, rest - mid)):
                part.append(value)
        out.append(jnp.concatenate(sum(parts, []), 0).astype(BF16))
    return out


def row_flags(s, start):
    rows = lax.broadcasted_iota(jnp.int32, (6, 1), 0)
    flags = jnp.zeros((6, 1), jnp.int32)
    for r in range(6):
        flags = jnp.where(rows == r, s.pad[lax.rem(start + r, 48)], flags)
    return rows, flags == 1


def expand_first(s, lat):
    for par, parts in enumerate(split_table(s, 0)):
        s.wide[par] = tn(parts, spread(1024, 12, par, 3))
    entry, token, parity = lane_info(1024, 12)
    token, odd = token[:, 0:864], parity[:, 0:864] == 1
    rows, valid = row_flags(s, 6 * lat)
    for lk in range(2):
        strips = []
        for par in range(2):
            strip = jnp.zeros((6, 1024), F32)
            for e in range(12):
                at = 72 * (e // 6) + 36 * lk + 6 * (e % 6)
                strip = jnp.where(entry == e, s.wide[par, at : at + 6, :], strip)
            strips.append(strip)
        for ck in range(12):
            turn = (1024 - (11 - ck) * 12) % 1024
            even_part, odd_part = [
                (pltpu.roll(x, turn, 1) if turn else x)[:, 0:864] for x in strips
            ]
            at = 12 * ck + 6 * lk
            keep = valid | (token == rows + at)
            s.bias1[at : at + 6, :] = jnp.where(
                keep, jnp.where(odd, odd_part, even_part), -1e30
            )


def expand_second(s, lat):
    for par, parts in enumerate(split_table(s, 1)):
        s.wide[par, :, 0:512] = tn(parts, spread(512, 6, par, 3))
    entry, token, parity = lane_info(512, 6)
    token, odd = token[:, 0:432], parity[:, 0:432] == 1
    rows, valid = row_flags(s, 6 * lat + 3)
    q_band = jnp.where(lat == 7, (entry[:, 0:432] >= 3).astype(jnp.int32), 0)
    k_band = jnp.where(lat == 7, (rows >= 3).astype(jnp.int32), 0)
    same = q_band == k_band
    for lev in range(2):
        strips = []
        for par in range(2):
            strip = jnp.zeros((6, 512), F32)
            for e in range(6):
                at = 108 * (1 - lev) + 6 * e
                strip = jnp.where(entry == e, s.wide[par, at : at + 6, 0:512], strip)
            strips.append(strip)
        for ck in range(12):
            turn = (512 - (11 - ck) * 6) % 512
            even_part, odd_part = [
                (pltpu.roll(x, turn, 1) if turn else x)[:, 0:432] for x in strips
            ]
            at = 6 * ck
            keep = (valid | (token == rows + at)) & same
            s.bias2[lev, at : at + 6, :] = jnp.where(
                keep, jnp.where(odd, odd_part, even_part), -1e30
            )


def fold_first(s):
    entry, _, parity = lane_info(1024, 12)
    for par in range(2):
        mine = parity == par
        for lk in range(2):
            acc = jnp.zeros((6, 1024), F32)
            for ck in range(12):
                at = 12 * ck + 6 * lk
                piece = jnp.where(mine, s.ds[at : at + 6, :], 0.0)
                turn = (11 - ck) * 12
                acc = acc + (pltpu.roll(piece, turn, 1) if turn else piece)
            for e in range(12):
                at = 72 * (e // 6) + 36 * lk + 6 * (e % 6)
                s.wide[par, at : at + 6, :] = jnp.where(entry == e, acc, 0.0)
    return [nt(spread(1024, 12, par, 1), s.wide[par].astype(BF16)) for par in range(2)]


def fold_second(s):
    entry, _, parity = lane_info(512, 6)
    s.wide[:, :, 0:512] = jnp.zeros((2, 144, 512), F32)
    for par in range(2):
        mine = parity == par
        for lev in range(2):
            acc = jnp.zeros((6, 512), F32)
            for ck in range(12):
                at = 72 * lev + 6 * ck
                piece = jnp.where(mine, s.ds[at : at + 6, 0:512], 0.0)
                turn = (11 - ck) * 6
                acc = acc + (pltpu.roll(piece, turn, 1) if turn else piece)
            for e in range(6):
                at = 108 * (1 - lev) + 6 * e
                s.wide[par, at : at + 6, 0:512] = jnp.where(entry == e, acc, 0.0)
    return [nt(spread(512, 6, par, 1), s.wide[par, :, 0:512].astype(BF16)) for par in range(2)]


def attend(s, j, x, gain, wqkv_ref, bias, groups):
    n = 144 // groups
    center = x - jnp.mean(x, -1, keepdims=True)
    inverse = lax.rsqrt(jnp.mean(center * center, -1, keepdims=True) + 1e-05)
    normed = center * inverse
    scaled = (normed * gain).astype(BF16)
    packed = nn(scaled, wqkv_ref[j])
    q, k, v = packed[:, 0:192], packed[:, 192:384], packed[:, 384:576]
    s.normed[j] = normed
    s.inverse[j] = inverse
    s.scaled[j] = scaled
    s.k[j] = k
    s.v[j] = v
    for g in range(groups):
        rows = slice(g * n, g * n + n)
        qm = head_stack(q[rows])
        s.qm[j, g * 6 * n : (g + 1) * 6 * n, :] = qm
        scores = nt(k[rows].astype(BF16), qm) * SCALE + bias(g)
        weight = jnp.exp(scores - jnp.max(scores, 0, keepdims=True))
        probs = weight * (1.0 / jnp.sum(weight, 0, keepdims=True))
        s.probs[j, rows, 0 : 6 * n] = probs


def project(s, j, x, wproj_ref, groups):
    n = 144 // groups
    attended = []
    for g in range(groups):
        rows = slice(g * n, g * n + n)
        v, probs = s.v[j, rows, :], s.probs[j, rows, 0 : 6 * n]
        mixed_t = head_diagonal(tn(v.astype(BF16), probs.astype(BF16)), n)
        s.mixed_t[j, g, :, 0:n] = mixed_t
        attended.append(tn(mixed_t.astype(BF16), wproj_ref[j]))
    att = attended[0] if groups == 1 else jnp.concatenate(attended, 0)
    return (x + att).astype(BF16)


def head_backs(s, j, g_in, wproj_ref, groups):
    n = 144 // groups
    back = nt(g_in, wproj_ref[j])
    for g in range(groups):
        s.backm[j, g * 6 * n : (g + 1) * 6 * n, :] = head_stack(back[g * n : g * n + n])


def backward(s, j, groups):
    n = 144 // groups
    dqs, dks, dvs = [], [], []
    for g in range(groups):
        rows = slice(g * n, g * n + n)
        backm = s.backm[j, g * 6 * n : (g + 1) * 6 * n, :]
        probs = s.probs[j, rows, 0 : 6 * n]
        k = s.k[j, rows, :].astype(BF16)
        v = s.v[j, rows, :].astype(BF16)
        qm = s.qm[j, g * 6 * n : (g + 1) * 6 * n, :]
        d_probs = nt(v, backm)
        dvs.append(nn(probs.astype(BF16), backm))
        d_scores = probs * (d_probs - jnp.sum(d_probs * probs, 0, keepdims=True))
        s.ds[rows, 0 : 6 * n] = d_scores
        d_rounded = (d_scores * SCALE).astype(BF16)
        dks.append(nn(d_rounded, qm))
        dqs.append(head_diagonal(tn(k, d_rounded), n).T)
    if groups == 1:
        dq, dk, dv = dqs[0], dks[0], dvs[0]
    else:
        dq, dk, dv = [jnp.concatenate(p, 0) for p in (dqs, dks, dvs)]
    return dq.astype(BF16), dk.astype(BF16), dv.astype(BF16)


def norm_backward(s, j, g_in, d_packed, gain, wqkv_ref):
    w = wqkv_ref[j]
    d_scaled = sum(nt(d_packed[i], w[:, 192 * i : 192 * i + 192]) for i in range(3))
    normed = s.normed[j]
    d_normed = d_scaled * gain
    d_hidden = s.inverse[j] * (
        d_normed
        - jnp.mean(d_normed, -1, keepdims=True)
        - normed * jnp.mean(d_normed * normed, -1, keepdims=True)
    )
    return (g_in.astype(F32) + d_hidden).astype(BF16), d_scaled


def weight_gradients(s, j, g_in, d_packed, groups):
    n = 144 // groups
    scaled = s.scaled[j]
    for i, part in enumerate(d_packed):
        s.grad[:, 192 * i : 192 * i + 192] = tn(scaled, part)
    d_proj = jnp.zeros((192, 192), F32)
    for g in range(groups):
        d_proj = d_proj + nn(
            s.mixed_t[j, g, :, 0:n].astype(BF16), g_in[g * n : g * n + n]
        )
    s.grad[:, 576:768] = d_proj
    for half in range(2):
        for slot in range(12):
            column, row = half * 384 + (slot // 4) * 128, (slot % 4) * 48
            s.payload[j, half, slot] = s.grad[row : row + 48, column : column + 128].astype(BF16)


def other_gradients(s, j, d_scaled, folded):
    for h in range(HEADS):
        s.extra[24 * h : 24 * h + 24, 0:144] = folded[h % 2][24 * (h // 2) : 24 * (h // 2) + 24]
    s.extra[144:145, 0:192] = jnp.sum(d_scaled * s.normed[j], 0, keepdims=True)
    for half in range(2):
        for slot, row in ((12, 144), (13, 0), (14, 48), (15, 96)):
            s.payload[j, half, slot] = s.extra[
                row : row + 48, 128 * half : 128 * half + 128
            ].astype(BF16)


class Halo:
    def __init__(self, s, which, forward_shift):
        lat, lon = lax.axis_index("lat"), lax.axis_index("lon")
        home_lat, home_lon = runs_at(lat, lon)
        nlat, nlon = lax.axis_size("lat"), lax.axis_size("lon")
        self.s, self.which = s, which
        self.copies, self.partners = [], []
        for quarter in range(4):
            down, right = quarter // 2, quarter % 2
            if forward_shift:
                peer = runs_at(
                    lax.rem(lat + down - 1 + nlat, nlat), lax.rem(lon + right - 1 + nlon, nlon)
                )
            else:
                peer = lax.rem(home_lat + down, nlat), lax.rem(home_lon + right, nlon)
            self.partners.append(peer)
            self.copies.append(
                pltpu.make_async_remote_copy(
                    src_ref=s.halo_out.at[which, quarter],
                    dst_ref=s.halo_in.at[which, 3 - quarter],
                    send_sem=s.halo_send.at[which],
                    recv_sem=s.halo_recv.at[which],
                    device_id=peer,
                    device_id_type=MESH,
                )
            )
        self.all = pltpu.make_async_remote_copy(
            src_ref=s.halo_out.at[which],
            dst_ref=s.halo_in.at[which],
            send_sem=s.halo_send.at[which],
            recv_sem=s.halo_recv.at[which],
            device_id=self.partners[0],
            device_id_type=MESH,
        )

    def start(self, quarters):
        self.s.halo_out[self.which] = quarters.reshape(4, 64, 128)
        for copy in self.copies:
            copy.start()

    def finish(self):
        self.all.wait_recv()
        return self.s.halo_in[self.which].reshape(256, 128)

    def sent(self):
        self.all.wait_send()


def place():
    lat, lon = lax.axis_index("lat"), lax.axis_index("lon")
    line = lax.rem(lon, 8)
    return lat, lon, lat // 2, lax.rem(lat, 2), lon // 8, line // 2, lax.rem(line, 2)


def runs_at(lat, lon):
    return lat, lax.rem(lon + 32, 64)


def sibling():
    lat, lon, y, zh, zl, x, core = place()
    return lat, zl * 8 + x * 2 + 1 - core


def plane_peers():
    lat, lon, y, zh, zl, x, core = place()
    hops = lambda step: min(step, 4 - step)
    steps = [(dx, dy) for dy in range(4) for dx in range(4) if dx or dy]
    out = []
    for dx, dy in sorted(steps, key=lambda step: -hops(step[0]) - hops(step[1])):
        py, px = lax.rem(y + dy, 4), lax.rem(x + dx, 4)
        out.append((dx if dy == 0 else 0, (py * 2 + zh, zl * 8 + px * 2 + core), py * 4 + px))
    return out


def near_peers():
    lat, lon, y, zh, zl, x, core = place()
    quad = (zl // 4) * 4
    return [(lat, (quad + lax.rem(zl + d, 4)) * 8 + x * 2 + core) for d in range(1, 4)]


def at_z(z):
    lat, lon, y, zh, zl, x, core = place()
    z = lax.rem(z, 16)
    return y * 2 + z // 8, lax.rem(z, 8) * 8 + x * 2 + core


def quad_ends():
    lat, lon, y, zh, zl, x, core = place()
    quad, member = zh * 2 + zl // 4, lax.rem(zl, 4)
    low = member == 0
    is_end = low | (member == 3)
    beside, across = quad + jnp.where(low, 3, 1), quad + 2
    sends = [at_z(4 * beside + i) for i in range(4)]
    sends += [at_z(4 * across + jnp.where(low, 2, 0) + i) for i in range(2)]
    takes = [
        at_z(4 * across + jnp.where(member < 2, 3, 0)),
        at_z(4 * (quad + 1)),
        at_z(4 * (quad + 3) + 3),
    ]
    return is_end, sends, takes


def half_peer():
    lat, lon, y, zh, zl, x, core = place()
    return lat, lax.rem(zl + 4, 8) * 8 + x * 2 + core


class Reduce:
    def __init__(self, s, j):
        lat, lon, y, zh, zl, x, core = place()
        self.s, self.j, self.core, self.x = s, j, core, x
        self.own = y * 4 + x
        self.near, self.far, self.half = lax.rem(zl, 4), zh * 2 + zl // 4, zl // 4
        own, table = self.own, 16 + x
        near, far, half = self.near, self.far, self.half
        stages = [[] for _ in range(6)]
        self.weight_sends, self.table_sends = [], []

        def add(number, src, dst, peer):
            stages[number].append(self.copy(number, src, dst, peer))

        for first, count in ((0, 12), (12, 4)):
            slots = pl.ds(first, count)
            add(0, s.payload.at[j, 1 - core, slots], s.in_core.at[j, slots], sibling())
        for i, (dx, peer, slot) in enumerate(plane_peers()):
            add(1, s.half.at[j, slot], s.in_plane.at[j, i], peer)
            self.weight_sends.append((slot, stages[1][-1]))
            add(4, s.red.at[j, core, own], s.red.at[j, core, own], peer)
            if dx:
                px = lax.rem(x + dx, 4)
                add(1, s.half.at[j, 13 + px], s.in_plane.at[j, 14 + dx], peer)
                self.table_sends.append(stages[1][-1])
                add(4, s.red.at[j, core, table], s.red.at[j, core, table], peer)
        for peer in near_peers():
            add(2, s.near.at[j, near], s.near.at[j, near], peer)
        self.is_end, sends, _ = quad_ends()
        for peer in sends:
            add(3, s.far.at[j, far], s.far.at[j, far], peer)
        self.far_tab = self.copy(6, s.far_tab.at[j, half], s.far_tab.at[j, half], half_peer())
        for first, count in ((0, 13), (16, 3)):
            slots = pl.ds(first, count)
            add(5, s.red.at[j, core, slots], s.red.at[j, core, slots], sibling())
        self.stages = stages
        sizes = (
            s.in_core.at[j], s.in_plane.at[j], s.near.at[j, pl.ds(0, 3)], s.far.at[j, pl.ds(0, 3)],
            s.red.at[j, core, pl.ds(0, 18)], s.red.at[j, core, pl.ds(0, 16)],
        )
        self.all = [self.copy(i, size, size, sibling()) for i, size in enumerate(sizes)]

    def copy(self, number, src, dst, peer):
        return pltpu.make_async_remote_copy(
            src_ref=src,
            dst_ref=dst,
            send_sem=self.s.ar_send.at[self.j, number],
            recv_sem=self.s.ar_recv.at[self.j, number],
            device_id=peer,
            device_id_type=MESH,
        )

    def step(self, number):
        s, j, core = self.s, self.j, self.core
        if number > 0:
            self.all[number - 1].wait_recv()
        if number == 4:
            self.far_tab.wait_recv()
        if number == 1:
            for slot, copy in [(self.own, None)] + self.weight_sends:
                total = s.payload[j, core, slot].astype(F32) + s.in_core[j, slot].astype(F32)
                s.half[j, slot] = total.astype(BF16)
                if copy is not None:
                    copy.start()
            for copy in self.table_sends:
                copy.start()
        if number == 2:
            total = s.half[j, self.own].astype(F32)
            for i in range(15):
                total = total + s.in_plane[j, i].astype(F32)
            table = s.half[j, 13 + self.x].astype(F32)
            for i in range(15, 18):
                table = table + s.in_plane[j, i].astype(F32)
            s.near[j, self.near, 0:48] = total.astype(BF16)
            s.near[j, self.near, 48:96] = table.astype(BF16)
        if number == 3:
            total = s.near[j, 0].astype(F32)
            for i in range(1, 4):
                total = total + s.near[j, i].astype(F32)
            s.far[j, self.far] = total[0:48].astype(BF16)
            s.far_tab[j, self.half] = total[48:96].astype(BF16)
        if number == 4:
            total = s.far[j, 0].astype(F32)
            for i in range(1, 4):
                total = total + s.far[j, i].astype(F32)
            s.red[j, core, self.own] = total.astype(BF16)
            table = s.far_tab[j, 0].astype(F32) + s.far_tab[j, 1].astype(F32)
            s.red[j, core, 16 + self.x] = table.astype(BF16)
        if number == 3:
            self.far_tab.start()

            @pl.when(self.is_end)
            def _():
                for copy in self.stages[3]:
                    copy.start()

        elif 1 < number < 6:
            for copy in self.stages[number]:
                copy.start()
        if number == 4:
            self.far_tab.wait_send()
            size = s.in_plane.at[j, pl.ds(0, 6)]

            @pl.when(self.is_end)
            def _():
                self.copy(3, size, size, sibling()).wait_send()

        elif number > 0:
            self.all[number - 1].wait_send()


def signal_partners(halos):
    barrier = pltpu.get_barrier_semaphore()
    partners = halos[0].partners + halos[-1].partners
    is_end, sends, takes = quad_ends()
    partners += [p for _, p, _ in plane_peers()] + near_peers() + [half_peer(), sibling()]
    expected = len(partners) + jnp.where(is_end, len(sends), 0)
    partners += takes
    for partner in partners:
        pl.semaphore_signal(barrier, inc=1, device_id=partner, device_id_type=MESH)
    return barrier, expected


SCRATCH = dict(
    x_in=pltpu.VMEM((6, 12, 2, 192), BF16),
    cot_in=pltpu.VMEM((6, 12, 2, 192), BF16),
    gains=pltpu.VMEM((2, 192), F32),
    wqkv=pltpu.VMEM((2, 192, 576), BF16),
    wproj=pltpu.VMEM((2, 192, 192), BF16),
    tab_in=pltpu.VMEM((2, 6, 23, 1, 144), F32),
    pad=pltpu.SMEM((48,), jnp.int32),
    loads=pltpu.SemaphoreType.DMA((7,)),
    out=pltpu.VMEM((6, 12, 2, 192), BF16),
    dx=pltpu.VMEM((6, 12, 2, 192), BF16),
    stores=pltpu.SemaphoreType.DMA((5,)),
    tab=pltpu.VMEM((6, 24, 144), F32),
    wide=pltpu.VMEM((2, 144, 1024), F32),
    bias1=pltpu.VMEM((144, 864), F32),
    bias2=pltpu.VMEM((2, 72, 432), F32),
    ds=pltpu.VMEM((144, 1024), F32),
    normed=pltpu.VMEM((2, 144, 192), F32),
    inverse=pltpu.VMEM((2, 144, 1), F32),
    scaled=pltpu.VMEM((2, 144, 192), BF16),
    k=pltpu.VMEM((2, 144, 192), F32),
    v=pltpu.VMEM((2, 144, 192), F32),
    qm=pltpu.VMEM((2, 864, 192), BF16),
    backm=pltpu.VMEM((2, 864, 192), BF16),
    probs=pltpu.VMEM((2, 144, 864), F32),
    mixed_t=pltpu.VMEM((2, 2, 192, 144), F32),
    grad=pltpu.VMEM((192, 768), F32),
    extra=pltpu.VMEM((192, 256), F32),
    to_slots=pltpu.VMEM((3, 256, 144), BF16),
    from_slots=pltpu.VMEM((6, 144, 256), BF16),
    halo_out=pltpu.VMEM((4, 4, 64, 128), BF16),
    halo_in=pltpu.VMEM((4, 4, 64, 128), BF16),
    payload=pltpu.VMEM((2, 2, 16, 48, 128), BF16),
    in_core=pltpu.VMEM((2, 16, 48, 128), BF16),
    half=pltpu.VMEM((2, 17, 48, 128), BF16),
    in_plane=pltpu.VMEM((2, 18, 48, 128), BF16),
    near=pltpu.VMEM((2, 4, 96, 128), BF16),
    far=pltpu.VMEM((2, 4, 48, 128), BF16),
    far_tab=pltpu.VMEM((2, 2, 48, 128), BF16),
    red=pltpu.VMEM((2, 2, 20, 48, 128), BF16),
    halo_send=pltpu.SemaphoreType.DMA((4,)),
    halo_recv=pltpu.SemaphoreType.DMA((4,)),
    ar_send=pltpu.SemaphoreType.DMA((2, 7)),
    ar_recv=pltpu.SemaphoreType.DMA((2, 7)),
)


class Names:
    pass


def main_kernel(
    x_ref, cot_ref, gains_ref, wqkv_ref, wproj_ref, tab_ref, pad_ref,
    out_ref, dx_ref, red_ref, *scratch,
):
    s = Names()
    for name, ref in zip(SCRATCH, scratch):
        setattr(s, name, ref)
    lat = lax.axis_index("lat")
    sources = dict(
        x_in=x_ref, tab_in=tab_ref, pad=pad_ref, gains=gains_ref, wqkv=wqkv_ref,
        wproj=wproj_ref, cot_in=cot_ref,
    )
    loads = {
        name: pltpu.make_async_copy(ref, getattr(s, name), s.loads.at[i])
        for i, (name, ref) in enumerate(sources.items())
    }
    for load in loads.values():
        load.start()
    h_first, h_cot, h_out, h_grad = halos = [Halo(s, i, i < 2) for i in range(4)]
    barrier, expected = signal_partners(halos)
    reduce2, reduce1 = Reduce(s, 1), Reduce(s, 0)

    s.tab[...] = jnp.zeros((6, 24, 144), F32)
    s.ds[:, 768:1024] = jnp.zeros((144, 256), F32)
    s.extra[...] = jnp.zeros((192, 256), F32)
    s.half[:, 16] = jnp.zeros((2, 48, 128), BF16)
    s.red[:, :, 19] = jnp.zeros((2, 2, 48, 128), BF16)

    def field(ref):
        return ref[...].astype(F32).reshape(144, 192).astype(BF16)

    def store(number, value, ref):
        copy = pltpu.make_async_copy(value, ref, s.stores.at[number])
        copy.start()
        return copy

    for name in ("x_in", "tab_in", "pad", "gains", "wqkv", "wproj"):
        loads[name].wait()
    gain1, gain2 = s.gains[0:1, :], s.gains[1:2, :]
    x1 = nn(reorder("a", "n"), field(s.x_in))
    expand_first(s, lat)
    attend(s, 0, x1, gain1, s.wqkv, lambda g: s.bias1[...], 1)
    first = pack(project(s, 0, x1, s.wproj, 1), "a")
    pl.semaphore_wait(barrier, expected)
    h_first.start(first)
    loads["cot_in"].wait()
    h_cot.start(pack(field(s.cot_in), "n"))

    expand_second(s, lat)
    for i, slots in enumerate(SLOTS):
        s.to_slots[i] = reorder(slots, "b")
        s.from_slots[i] = reorder("b", slots)
        s.from_slots[3 + i] = reorder("a", slots)
    x2 = unpack(h_first.finish(), "b", [s.from_slots[i] for i in range(3)])
    attend(s, 1, x2, gain2, s.wqkv, lambda g: s.bias2[g], 2)
    g2 = unpack(h_cot.finish(), "b", [s.from_slots[i] for i in range(3)]).astype(BF16)
    head_backs(s, 1, g2, s.wproj, 2)
    d_packed = backward(s, 1, 2)
    dh2, d_scaled = norm_backward(s, 1, g2, d_packed, gain2, s.wqkv)
    h_grad.start(pack(dh2, "b", [s.to_slots[i] for i in range(3)]))
    second = project(s, 1, x2, s.wproj, 2)
    second = pack(second, "b", [s.to_slots[i] for i in range(3)])
    weight_gradients(s, 1, g2, d_packed, 2)
    reduce2.stages[0][0].start()
    other_gradients(s, 1, d_scaled, fold_second(s))
    reduce2.stages[0][1].start()
    h_cot.sent()
    h_first.sent()
    reduce2.step(1)
    g1 = unpack(h_grad.finish(), "a", [s.from_slots[3 + i] for i in range(3)]).astype(BF16)
    h_out.start(second)
    head_backs(s, 0, g1, s.wproj, 1)
    d_packed = backward(s, 0, 1)
    weight_gradients(s, 0, g1, d_packed, 1)
    reduce1.stages[0][0].start()
    dx, d_scaled = norm_backward(s, 0, g1, d_packed, gain1, s.wqkv)
    other_gradients(s, 0, d_scaled, fold_first(s))
    reduce1.stages[0][1].start()
    reduce1.step(1)
    reduce2.step(2)
    s.dx[...] = nn(reorder("n", "a"), dx).reshape(6, 12, 2, 192).astype(BF16)
    stores = [store(0, s.dx, dx_ref)]
    h_grad.sent()
    reduce2.step(3)
    s.out[...] = unpack(h_out.finish(), "n").reshape(6, 12, 2, 192).astype(BF16)
    stores.append(store(1, s.out, out_ref))
    h_out.sent()
    reduce1.step(2)
    reduce1.step(3)
    reduce2.step(4)
    reduce1.step(4)
    reduce2.step(5)
    reduce2.step(6)
    stores.append(store(2, s.red.at[1], red_ref.at[1]))
    reduce1.step(5)
    core = reduce1.core
    stores.append(store(3, s.red.at[0, core], red_ref.at[0, core]))
    reduce1.step(6)
    stores.append(store(4, s.red.at[0, 1 - core], red_ref.at[0, 1 - core]))
    for copy in stores:
        copy.wait()


def finish_kernel(
    red_ref, o_ref, d_ref, out_ref, dx_ref, gains_ref, dqkv_ref, dproj_ref, dtab_ref, red, sems
):
    copies = [
        pltpu.make_async_copy(source, target, sems.at[i])
        for i, (source, target) in enumerate(
            ((red_ref.at[1], red.at[1]), (red_ref.at[0], red.at[0]), (o_ref, out_ref), (d_ref, dx_ref))
        )
    ]
    for copy in copies:
        copy.start()
    for j in (1, 0):
        copies[1 - j].wait()
        for half in range(2):
            for slot in range(12):
                column, row = half * 3 + slot // 4, (slot % 4) * 48
                rows = slice(row, row + 48)
                value = red[j, half, slot].astype(F32)
                if column < 4:
                    dqkv_ref[j, rows, 128 * column : 128 * column + 128] = value
                elif column == 4:
                    dqkv_ref[j, rows, 512:576] = value[:, 0:64]
                    dproj_ref[j, rows, 0:64] = value[:, 64:128]
                else:
                    dproj_ref[j, rows, 64:192] = value
            width = 128 if half == 0 else 16
            lanes = slice(128 * half, 128 * half + width)
            for third in range(3):
                value = red[j, half, 16 + third].astype(F32)
                for i in range(2):
                    dtab_ref[j, 2 * third + i, :, 0, lanes] = value[24 * i : 24 * i + 23, 0:width]
        gains_ref[j : j + 1, 0:128] = red[j, 0, 12].astype(F32)[0:1]
        gains_ref[j : j + 1, 128:192] = red[j, 1, 12].astype(F32)[0:1, 0:64]
    for copy in copies[2:]:
        copy.wait()


def body(inputs, cotangent, gains, qkv_weights, proj_weights, bias_tables, pad_rows):
    vmem = pl.BlockSpec(memory_space=pltpu.VMEM)
    hbm = pl.BlockSpec(memory_space=pltpu.HBM)
    field = jax.ShapeDtypeStruct((6, 12, 2, 192), BF16)
    out, dx, red = pl.pallas_call(
        main_kernel,
        out_shape=(field, field, jax.ShapeDtypeStruct((2, 2, 20, 48, 128), BF16)),
        in_specs=[hbm] * 7,
        out_specs=(hbm,) * 3,
        scratch_shapes=list(SCRATCH.values()),
        compiler_params=pltpu.CompilerParams(
            collective_id=0, has_side_effects=True, vmem_limit_bytes=VMEM_LIMIT
        ),
        name="both_blocks",
    )(
        inputs.transpose(1, 2, 0, 3),
        cotangent.transpose(1, 2, 0, 3),
        gains,
        qkv_weights,
        proj_weights,
        bias_tables.transpose(0, 2, 3, 1, 4),
        pad_rows,
    )
    out, dx, d_gains, d_qkv, d_proj, d_tables = pl.pallas_call(
        finish_kernel,
        out_shape=(
            field,
            field,
            jax.ShapeDtypeStruct((2, 192), F32),
            jax.ShapeDtypeStruct((2, 192, 576), F32),
            jax.ShapeDtypeStruct((2, 192, 192), F32),
            jax.ShapeDtypeStruct((2, 6, 23, 1, 144), F32),
        ),
        in_specs=[hbm] * 3,
        out_specs=(vmem,) * 6,
        scratch_shapes=[
            pltpu.VMEM((2, 2, 20, 48, 128), BF16),
            pltpu.SemaphoreType.DMA((4,)),
        ],
        compiler_params=pltpu.CompilerParams(vmem_limit_bytes=VMEM_LIMIT),
        name="unpack",
    )(red, out, dx)
    return (
        out.transpose(2, 0, 1, 3),
        dx.transpose(2, 0, 1, 3),
        d_gains,
        d_qkv,
        d_proj,
        d_tables.transpose(0, 3, 1, 2, 4),
    )


def solution(mesh):
    field = P(None, "lat", "lon", None)
    tables = P(None, "lat", None, None, None)
    return jax.shard_map(
        body,
        mesh=mesh,
        in_specs=(field, field, P(), P(), P(), tables, P()),
        out_specs=(field, field, P(), P(), P(), tables),
        check_vma=False,
    )
```
